32 devices in a mesh: dp: 16 (over z, y, x), chan: 2 (over core).
Axes of the slice: x: 2, y: 2, z: 4, core: 2. Of those that a mesh axis runs over, the one named last changes fastest.
Arguments:
- images: bfloat16 [32, 18, 32, 1024], P('dp', None, None, 'chan'), may hold values from -12 to 12
- extents: int32 [32, 2], P('dp'), may hold values from 5 to 16, as said below
- cotangent: bfloat16 [32, 9, 16, 2048], P('dp', None, None, 'chan'), may hold values from -6 to 6
- reduce1: bfloat16 [1024, 512], P(None, 'chan'), may hold values from -0.1875 to 0.1875
- spatial1: bfloat16 [3, 3, 512, 512], P(None, None, None, 'chan'), may hold values from -0.09375 to 0.09375
- expand1: bfloat16 [512, 2048], P(None, 'chan'), may hold values from -0.25 to 0.25
- shortcut: bfloat16 [1024, 2048], P(None, 'chan'), may hold values from -0.1875 to 0.1875
- reduce2: bfloat16 [2048, 512], P(None, 'chan'), may hold values from -0.125 to 0.125
- spatial2: bfloat16 [3, 3, 512, 512], P(None, None, None, 'chan'), may hold values from -0.09375 to 0.09375
- expand2: bfloat16 [512, 2048], P(None, 'chan'), may hold values from -0.25 to 0.25
- norm_one: float32 [2, 512], P(None, 'chan'), may hold values from -1 to 1.5, as said below
- norm_two: float32 [2, 512], P(None, 'chan'), may hold values from -1 to 1.5, as said below
- norm_three: float32 [2, 2048], P(None, 'chan'), may hold values from -1 to 1.5, as said below
- norm_skip: float32 [2, 2048], P(None, 'chan'), may hold values from -1 to 1.5, as said below
- norm_four: float32 [2, 512], P(None, 'chan'), may hold values from -1 to 1.5, as said below
- norm_five: float32 [2, 512], P(None, 'chan'), may hold values from -1 to 1.5, as said below
- norm_six: float32 [2, 2048], P(None, 'chan'), may hold values from -1 to 1.5, as said below
Outputs:
- block_one: bfloat16 [32, 9, 16, 2048], P('dp', None, None, 'chan')
- block_two: bfloat16 [32, 9, 16, 2048], P('dp', None, None, 'chan')
- input_grad: bfloat16 [32, 18, 32, 1024], P('dp', None, None, 'chan')
- reduce1_grad: float32 [1024, 512], P(None, 'chan')
- spatial1_grad: float32 [3, 3, 512, 512], P(None, None, None, 'chan')
- expand1_grad: float32 [512, 2048], P(None, 'chan')
- shortcut_grad: float32 [1024, 2048], P(None, 'chan')
- reduce2_grad: float32 [2048, 512], P(None, 'chan')
- spatial2_grad: float32 [3, 3, 512, 512], P(None, None, None, 'chan')
- expand2_grad: float32 [512, 2048], P(None, 'chan')
- norm_one_grad: float32 [2, 512], P(None, 'chan')
- norm_two_grad: float32 [2, 512], P(None, 'chan')
- norm_three_grad: float32 [2, 2048], P(None, 'chan')
- norm_skip_grad: float32 [2, 2048], P(None, 'chan')
- norm_four_grad: float32 [2, 512], P(None, 'chan')
- norm_five_grad: float32 [2, 512], P(None, 'chan')
- norm_six_grad: float32 [2, 2048], P(None, 'chan')
The draws below stay inside these ranges and needn't reach their ends.
Inputs may be any that keep to these rules, and one draw needn't show every extreme that they name: `extents`: column 0 is an image's valid rows, from 5 to 9; column 1 its valid columns, from 8 to 16. The first of the 2 images of each index of dp fills the whole grid. `norm_one`: row 0 lies in 0.5 to 1.5, row 1 in -1 to 1. `norm_two`: row 0 lies in 0.5 to 1.5, row 1 in -1 to 1. `norm_three`: row 0 lies in 0.5 to 1.5, row 1 in -1 to 1. `norm_skip`: row 0 lies in 0.5 to 1.5, row 1 in -1 to 1. `norm_four`: row 0 lies in 0.5 to 1.5, row 1 in -1 to 1. `norm_five`: row 0 lies in 0.5 to 1.5, row 1 in -1 to 1. `norm_six`: row 0 lies in 0.5 to 1.5, row 1 in -1 to 1.
All inputs are finite; a program needn't handle non-finite values.
Results may differ from the reference program's by a relative error of at most 0.025.
Values may be sent and summed in bfloat16 or wider, within the bound.
No kernel may reach another device: no remote copies, remote signals or barrier semaphores. Data moves between devices by JAX's collectives and lax.ppermute only.
A program may use at most 640 MiB of HBM per device.

```python
import jax
import jax.numpy as jnp
from jax import lax

CIN = 1024
CMID = 512
COUT = 2048
IMG = 2
HO = 9
WO = 16
IMAGES = 32


def norm_pair(key, channels):
    scale_key, shift_key = jax.random.split(key)
    scales = jax.random.uniform(scale_key, (1, channels), jnp.float32, 0.5, 1.5)
    shifts = jax.random.uniform(shift_key, (1, channels), jnp.float32, -1.0, 1.0)
    return jnp.concatenate([scales, shifts], axis=0)


def draw_images(key, part):
    key = jax.random.fold_in(key, 11)
    shape = (IMAGES, 2 * HO, 2 * WO, CIN)
    position = jnp.arange(IMAGES, dtype=jnp.float32) / max(IMAGES - 1, 1)
    normal_part = jnp.clip(jax.random.normal(key, shape, jnp.float32), -4.0, 4.0)
    image_scale = 0.3 * jnp.power(10.0, position)
    return (normal_part * image_scale[:, None, None, None]).astype(jnp.bfloat16)


def draw_extents(key, part):
    key = jax.random.fold_in(key, 7)
    high_key, wide_key = jax.random.split(key)
    heights = jax.random.randint(high_key, (IMAGES,), (HO + 1) // 2, HO + 1)
    widths = jax.random.randint(wide_key, (IMAGES,), WO // 2, WO + 1)
    leading = jnp.arange(IMAGES) % IMG == 0
    heights = jnp.where(leading, HO, heights)
    widths = jnp.where(leading, WO, widths)
    return jnp.stack([heights, widths], axis=1).astype(jnp.int32)


def draw_norm_one(key, part):
    key = jax.random.fold_in(key, 21)
    return norm_pair(key, CMID)


def draw_norm_two(key, part):
    key = jax.random.fold_in(key, 22)
    return norm_pair(key, CMID)


def draw_norm_three(key, part):
    key = jax.random.fold_in(key, 23)
    return norm_pair(key, COUT)


def draw_norm_skip(key, part):
    key = jax.random.fold_in(key, 24)
    return norm_pair(key, COUT)


def draw_norm_four(key, part):
    key = jax.random.fold_in(key, 25)
    return norm_pair(key, CMID)


def draw_norm_five(key, part):
    key = jax.random.fold_in(key, 26)
    return norm_pair(key, CMID)


def draw_norm_six(key, part):
    key = jax.random.fold_in(key, 27)
    return norm_pair(key, COUT)


def level_of(own_key, dims, cuts, low, top_value):
    def one(axis_at, shards_of):
        draws = jax.random.uniform(jax.random.fold_in(jax.random.fold_in(own_key, 6), axis_at), (shards_of,), jnp.float32, low / len(cuts), top_value / len(cuts))
        return jnp.repeat(jnp.exp(draws), dims[axis_at] // shards_of).reshape((-1,) + (1,) * (len(dims) - axis_at - 1))

    gain = one(*cuts[0])
    for cut in cuts[1:]:
        gain = gain * one(*cut)
    return gain


def gaussian(own_key, extent, spread, reach, pieces=(), kind=jnp.bfloat16):
    values = jax.random.normal(own_key, extent, jnp.float32) * spread
    if len(pieces) > 0:
        values = level_of(own_key, extent, pieces, -0.22, 0.18) * values
    return jnp.clip(values, min=-reach, max=reach).astype(kind)


def setup_inputs(seed: int = 0) -> dict:
    streams_of = jax.random.split(jax.random.key(seed), 18)
    return {
        "images": draw_images(jax.random.fold_in(streams_of[17], 71), 0),
        "extents": draw_extents(jax.random.fold_in(streams_of[17], 71), 0),
        "cotangent": gaussian(streams_of[2], (IMAGES, HO, WO, COUT), 1.0, 6.0, ((0, 16), (3, 2))),
        "reduce1": gaussian(streams_of[3], (CIN, CMID), CIN ** -0.5, 0.1875, ((1, 2),)),
        "spatial1": gaussian(streams_of[4], (3, 3, CMID, CMID), (9 * CMID) ** -0.5, 0.09375, ((3, 2),)),
        "expand1": gaussian(streams_of[5], (CMID, COUT), CMID ** -0.5, 0.25, ((1, 2),)),
        "shortcut": gaussian(streams_of[6], (CIN, COUT), CIN ** -0.5, 0.1875, ((1, 2),)),
        "reduce2": gaussian(streams_of[7], (COUT, CMID), COUT ** -0.5, 0.125, ((1, 2),)),
        "spatial2": gaussian(streams_of[8], (3, 3, CMID, CMID), (9 * CMID) ** -0.5, 0.09375, ((3, 2),)),
        "expand2": gaussian(streams_of[9], (CMID, COUT), CMID ** -0.5, 0.25, ((1, 2),)),
        "norm_one": draw_norm_one(jax.random.fold_in(streams_of[17], 71), 0),
        "norm_two": draw_norm_two(jax.random.fold_in(streams_of[17], 71), 0),
        "norm_three": draw_norm_three(jax.random.fold_in(streams_of[17], 71), 0),
        "norm_skip": draw_norm_skip(jax.random.fold_in(streams_of[17], 71), 0),
        "norm_four": draw_norm_four(jax.random.fold_in(streams_of[17], 71), 0),
        "norm_five": draw_norm_five(jax.random.fold_in(streams_of[17], 71), 0),
        "norm_six": draw_norm_six(jax.random.fold_in(streams_of[17], 71), 0),
    }


epsilon = 1e-05

@jax.custom_vjp
def low(v):
    return lax.optimization_barrier(v.astype(jnp.bfloat16)).astype(jnp.float32)

@jax.custom_vjp
def low_back(v):
    return v

def low_keep(v):
    return (low(v), None)

def low_pass(kept, grad):
    return (grad,)

def back_keep(v):
    return (v, None)

def back_low(kept, grad):
    return (low(grad),)
low.defvjp(low_keep, low_pass)
low_back.defvjp(back_keep, back_low)

def pixel_masks(extents, row_count, col_count, factor):
    heights = extents[:, 0][:, None, None] * factor
    widths = extents[:, 1][:, None, None] * factor
    row_index = lax.broadcasted_iota(jnp.int32, (1, row_count, col_count), 1)
    col_index = lax.broadcasted_iota(jnp.int32, (1, row_count, col_count), 2)
    return ((row_index < heights) & (col_index < widths)).astype(jnp.float32)

def dense(active, matrix):
    return jnp.einsum('nhwk,kc->nhwc', active, matrix, precision=lax.Precision.HIGHEST)

def spatial(active, kernel, stride):
    return lax.conv_general_dilated(active, kernel, (stride, stride), ((1, 1), (1, 1)), dimension_numbers=('NHWC', 'HWIO', 'NHWC'), precision=lax.Precision.HIGHEST)

def batch_norm(conv_out, pixel_mask, norm_params):
    cells = pixel_mask[..., None]
    pixels = jnp.sum(pixel_mask)
    average = lax.optimization_barrier(jnp.sum(conv_out * cells, axis=(0, 1, 2))) / pixels
    centred = conv_out - average
    variance = lax.optimization_barrier(jnp.sum(centred * centred * cells, axis=(0, 1, 2))) / pixels
    return norm_params[0] * centred * lax.rsqrt(variance + epsilon) + norm_params[1]

def reference(images, extents, cotangent, reduce1, spatial1, expand1, shortcut, reduce2, spatial2, expand2, norm_one, norm_two, norm_three, norm_skip, norm_four, norm_five, norm_six):
    inner_mask = pixel_masks(extents, 2 * HO, 2 * WO, 2)
    outer_mask = pixel_masks(extents, HO, WO, 1)
    inner_cells = inner_mask[..., None]
    outer_cells = outer_mask[..., None]

    def forward(inputs, weights, norm_set):
        masked_in = inputs * inner_cells
        conv_one = low_back(dense(masked_in, weights[0]))
        act_one = low(jax.nn.silu(batch_norm(conv_one, inner_mask, norm_set[0])) * inner_cells)
        conv_two = low_back(spatial(act_one, weights[1], 2))
        act_two = low(jax.nn.silu(batch_norm(conv_two, outer_mask, norm_set[1])) * outer_cells)
        conv_three = low_back(dense(act_two, weights[2]))
        conv_skip = low_back(dense(masked_in[:, 0::2, 0::2, :], weights[3]))
        joined_one = batch_norm(conv_three, outer_mask, norm_set[2]) + batch_norm(conv_skip, outer_mask, norm_set[3])
        block_one = low(jax.nn.silu(joined_one) * outer_cells)
        conv_four = low_back(dense(block_one, weights[4]))
        act_four = low(jax.nn.silu(batch_norm(conv_four, outer_mask, norm_set[4])) * outer_cells)
        conv_five = low_back(spatial(act_four, weights[5], 1))
        act_five = low(jax.nn.silu(batch_norm(conv_five, outer_mask, norm_set[5])) * outer_cells)
        conv_six = low_back(dense(act_five, weights[6]))
        joined_two = batch_norm(conv_six, outer_mask, norm_set[6]) + block_one
        block_two = jax.nn.silu(joined_two) * outer_cells
        return (block_two, block_one)
    weights = tuple((matrix.astype(jnp.float32) for matrix in (reduce1, spatial1, expand1, shortcut, reduce2, spatial2, expand2)))
    norm_set = (norm_one, norm_two, norm_three, norm_skip, norm_four, norm_five, norm_six)
    block_two, pullback, block_one = jax.vjp(forward, images.astype(jnp.float32), weights, norm_set, has_aux=True)
    input_grad, weight_grads, norm_grads = pullback(cotangent.astype(jnp.float32))
    return (block_one.astype(jnp.bfloat16), block_two.astype(jnp.bfloat16), input_grad.astype(jnp.bfloat16), weight_grads[0], weight_grads[1], weight_grads[2], weight_grads[3], weight_grads[4], weight_grads[5], weight_grads[6], norm_grads[0], norm_grads[1], norm_grads[2], norm_grads[3], norm_grads[4], norm_grads[5], norm_grads[6])
```

```python
import jax
import jax.numpy as jnp
from jax import lax
from jax.sharding import PartitionSpec as P

epsilon = 1e-05
f32 = jnp.float32
bf16 = jnp.bfloat16
SWAP = [(0, 1), (1, 0)]


def swap(value):
    return lax.ppermute(value, "chan", SWAP)


def in_order(core, own, other, axis=-1):
    return jnp.where(
        core == 0,
        jnp.concatenate([own, other], axis),
        jnp.concatenate([other, own], axis),
    )


def part_of(value, index, axis=-1):
    axis = axis % value.ndim
    size = value.shape[axis] // 2
    return lax.dynamic_slice_in_dim(value, index * size, size, axis)


def exchange(local, count):
    spread = jnp.broadcast_to(local[None], (count,) + local.shape)
    return lax.all_to_all(spread, "dp", 0, 0, tiled=True)


def matmul(left, right):
    return lax.dot_general(left, right, (((1,), (0,)), ((), ())), preferred_element_type=f32)


def matmul_nt(left, right):
    return lax.dot_general(left, right, (((1,), (1,)), ((), ())), preferred_element_type=f32)


def matmul_tn(left, right):
    return lax.dot_general(left, right, (((0,), (0,)), ((), ())), preferred_element_type=f32)


def local_stats(values, mask, cells):
    total = jnp.sum(values * mask, axis=0)
    centred = values - total / cells
    return jnp.stack([total, jnp.sum(centred * centred * mask, axis=0)])


def moments(gathered, cells_each, pixels):
    totals, squares = gathered[:, 0], gathered[:, 1]
    average = jnp.sum(totals, axis=0) / pixels
    offsets = totals / cells_each[:, None] - average
    variance = (jnp.sum(squares, axis=0) + jnp.sum(cells_each[:, None] * offsets * offsets, axis=0)) / pixels
    return average, lax.rsqrt(variance + epsilon)


def silu_slope(values):
    logistic = jax.nn.sigmoid(values)
    return logistic * (1.0 + values * (1.0 - logistic))


def shifted(values, rows, cols):
    height, width = values.shape[1:3]
    padded = jnp.pad(values, ((0, 0), (1, 1), (1, 1), (0, 0)))
    return padded[:, 1 + rows : 1 + rows + height, 1 + cols : 1 + cols + width, :]


def solution(mesh):
    count = mesh.shape["dp"]

    def local(images, extents, cotangent, reduce1, spatial1, expand1, shortcut, reduce2, spatial2, expand2,
              norm_one, norm_two, norm_three, norm_skip, norm_four, norm_five, norm_six):
        core = lax.axis_index("chan")
        imgs, height, width = cotangent.shape[:3]
        grid = height * width
        outer = imgs * grid
        cid = images.shape[3]
        mid = reduce1.shape[1]

        cell = lax.broadcasted_iota(jnp.int32, (imgs, grid), 1)
        valid = (cell // width < extents[:, 0:1]) & (cell % width < extents[:, 1:2])
        mask = valid.astype(f32).reshape(outer, 1)
        mask4 = jnp.tile(mask, (4, 1))
        cells = jnp.sum(extents[:, 0] * extents[:, 1]).astype(f32)

        target = lax.broadcasted_iota(jnp.int32, (4 * grid, 4 * grid), 0)
        source = lax.broadcasted_iota(jnp.int32, (4 * grid, 4 * grid), 1)
        plane, place = target // grid, target % grid
        place = (2 * (place // width) + plane // 2) * 2 * width + 2 * (place % width) + plane % 2
        pick = (source == place).astype(bf16)
        flat = images.reshape(imgs, 4 * grid, cid)
        sorted_x = [matmul(pick, flat[n]).astype(bf16).reshape(4, 1, grid, cid) for n in range(imgs)]
        own_x = (jnp.concatenate(sorted_x, axis=1).reshape(4 * outer, cid) * mask4.astype(bf16))
        all_x = in_order(core, own_x, swap(own_x))

        def activate(pre, cell_mask):
            return (jax.nn.silu(pre) * cell_mask).astype(bf16)

        def gather(own):
            return in_order(core, own, swap(own))

        conv_one = matmul(all_x, reduce1)
        stats_one = local_stats(conv_one, mask4, 4 * cells)
        got_one = exchange(jnp.concatenate([stats_one, jnp.full((1, mid), cells)]), count)
        cells_each = got_one[:, 2, 0]
        pixels = jnp.sum(cells_each)
        conv_skip = matmul(all_x[:outer], shortcut)
        stats_skip = local_stats(conv_skip, mask, cells)
        mean_one, inv_one = moments(got_one, 4 * cells_each, 4 * pixels)
        hat_one = (conv_one - mean_one) * inv_one
        pre_one = norm_one[0] * hat_one + norm_one[1]
        act_one = gather(activate(pre_one, mask4))

        planes = act_one.reshape(4, imgs, height, width, 2 * mid)
        taps = []
        for r in range(3):
            for s in range(3):
                which = (2 if r != 1 else 0) + (1 if s != 1 else 0)
                taps.append(shifted(planes[which], -1 if r == 0 else 0, -1 if s == 0 else 0).reshape(outer, 2 * mid))
        taps_one = jnp.concatenate(taps, axis=1)
        conv_two = matmul(taps_one, spatial1.reshape(18 * mid, mid))
        got_two = exchange(jnp.concatenate([local_stats(conv_two, mask, cells), stats_skip], axis=1), count)
        mean_two, inv_two = moments(got_two[:, :, :mid], cells_each, pixels)
        hat_two = (conv_two - mean_two) * inv_two
        pre_two = norm_two[0] * hat_two + norm_two[1]
        act_two = gather(activate(pre_two, mask))

        conv_three = matmul(act_two, expand1)
        got_three = exchange(local_stats(conv_three, mask, cells), count)
        mean_skip, inv_skip = moments(got_two[:, :, mid:], cells_each, pixels)
        hat_skip = (conv_skip - mean_skip) * inv_skip
        pre_skip = norm_skip[0] * hat_skip + norm_skip[1]
        mean_three, inv_three = moments(got_three, cells_each, pixels)
        hat_three = (conv_three - mean_three) * inv_three
        joined_one = norm_three[0] * hat_three + norm_three[1] + pre_skip
        block_one = activate(joined_one, mask)
        all_block = gather(block_one)

        conv_four = matmul(all_block, reduce2)
        mean_four, inv_four = moments(exchange(local_stats(conv_four, mask, cells), count), cells_each, pixels)
        hat_four = (conv_four - mean_four) * inv_four
        pre_four = norm_four[0] * hat_four + norm_four[1]
        act_four = gather(activate(pre_four, mask))

        grid_four = act_four.reshape(imgs, height, width, 2 * mid)
        taps_four = jnp.concatenate(
            [shifted(grid_four, r - 1, s - 1).reshape(outer, 2 * mid) for r in range(3) for s in range(3)], axis=1)
        conv_five = matmul(taps_four, spatial2.reshape(18 * mid, mid))
        mean_five, inv_five = moments(exchange(local_stats(conv_five, mask, cells), count), cells_each, pixels)
        hat_five = (conv_five - mean_five) * inv_five
        pre_five = norm_five[0] * hat_five + norm_five[1]
        act_five = gather(activate(pre_five, mask))

        conv_six = matmul(act_five, expand2)
        mean_six, inv_six = moments(exchange(local_stats(conv_six, mask, cells), count), cells_each, pixels)
        hat_six = (conv_six - mean_six) * inv_six
        joined_two = norm_six[0] * hat_six + norm_six[1] + block_one.astype(f32)
        block_two = activate(joined_two, mask)

        grad_join2 = cotangent.reshape(outer, -1).astype(f32) * mask * silu_slope(joined_two)

        def norm_sums(grad, *hats):
            local_sums = jnp.stack([jnp.sum(grad, axis=0)] + [jnp.sum(grad * hat, axis=0) for hat in hats])
            return jnp.sum(exchange(local_sums, count), axis=0)

        def norm_back(grad, hat, inv, beta_grad, gamma_grad, norm, cell_mask, total):
            out = cell_mask * norm[0] * inv * (grad - (beta_grad + hat * gamma_grad) / total)
            return out.astype(bf16), jnp.stack([gamma_grad, beta_grad])

        def spread_out(own_part, other_part):
            return own_part + swap(other_part.astype(bf16)).astype(f32)

        def back_1x1(grad, weight):
            return spread_out(matmul_nt(grad, part_of(weight, core, 0)),
                              matmul_nt(grad, part_of(weight, 1 - core, 0)))

        sums = norm_sums(grad_join2, hat_six)
        grad_six, norm_six_grad = norm_back(grad_join2, hat_six, inv_six, sums[0], sums[1], norm_six, mask, pixels)
        expand2_grad = matmul_tn(act_five, grad_six)
        pre_grad = back_1x1(grad_six, expand2) * mask * silu_slope(pre_five)
        sums = norm_sums(pre_grad, hat_five)
        grad_five, norm_five_grad = norm_back(pre_grad, hat_five, inv_five, sums[0], sums[1], norm_five, mask, pixels)

        def shifts_of(grad, choices):
            cube = grad.reshape(imgs, height, width, -1)
            return [shifted(cube, i, j).reshape(outer, -1) for i, j in choices]

        def kernel_rows(kernel, index):
            return part_of(kernel, index, 2)

        moved = shifts_of(grad_five, [(1 - r, 1 - s) for r in range(3) for s in range(3)])
        moved_five = jnp.concatenate(moved, axis=1)
        spatial2_grad = matmul_tn(act_four, moved_five).reshape(2 * mid, 9, mid).transpose(1, 0, 2).reshape(3, 3, 2 * mid, mid)

        def back_five(index):
            rows = kernel_rows(spatial2, index)
            return sum(matmul_nt(moved[3 * r + s], rows[r, s]) for r in range(3) for s in range(3))

        pre_grad = spread_out(back_five(core), back_five(1 - core)) * mask * silu_slope(pre_four)
        sums = norm_sums(pre_grad, hat_four)
        grad_four, norm_four_grad = norm_back(pre_grad, hat_four, inv_four, sums[0], sums[1], norm_four, mask, pixels)
        reduce2_grad = matmul_tn(all_block, grad_four)
        grad_join1 = (grad_join2 + back_1x1(grad_four, reduce2)) * mask * silu_slope(joined_one)

        sums = norm_sums(grad_join1, hat_three, hat_skip)
        grad_three, norm_three_grad = norm_back(grad_join1, hat_three, inv_three, sums[0], sums[1], norm_three, mask, pixels)
        grad_skip, norm_skip_grad = norm_back(grad_join1, hat_skip, inv_skip, sums[0], sums[2], norm_skip, mask, pixels)
        expand1_grad = matmul_tn(act_two, grad_three)
        shortcut_grad = matmul_tn(all_x[:outer], grad_skip)
        pre_grad = back_1x1(grad_three, expand1) * mask * silu_slope(pre_two)
        sums = norm_sums(pre_grad, hat_two)
        grad_two, norm_two_grad = norm_back(pre_grad, hat_two, inv_two, sums[0], sums[1], norm_two, mask, pixels)

        g00, g01, g10, g11 = shifts_of(grad_two, [(0, 0), (0, 1), (1, 0), (1, 1)])
        act_planes = act_one.reshape(4, outer, 2 * mid)
        uses = {(1, 1): (0, g00), (1, 2): (1, g00), (1, 0): (1, g01), (2, 1): (2, g00), (0, 1): (2, g10),
                (2, 2): (3, g00), (2, 0): (3, g01), (0, 2): (3, g10), (0, 0): (3, g11)}
        spatial1_grad = jnp.stack([
            jnp.stack([matmul_tn(act_planes[uses[r, s][0]], uses[r, s][1]) for s in range(3)]) for r in range(3)])

        def back_two(index):
            rows = kernel_rows(spatial1, index)
            out = [0.0] * 4
            for (r, s), (which, grad) in uses.items():
                out[which] = out[which] + matmul_nt(grad, rows[r, s])
            return jnp.concatenate(out, axis=0)

        pre_grad = spread_out(back_two(core), back_two(1 - core)) * mask4 * silu_slope(pre_one)
        sums = norm_sums(pre_grad, hat_one)
        grad_one, norm_one_grad = norm_back(pre_grad, hat_one, inv_one, sums[0], sums[1], norm_one, mask4, 4 * pixels)
        reduce1_grad = matmul_tn(all_x, grad_one)

        def back_x(index):
            part = matmul_nt(grad_one, part_of(reduce1, index, 0))
            skip = matmul_nt(grad_skip, part_of(shortcut, index, 0))
            return jnp.concatenate([part[:outer] + skip, part[outer:]], axis=0)

        grad_x = (spread_out(back_x(core), back_x(1 - core)) * mask4).astype(bf16).reshape(4, imgs, grid, cid)
        input_grad = jnp.stack([matmul_tn(pick, grad_x[:, n].reshape(4 * grid, cid)).astype(bf16) for n in range(imgs)])

        grads = (reduce1_grad, spatial1_grad, expand1_grad, shortcut_grad, reduce2_grad, spatial2_grad, expand2_grad)
        grads = tuple(lax.psum(g.astype(bf16), "dp").astype(f32) for g in grads)
        return (block_one.reshape(cotangent.shape), block_two.reshape(cotangent.shape), input_grad.reshape(images.shape),
                *grads, norm_one_grad, norm_two_grad, norm_three_grad, norm_skip_grad, norm_four_grad, norm_five_grad,
                norm_six_grad)

    wide = P("dp", None, None, "chan")
    weights = (P(None, "chan"), P(None, None, None, "chan")) + (P(None, "chan"),) * 3 + (P(None, None, None, "chan"), P(None, "chan"))
    norms = (P(None, "chan"),) * 7
    return jax.shard_map(
        local, mesh=mesh,
        in_specs=(wide, P("dp", None), wide) + weights + norms,
        out_specs=(wide, wide, wide) + weights + norms,
        check_vma=False)
```

```python
import functools
import math

import jax
import jax.numpy as jnp
from jax import lax
from jax.experimental import pallas as pl
from jax.experimental.pallas import tpu as pltpu
from jax.sharding import PartitionSpec as P

epsilon = 1e-05
f32 = jnp.float32
bf16 = jnp.bfloat16
SWAP = [(0, 1), (1, 0)]


def swap(value):
    return lax.ppermute(value, "chan", SWAP)


def in_order(core, own, other, axis=-1):
    return jnp.where(
        core == 0,
        jnp.concatenate([own, other], axis),
        jnp.concatenate([other, own], axis),
    )


def tie(early, late):
    return lax.optimization_barrier((early, late))


def send(value, count, bits):
    return lax.ppermute(value, "dp", [(at, at ^ bits) for at in range(count)])


def slot(value, index, size, axis):
    return lax.dynamic_slice_in_dim(value, index * size, size, axis)


def lay_kernel(near, far, layouts, chunks, at_ref, *refs):
    ins, outs = refs[: len(refs) - len(layouts)], refs[len(refs) - len(layouts) :]
    near_at, far_at = at_ref[0], at_ref[1]
    for which, start, member, relative, b in chunks:
        owner = b
        if relative:
            member = near_at ^ member
            owner = far_at ^ b
        for (kind, dims), out in zip(layouts, outs):
            if kind == "kernel":
                size = dims[2] // near // far
                for tap in range(9):
                    first = pl.multiple_of(member * (size * far) + owner * size, size)
                    out[tap // 3, tap % 3, pl.ds(first, size), :] = ins[which][start : start + size, :].astype(f32)
                    start += size
            elif kind == "rows":
                size = dims[0] // near // far
                first = pl.multiple_of(member * (size * far) + owner * size, size)
                out[pl.ds(first, size), :] = ins[which][start : start + size, :].astype(f32)
                start += size
            else:
                size, lanes = dims[0] // far, dims[1] // near
                first = pl.multiple_of(owner * size, size)
                lane = pl.multiple_of(member * lanes, lanes)
                out[pl.ds(first, size), pl.ds(lane, lanes)] = ins[which][start : start + size, :].astype(f32)
                start += size


def laid_out(arrays, chunks, near, far, near_at, far_at, layouts):
    return pl.pallas_call(
        functools.partial(lay_kernel, near, far, layouts, chunks),
        out_shape=[jax.ShapeDtypeStruct(dims, f32) for _, dims in layouts],
        in_specs=[pl.BlockSpec(memory_space=pltpu.SMEM)] + [pl.BlockSpec(memory_space=pltpu.VMEM)] * len(arrays),
        out_specs=[pl.BlockSpec(memory_space=pltpu.VMEM)] * len(layouts),
        compiler_params=pltpu.CompilerParams(vmem_limit_bytes=40 * 2**20),
    )(jnp.stack([near_at, far_at]).astype(jnp.int32), *arrays)


def spec(kind):
    return pl.BlockSpec(memory_space=kind)


def staged(body, scalars, ins, outs, *refs):
    head, refs = refs[:scalars], refs[scalars:]
    given, results, refs = refs[:ins], refs[ins : ins + outs], refs[ins + outs :]
    here, made, extra = refs[:ins], refs[ins : ins + outs], refs[ins + outs : -2]
    in_sems, out_sems = refs[-2:]
    arrivals = [pltpu.make_async_copy(given[at], here[at], in_sems.at[at]) for at in range(ins)]
    for copy in arrivals:
        copy.start()
    for copy in arrivals:
        copy.wait()
    body(*head, *here, *made, *extra)
    leaving = [pltpu.make_async_copy(made[at], results[at], out_sems.at[at]) for at in range(outs)]
    for copy in leaving:
        copy.start()
    for copy in leaving:
        copy.wait()


def run_kernel(body, outs, scalars, arrays, flops=0, scratch=()):
    size = sum(x.size * x.dtype.itemsize for x in arrays) + sum(math.prod(s) * jnp.dtype(d).itemsize for s, d in outs)
    return pl.pallas_call(
        functools.partial(staged, body, len(scalars), len(arrays), len(outs)),
        out_shape=[pltpu.HBM(shape, dtype) for shape, dtype in outs],
        in_specs=[spec(pltpu.SMEM)] * len(scalars) + [spec(pltpu.HBM)] * len(arrays),
        out_specs=[spec(pltpu.HBM)] * len(outs),
        scratch_shapes=[pltpu.VMEM(x.shape, x.dtype) for x in arrays] + [pltpu.VMEM(shape, dtype) for shape, dtype in outs]
        + list(scratch) + [pltpu.SemaphoreType.DMA((len(arrays),)), pltpu.SemaphoreType.DMA((len(outs),))],
        cost_estimate=pl.CostEstimate(flops=1, bytes_accessed=1, transcendentals=0),
        compiler_params=pltpu.CompilerParams(vmem_limit_bytes=48 * 2**20),
    )(*scalars, *[pltpu.with_memory_space_constraint(x, pltpu.HBM) for x in arrays])


def widen(mask_ref, lanes):
    mask = mask_ref[...]
    return mask if lanes == 128 else jnp.concatenate([mask] * (lanes // 128), axis=1)


def dot(left, right):
    return lax.dot_general(left, right, (((1,), (0,)), ((), ())), preferred_element_type=f32)


def dot_nt(left, right):
    return lax.dot_general(left, right, (((1,), (1,)), ((), ())), preferred_element_type=f32)


def halves(ref, core, size):
    own = pl.ds(pl.multiple_of(core * size, size), size)
    other = pl.ds(pl.multiple_of((1 - core) * size, size), size)
    return own, other


def stats(values, mask, cells):
    total = jnp.sum(values * mask, axis=0, keepdims=True)
    centred = (values - total / cells) * mask
    return [total, jnp.sum(centred * centred, axis=0, keepdims=True)]


def put_rows(out_ref, rows):
    tile = jnp.concatenate(rows, axis=0)
    for at in range(out_ref.shape[0]):
        out_ref[at] = tile


def moments(tiles, cells_ref, scale=1.0, first=0):
    lanes = tiles[0].shape[1]
    cells = jnp.concatenate([cells_ref[...]] * (lanes // 128), axis=1) * scale
    pixels = jnp.sum(cells, axis=0, keepdims=True)
    totals = [tile[first : first + 1] for tile in tiles]
    mean = functools.reduce(jnp.add, totals) / pixels
    spread = functools.reduce(jnp.add, [tile[first + 1 : first + 2] for tile in tiles])
    offsets = jnp.concatenate(totals, axis=0) / cells - mean
    spread = spread + jnp.sum(cells * offsets * offsets, axis=0, keepdims=True)
    return mean, lax.rsqrt(spread / pixels + epsilon), pixels


def put_moments(out_ref, mean, inverse, pixels):
    lanes = mean.shape[1]
    out_ref[...] = jnp.concatenate([mean, inverse, pixels, jnp.zeros((5, lanes), f32)], axis=0)


def silu_slope(values):
    logistic = jax.nn.sigmoid(values)
    return logistic * (1.0 + values * (1.0 - logistic))


def shift_cols(values, by, width):
    rows = values.shape[0]
    column = lax.broadcasted_iota(jnp.int32, values.shape, 0) & (width - 1)
    moved = pltpu.roll(values, (-by) % rows, 0)
    return jnp.where(column == (0 if by < 0 else width - 1), 0.0, moved)


def shift_rows(values, by, width, grid):
    if by == 0:
        return values
    zeros = jnp.zeros((width, values.shape[1]), values.dtype)
    out = []
    for start in range(0, values.shape[0], grid):
        if by < 0:
            out += [zeros, values[start : start + grid - width]]
        else:
            out += [values[start + width : start + grid], zeros]
    return jnp.concatenate(out, axis=0)


def pixel_of(index, grid, width):
    plane = jnp.zeros_like(index)
    for at in range(1, 4):
        plane = plane + (index >= at * grid).astype(jnp.int32)
    inside = index - plane * grid
    line = inside >> (width.bit_length() - 1)
    column = inside & (width - 1)
    return (2 * line + (plane >> 1)) * (2 * width) + 2 * column + (plane & 1)


def sort_kernel(grid, width, images_ref, mask_ref, out_ref):
    size = 4 * grid
    target = lax.broadcasted_iota(jnp.int32, (size, size), 0)
    source = lax.broadcasted_iota(jnp.int32, (size, size), 1)
    pick = jnp.where(source == pixel_of(target, grid, width), 1.0, 0.0).astype(bf16)
    imgs = images_ref.shape[0]
    lanes = images_ref.shape[2]
    mask = widen(mask_ref, lanes)
    for n in range(imgs):
        ordered = dot(pick, images_ref[n])
        for plane in range(4):
            first = (plane * imgs + n) * grid
            rows = ordered[plane * grid : (plane + 1) * grid] * mask[n * grid : (n + 1) * grid]
            out_ref[first : first + grid, :] = rows.astype(bf16)


def conv_one_kernel(core_ref, cells_ref, own_ref, other_ref, weight_ref, mask_ref, out_ref, stats_ref):
    own, other = halves(weight_ref, core_ref[0], own_ref.shape[1])
    values = dot(own_ref[...], weight_ref[own, :]) + dot(other_ref[...], weight_ref[other, :])
    out_ref[...] = values
    mask = widen(mask_ref, values.shape[1])
    cells = jnp.full((1, values.shape[1]), cells_ref[0])
    put_rows(stats_ref, stats(values, jnp.concatenate([mask] * 4, axis=0), 4.0 * cells_ref[0]) + [cells, cells])


def conv_skip_kernel(core_ref, cells_ref, own_ref, other_ref, weight_ref, mask_ref, out_ref, stats_ref):
    rows = mask_ref.shape[0]
    own, other = halves(weight_ref, core_ref[0], own_ref.shape[1])
    values = dot(own_ref[:rows], weight_ref[own, :]) + dot(other_ref[:rows], weight_ref[other, :])
    out_ref[...] = values
    mask = widen(mask_ref, values.shape[1])
    stats_ref[...] = jnp.concatenate(stats(values, mask, cells_ref[0]), axis=0)


def norm_act(got_ref, all_cells_ref, scale, own_ref, other_ref, norm_ref, mask, core, raw_ref, act_ref, moments_ref):
    lanes = own_ref.shape[1]
    own, other = halves(None, core, lanes)
    raw_ref[:, own] = own_ref[...]
    raw_ref[:, other] = other_ref[...]
    count = got_ref.shape[0] // 2
    for half in range(2):
        mean, inverse, pixels = moments([got_ref[2 * at + half] for at in range(count)], all_cells_ref, scale)

        @pl.when(core == half)
        def _():
            put_moments(moments_ref, mean, inverse, pixels)

        at = slice(half * lanes, (half + 1) * lanes)
        pre = norm_ref[0:1, at] * ((raw_ref[:, at] - mean) * inverse) + norm_ref[1:2, at]
        act_ref[:, at] = (pre * jax.nn.sigmoid(pre) * mask).astype(bf16)


def conv_two_kernel(grid, width, core_ref, cells_ref, got_ref, own_ref, other_ref, norm_ref, mask_ref, weight_ref,
                    act_ref, out_ref, stats_ref, moments_ref, all_cells_ref, raw_ref):
    rows = mask_ref.shape[0]
    lanes = own_ref.shape[1]
    mask = widen(mask_ref, lanes)
    for at in range(got_ref.shape[0] // 2):
        all_cells_ref[at : at + 1, :] = got_ref[2 * at, 2:3, :128]
    norm_act(got_ref, all_cells_ref, 4.0, own_ref, other_ref, norm_ref, jnp.concatenate([mask] * 4, axis=0), core_ref[0],
             raw_ref, act_ref, moments_ref)
    values = jnp.zeros((rows, out_ref.shape[1]), f32)
    for plane in range(4):
        here = act_ref[plane * rows : (plane + 1) * rows, :]
        by_col = {1: here} if plane % 2 == 0 else {2: here, 0: shift_cols(here.astype(f32), -1, width).astype(bf16)}
        for s, moved in by_col.items():
            for r in ((1,) if plane < 2 else (0, 2)):
                values = values + dot(shift_rows(moved, -1 if r == 0 else 0, width, grid), weight_ref[r, s])
    out_ref[...] = values
    put_rows(stats_ref, stats(values, mask, cells_ref[0]))


def conv_five_kernel(grid, width, core_ref, cells_ref, got_ref, all_cells_ref, own_ref, other_ref, norm_ref, mask_ref, weight_ref,
                     act_ref, out_ref, stats_ref, moments_ref, raw_ref):
    rows = mask_ref.shape[0]
    mask = widen(mask_ref, own_ref.shape[1])
    norm_act(got_ref, all_cells_ref, 1.0, own_ref, other_ref, norm_ref, mask, core_ref[0], raw_ref, act_ref, moments_ref)
    values = jnp.zeros((rows, out_ref.shape[1]), f32)
    here = act_ref[...]
    for s in range(3):
        moved = here if s == 1 else shift_cols(here.astype(f32), s - 1, width).astype(bf16)
        for r in range(3):
            values = values + dot(shift_rows(moved, r - 1, width, grid), weight_ref[r, s])
    out_ref[...] = values
    put_rows(stats_ref, stats(values, mask, cells_ref[0]))


def expand_kernel(core_ref, cells_ref, got_ref, all_cells_ref, own_ref, other_ref, norm_ref, mask_ref, weight_ref, *refs):
    more_refs, (act_ref, out_ref, stats_ref, moments_ref, raw_ref) = refs[:-5], refs[-5:]
    norm_act(got_ref, all_cells_ref, 1.0, own_ref, other_ref, norm_ref, widen(mask_ref, own_ref.shape[1]), core_ref[0],
             raw_ref, act_ref, moments_ref)
    values = dot(act_ref[...], weight_ref[...])
    out_ref[...] = values
    more = [more_refs[0][...]] if more_refs else []
    put_rows(stats_ref, stats(values, widen(mask_ref, values.shape[1]), cells_ref[0]) + more)


def normed(raw_ref, moments_ref):
    return (raw_ref[...] - moments_ref[0:1]) * moments_ref[1:2]


def scaled(norm_ref, hat):
    return norm_ref[0:1] * hat + norm_ref[1:2]


def join_kernel(got_ref, all_cells_ref, three_ref, skip_ref, norm_three_ref, norm_skip_ref, mask_ref, out_ref, moments_three_ref,
                moments_skip_ref):
    tiles = [got_ref[at] for at in range(got_ref.shape[0])]
    put_moments(moments_three_ref, *moments(tiles, all_cells_ref))
    put_moments(moments_skip_ref, *moments(tiles, all_cells_ref, first=2))
    joined = scaled(norm_three_ref, normed(three_ref, moments_three_ref)) + scaled(
        norm_skip_ref, normed(skip_ref, moments_skip_ref))
    out_ref[...] = (joined * jax.nn.sigmoid(joined) * widen(mask_ref, joined.shape[1])).astype(bf16)


def conv_four_kernel(core_ref, cells_ref, own_ref, other_ref, weight_ref, mask_ref, out_ref, stats_ref):
    own, other = halves(weight_ref, core_ref[0], own_ref.shape[1])
    values = dot(own_ref[...], weight_ref[own, :]) + dot(other_ref[...], weight_ref[other, :])
    out_ref[...] = values
    put_rows(stats_ref, stats(values, widen(mask_ref, values.shape[1]), cells_ref[0]))


def put_sums(out_ref, grad, *hats):
    rows = [jnp.sum(grad, axis=0, keepdims=True)] + [jnp.sum(grad * hat, axis=0, keepdims=True) for hat in hats]
    put_rows(out_ref, rows + [rows[0]] * (out_ref.shape[1] - len(rows)))


def top_kernel(got_ref, all_cells_ref, six_ref, block_ref, cotangent_ref, norm_ref, mask_ref, out_ref, grad_ref, sums_ref, moments_ref):
    put_moments(moments_ref, *moments([got_ref[at] for at in range(got_ref.shape[0])], all_cells_ref))
    hat = normed(six_ref, moments_ref)
    joined = scaled(norm_ref, hat) + block_ref[...].astype(f32)
    mask = widen(mask_ref, joined.shape[1])
    logistic = jax.nn.sigmoid(joined)
    out_ref[...] = (joined * logistic * mask).astype(bf16)
    grad = cotangent_ref[...].astype(f32) * mask * (logistic * (1.0 + joined * (1.0 - logistic)))
    grad_ref[...] = grad
    put_sums(sums_ref, grad, hat)


def sums_of(got_ref, core=None):
    if core is None:
        return functools.reduce(jnp.add, [got_ref[at] for at in range(got_ref.shape[0])])
    return functools.reduce(jnp.add, [got_ref[2 * at + core] for at in range(got_ref.shape[0] // 2)])


def norm_back(grad, hat, moments_ref, norm_ref, beta, gamma, mask):
    inside = grad - (beta + hat * gamma) / moments_ref[2:3]
    return (mask * (norm_ref[0:1] * moments_ref[1:2]) * inside).astype(bf16)


def back_dense_kernel(both, core_ref, got_ref, grad_ref, raw_ref, moments_ref, norm_ref, mask_ref, weight_ref, out_ref,
                    norm_grad_ref, send_ref):
    sums = sums_of(got_ref, core_ref[0] if both else None)
    beta, gamma = sums[0:1], sums[1:2]
    norm_grad_ref[...] = jnp.concatenate([gamma, beta], axis=0)
    grad = norm_back(grad_ref[...], normed(raw_ref, moments_ref), moments_ref, norm_ref, beta, gamma,
                     widen(mask_ref, raw_ref.shape[1]))
    out_ref[...] = grad
    own, other = halves(weight_ref, core_ref[0], weight_ref.shape[0] // 2)
    send_ref[...] = dot_nt(grad, weight_ref[other, :]).astype(bf16)


def own_dense_kernel(core_ref, up_ref, got_ref, weight_ref, raw_ref, moments_ref, norm_ref, mask_ref, out_ref, sums_ref):
    own, other = halves(weight_ref, core_ref[0], weight_ref.shape[0] // 2)
    back = dot_nt(up_ref[...], weight_ref[own, :]) + got_ref[...].astype(f32)
    hat = normed(raw_ref, moments_ref)
    grad = back * widen(mask_ref, raw_ref.shape[1]) * silu_slope(scaled(norm_ref, hat))
    out_ref[...] = grad
    put_sums(sums_ref, grad, hat)


def moved_grads(grad, cols, rows, width, grid):
    wide = grad.astype(f32)
    out = {}
    for col in cols:
        moved = grad if col == 0 else shift_cols(wide, col, width).astype(bf16)
        for row in rows:
            out[row, col] = shift_rows(moved, row, width, grid)
    return out


def back_five_kernel(grid, width, core_ref, got_ref, grad_ref, raw_ref, moments_ref, norm_ref, mask_ref, weight_ref,
                     out_ref, norm_grad_ref, send_ref):
    sums = sums_of(got_ref, core_ref[0])
    beta, gamma = sums[0:1], sums[1:2]
    norm_grad_ref[...] = jnp.concatenate([gamma, beta], axis=0)
    grad = norm_back(grad_ref[...], normed(raw_ref, moments_ref), moments_ref, norm_ref, beta, gamma,
                     widen(mask_ref, raw_ref.shape[1]))
    out_ref[...] = grad
    own, other = halves(weight_ref, core_ref[0], weight_ref.shape[2] // 2)
    moved = moved_grads(grad, (-1, 0, 1), (-1, 0, 1), width, grid)
    back = functools.reduce(
        jnp.add, [dot_nt(moved[1 - r, 1 - s], weight_ref[r, s, other, :]) for r in range(3) for s in range(3)])
    send_ref[...] = back.astype(bf16)


def own_five_kernel(grid, width, core_ref, up_ref, got_ref, weight_ref, raw_ref, moments_ref, norm_ref, mask_ref, out_ref,
                    sums_ref):
    own, other = halves(weight_ref, core_ref[0], weight_ref.shape[2] // 2)
    moved = moved_grads(up_ref[...], (-1, 0, 1), (-1, 0, 1), width, grid)
    back = functools.reduce(
        jnp.add, [dot_nt(moved[1 - r, 1 - s], weight_ref[r, s, own, :]) for r in range(3) for s in range(3)])
    hat = normed(raw_ref, moments_ref)
    grad = (back + got_ref[...].astype(f32)) * widen(mask_ref, raw_ref.shape[1]) * silu_slope(scaled(norm_ref, hat))
    out_ref[...] = grad
    put_sums(sums_ref, grad, hat)


def own_four_kernel(core_ref, up_ref, got_ref, weight_ref, top_ref, three_ref, moments_three_ref, norm_three_ref, skip_ref,
                    moments_skip_ref, norm_skip_ref, mask_ref, out_ref, sums_ref):
    own, other = halves(weight_ref, core_ref[0], weight_ref.shape[0] // 2)
    back = dot_nt(up_ref[...], weight_ref[own, :]) + got_ref[...].astype(f32) + top_ref[...]
    hat_three = normed(three_ref, moments_three_ref)
    hat_skip = normed(skip_ref, moments_skip_ref)
    joined = scaled(norm_three_ref, hat_three) + scaled(norm_skip_ref, hat_skip)
    grad = back * widen(mask_ref, joined.shape[1]) * silu_slope(joined)
    out_ref[...] = grad
    put_sums(sums_ref, grad, hat_three, hat_skip)


def back_join_kernel(core_ref, got_ref, grad_ref, three_ref, moments_three_ref, norm_three_ref, skip_ref, moments_skip_ref,
                     norm_skip_ref, mask_ref, weight_ref, out_three_ref, out_skip_ref, norm_three_grad_ref,
                     norm_skip_grad_ref, send_ref):
    sums = sums_of(got_ref)
    beta, gamma_three, gamma_skip = sums[0:1], sums[1:2], sums[2:3]
    norm_three_grad_ref[...] = jnp.concatenate([gamma_three, beta], axis=0)
    norm_skip_grad_ref[...] = jnp.concatenate([gamma_skip, beta], axis=0)
    mask = widen(mask_ref, three_ref.shape[1])
    grad = norm_back(grad_ref[...], normed(three_ref, moments_three_ref), moments_three_ref, norm_three_ref, beta,
                     gamma_three, mask)
    out_three_ref[...] = grad
    own, other = halves(weight_ref, core_ref[0], weight_ref.shape[0] // 2)
    send_ref[...] = dot_nt(grad, weight_ref[other, :]).astype(bf16)
    out_skip_ref[...] = norm_back(grad_ref[...], normed(skip_ref, moments_skip_ref), moments_skip_ref, norm_skip_ref, beta,
                                  gamma_skip, mask)


def planes_back(moved, weight_ref, at):
    def term(r, s, row, col):
        return dot_nt(moved[row, col], weight_ref[r, s, at, :])

    return [
        term(1, 1, 0, 0),
        term(1, 2, 0, 0) + term(1, 0, 0, 1),
        term(2, 1, 0, 0) + term(0, 1, 1, 0),
        term(2, 2, 0, 0) + term(2, 0, 0, 1) + term(0, 2, 1, 0) + term(0, 0, 1, 1),
    ]


def back_two_kernel(grid, width, core_ref, got_ref, grad_ref, raw_ref, moments_ref, norm_ref, mask_ref, weight_ref, out_ref,
                    norm_grad_ref, send_ref):
    sums = sums_of(got_ref, core_ref[0])
    beta, gamma = sums[0:1], sums[1:2]
    norm_grad_ref[...] = jnp.concatenate([gamma, beta], axis=0)
    grad = norm_back(grad_ref[...], normed(raw_ref, moments_ref), moments_ref, norm_ref, beta, gamma,
                     widen(mask_ref, raw_ref.shape[1]))
    out_ref[...] = grad
    own, other = halves(weight_ref, core_ref[0], weight_ref.shape[2] // 2)
    rows = grad.shape[0]
    for plane, back in enumerate(planes_back(moved_grads(grad, (0, 1), (0, 1), width, grid), weight_ref, other)):
        send_ref[plane * rows : (plane + 1) * rows, :] = back.astype(bf16)


def own_two_kernel(grid, width, core_ref, up_ref, got_ref, weight_ref, raw_ref, moments_ref, norm_ref, mask_ref, out_ref,
                   sums_ref):
    own, other = halves(weight_ref, core_ref[0], weight_ref.shape[2] // 2)
    rows = up_ref.shape[0]
    mask = widen(mask_ref, raw_ref.shape[1])
    beta = jnp.zeros((1, raw_ref.shape[1]), f32)
    gamma = beta
    for plane, back in enumerate(planes_back(moved_grads(up_ref[...], (0, 1), (0, 1), width, grid), weight_ref, own)):
        at = slice(plane * rows, (plane + 1) * rows)
        hat = (raw_ref[at, :] - moments_ref[0:1]) * moments_ref[1:2]
        grad = (back + got_ref[at, :].astype(f32)) * mask * silu_slope(scaled(norm_ref, hat))
        out_ref[at, :] = grad
        beta = beta + jnp.sum(grad, axis=0, keepdims=True)
        gamma = gamma + jnp.sum(grad * hat, axis=0, keepdims=True)
    put_rows(sums_ref, [beta, gamma])


def back_one_kernel(core_ref, got_ref, grad_ref, raw_ref, moments_ref, norm_ref, mask_ref, weight_ref, up_skip_ref,
                    shortcut_ref, out_ref, norm_grad_ref, send_ref):
    sums = sums_of(got_ref, core_ref[0])
    beta, gamma = sums[0:1], sums[1:2]
    norm_grad_ref[...] = jnp.concatenate([gamma, beta], axis=0)
    mask = jnp.concatenate([widen(mask_ref, raw_ref.shape[1])] * 4, axis=0)
    grad = norm_back(grad_ref[...], normed(raw_ref, moments_ref), moments_ref, norm_ref, beta, gamma, mask)
    out_ref[...] = grad
    own, other = halves(weight_ref, core_ref[0], weight_ref.shape[0] // 2)
    rows = mask_ref.shape[0]
    skip = dot_nt(up_skip_ref[...], shortcut_ref[other, :])
    send_ref[:rows, :] = (dot_nt(grad[:rows], weight_ref[other, :]) + skip).astype(bf16)
    send_ref[rows:, :] = dot_nt(grad[rows:], weight_ref[other, :]).astype(bf16)


def own_x_kernel(grid, width, core_ref, up_ref, got_ref, weight_ref, up_skip_ref, shortcut_ref, mask_ref, out_ref):
    own, other = halves(weight_ref, core_ref[0], weight_ref.shape[0] // 2)
    rows = mask_ref.shape[0]
    imgs = out_ref.shape[0]
    back = dot_nt(up_ref[...], weight_ref[own, :]) + got_ref[...].astype(f32)
    skip = dot_nt(up_skip_ref[...], shortcut_ref[own, :])
    mask = widen(mask_ref, back.shape[1])
    planes = [back[:rows] + skip] + [back[at * rows : (at + 1) * rows] for at in range(1, 4)]
    planes = [(plane * mask).astype(bf16) for plane in planes]
    size = 4 * grid
    target = lax.broadcasted_iota(jnp.int32, (size, size), 1)
    source = lax.broadcasted_iota(jnp.int32, (size, size), 0)
    place = jnp.where(source == pixel_of(target, grid, width), 1.0, 0.0).astype(bf16)
    for n in range(imgs):
        ordered = jnp.concatenate([plane[n * grid : (n + 1) * grid] for plane in planes], axis=0)
        out_ref[n] = dot(place, ordered).astype(bf16)


def turn(value):
    return value.astype(f32).T.astype(bf16)


def put_parts(outs, start, total_ref, far_at):
    size = total_ref.shape[0] // len(outs)
    for b, out in enumerate(outs):
        first = pl.multiple_of((far_at ^ b) * size, size)
        out[start : start + size, :] = total_ref[pl.ds(first, size), :].astype(bf16)
    return start + size


def put_tap_parts(outs, start, total_ref, far_at):
    size = total_ref.shape[1] // len(outs)
    for b, out in enumerate(outs):
        first = pl.multiple_of((far_at ^ b) * size, size)
        for tap in range(9):
            at = start + tap * size
            out[at : at + size, :] = total_ref[tap, pl.ds(first, size), :].astype(bf16)
    return start + 9 * size


def add_into(ref, at, part, block):
    ref[at] = part if block == 0 else ref[at] + part


def weight_top_kernel(grid, width, near, far, core_ref, near_at_ref, own_five_ref, other_five_ref, *refs):
    up_six, act_four, up_five = refs[:near], refs[near : 2 * near], refs[2 * near : 3 * near]
    out_ref, dense_ref, taps_ref = refs[3 * near :]
    rows = up_six[0].shape[0]
    depth = own_five_ref.shape[1]
    for half, act_ref in zip(halves(None, core_ref[0], depth), (own_five_ref, other_five_ref)):
        for block in range(near):
            first = pl.multiple_of((near_at_ref[0] ^ block) * rows, rows)
            add_into(dense_ref, half, dot(turn(act_ref[pl.ds(first, rows), :]), up_six[block][...]), block)
    for block in range(near):
        turned = turn(act_four[block][...])
        moved = moved_grads(up_five[block][...], (-1, 0, 1), (-1, 0, 1), width, grid)
        for r in range(3):
            for s in range(3):
                add_into(taps_ref, 3 * r + s, dot(turned, moved[1 - r, 1 - s]), block)
    start = 0
    for owner in range(far):
        size = dense_ref.shape[0] // far
        out_ref[start : start + size, :] = dense_ref[owner * size : (owner + 1) * size, :].astype(bf16)
        start += size
        size = taps_ref.shape[1] // far
        for tap in range(9):
            out_ref[start : start + size, :] = taps_ref[tap, owner * size : (owner + 1) * size, :].astype(bf16)
            start += size


def weight_four_kernel(near, core_ref, near_at_ref, own_ref, other_ref, up_ref, *refs):
    outs, sum_ref = refs[:near], refs[near]
    own, other = halves(None, core_ref[0], own_ref.shape[1])
    sum_ref[own, :] = dot(turn(own_ref[...]), up_ref[...])
    sum_ref[other, :] = dot(turn(other_ref[...]), up_ref[...])
    put_parts(outs, 0, sum_ref, near_at_ref[0])


def weight_bottom_kernel(near, far, split, core_ref, near_at_ref, far_at_ref, own_ref, other_ref, *refs):
    parts, up_join = refs[:near], refs[near : 2 * near]
    outs, (reduce_ref, expand_ref, shortcut_ref) = refs[2 * near : 2 * near + far], refs[2 * near + far :]
    rows, lanes = up_join[0].shape[0], up_join[0].shape[1] // 2
    depth = own_ref.shape[1] - split
    reduce_ref[...] = functools.reduce(jnp.add, [part[...].astype(f32) for part in parts])
    for half, act_ref in zip(halves(None, core_ref[0], split), (own_ref, other_ref)):
        for block in range(near):
            first = pl.multiple_of((near_at_ref[0] ^ block) * rows, rows)
            turned = turn(act_ref[pl.ds(first, rows), :])
            add_into(shortcut_ref, half, dot(turned[:split], up_join[block][:, lanes:]), block)
    for half, act_ref in zip(halves(None, core_ref[0], depth), (own_ref, other_ref)):
        for block in range(near):
            first = pl.multiple_of((near_at_ref[0] ^ block) * rows, rows)
            turned = turn(act_ref[pl.ds(first, rows), split:])
            add_into(expand_ref, half, dot(turned, up_join[block][:, :lanes]), block)
    start = put_parts(outs, 0, reduce_ref, far_at_ref[0])
    start = put_parts(outs, start, expand_ref, far_at_ref[0])
    put_parts(outs, start, shortcut_ref, far_at_ref[0])


def weight_two_kernel(grid, width, near, far, far_at_ref, *refs):
    acts, ups, outs, taps_ref = refs[:near], refs[near : 2 * near], refs[2 * near : 2 * near + far], refs[2 * near + far]
    rows = ups[0].shape[0]
    for block in range(near):
        moved = moved_grads(ups[block][...], (0, 1), (0, 1), width, grid)
        for plane in range(4):
            turned = turn(acts[block][plane * rows : (plane + 1) * rows, :])
            for r in ((1,) if plane < 2 else (0, 2)):
                for s in ((1,) if plane % 2 == 0 else (0, 2)):
                    add_into(taps_ref, 3 * r + s, dot(turned, moved[int(r == 0), int(s == 0)]), block)
    put_tap_parts(outs, 0, taps_ref, far_at_ref[0])


def weight_one_kernel(near, core_ref, near_at_ref, own_ref, other_ref, up_ref, *refs):
    outs, sum_ref = refs[:near], refs[near]
    own, other = halves(None, core_ref[0], own_ref.shape[1])
    sum_ref[own, :] = dot(turn(own_ref[...]), up_ref[...])
    sum_ref[other, :] = dot(turn(other_ref[...]), up_ref[...])
    put_parts(outs, 0, sum_ref, near_at_ref[0])


def solution(mesh):
    count = mesh.shape["dp"]
    near = 4
    far = count // near
    def to_near(pieces):
        return [pieces[0]] + [send(pieces[b], count, b) for b in range(1, near)]

    def to_far(pieces):
        return [pieces[0]] + [send(pieces[b].astype(bf16), count, b * near) for b in range(1, far)]

    def tell_far(value):
        return [value] + [send(value, count, b * near) for b in range(1, far)]

    far_groups = [[at * near + b for at in range(far)] for b in range(near)]
    near_groups = [[at * near + b for b in range(near)] for at in range(far)]

    def gather_near(value):
        return lax.all_gather(value, "dp", axis=0, tiled=True, axis_index_groups=near_groups)

    def near_chunks(rows):
        return [(b, at * (rows // far), b, True, at) for b in range(near) for at in range(far)]

    def total(pieces):
        return functools.reduce(jnp.add, [piece.astype(f32) for piece in pieces])

    def local(images, extents, cotangent, reduce1, spatial1, expand1, shortcut, reduce2, spatial2, expand2,
              norm_one, norm_two, norm_three, norm_skip, norm_four, norm_five, norm_six):
        core = lax.axis_index("chan")
        place = lax.axis_index("dp")
        near_at, far_at = place % near, place // near
        near_order = [near_at ^ b for b in range(near)]
        far_order = [far_at ^ b for b in range(far)]
        imgs, height, width = cotangent.shape[:3]
        grid = height * width
        outer = imgs * grid
        cid = images.shape[3]
        mid = reduce1.shape[1]
        wide = cotangent.shape[3]
        share = 2 * mid // near
        near_place = near_at.reshape(1).astype(jnp.int32)
        far_place = far_at.reshape(1).astype(jnp.int32)
        core_at = core.reshape(1).astype(jnp.int32)

        cell = lax.broadcasted_iota(jnp.int32, (imgs, grid), 1)
        valid = (cell // width < extents[:, 0:1]) & (cell % width < extents[:, 1:2])
        mask = jnp.broadcast_to(valid.astype(f32).reshape(outer, 1), (outer, 128))
        cells = jnp.sum(extents[:, 0] * extents[:, 1]).astype(f32).reshape(1)

        def gridded(body):
            return functools.partial(body, grid, width)

        def spread(local_sums, both):
            return lax.all_to_all(local_sums, ("dp", "chan") if both else "dp", 0, 0, tiled=True)

        first_sums = ((2 * count, 4, mid), f32)
        narrow_sums = ((2 * count, 2, mid), f32)
        own_sums = ((2 * count, 2, mid), f32)
        wide_sums = ((count, 2, wide), f32)
        join_sums = ((count, 4, wide), f32)
        all_cells_out = ((count, 128), f32)
        narrow_moments = ((8, mid), f32)
        wide_moments = ((8, wide), f32)
        inner = 4 * outer

        norms = jnp.concatenate([norm_one, norm_two, norm_four, norm_five])
        norms = in_order(core, norms, swap(norms))
        both_one, both_two, both_four, both_five = norms[0:2], norms[2:4], norms[4:6], norms[6:8]

        own_x, = run_kernel(gridded(sort_kernel), [((inner, cid), bf16)], [],
                            [images.reshape(imgs, 4 * grid, cid), mask], flops=2 * imgs * 16 * grid * grid * cid)
        other_x = swap(own_x)
        conv_one, sums = run_kernel(conv_one_kernel, [((inner, mid), f32), first_sums], [core_at, cells],
                                    [own_x, other_x, reduce1, mask], flops=4 * inner * cid * mid)
        got = spread(sums, True)
        other_one = swap(conv_one)
        conv_skip, skip_stats = run_kernel(conv_skip_kernel, [((outer, wide), f32), ((2, wide), f32)], [core_at, cells],
                                           [own_x, other_x, shortcut, mask], flops=4 * outer * cid * wide)
        act_one, conv_two, sums, moments_one, all_cells = run_kernel(
            gridded(conv_two_kernel),
            [((inner, 2 * mid), bf16), ((outer, mid), f32), narrow_sums, narrow_moments, all_cells_out], [core_at, cells],
            [got, conv_one, other_one, both_one, mask, spatial1], flops=36 * outer * mid * mid,
            scratch=[pltpu.VMEM((inner, 2 * mid), f32)])
        act_one, sums = tie(act_one, sums)
        got = spread(sums, True)
        other_two = swap(conv_two)
        near_one = [slot(act_one, at, share, 1) for at in near_order]
        near_one[1] = send(near_one[1], count, 1)
        near_one[1], got = tie(near_one[1], got)
        act_two, conv_three, sums, moments_two = run_kernel(
            expand_kernel, [((outer, 2 * mid), bf16), ((outer, wide), f32), join_sums, narrow_moments], [core_at, cells],
            [got, all_cells, conv_two, other_two, both_two, mask, expand1, skip_stats], flops=4 * outer * mid * wide,
            scratch=[pltpu.VMEM((outer, 2 * mid), f32)])
        near_one[2], sums = tie(near_one[2], sums)
        got = spread(sums, False)
        near_one[2] = send(near_one[2], count, 2)
        near_one[2], got = tie(near_one[2], got)
        block_one, moments_three, moments_skip = run_kernel(
            join_kernel, [((outer, wide), bf16), wide_moments, wide_moments], [],
            [got, all_cells, conv_three, conv_skip, norm_three, norm_skip, mask], flops=20 * outer * wide)
        other_block = swap(block_one)
        conv_four, sums = run_kernel(conv_four_kernel, [((outer, mid), f32), narrow_sums], [core_at, cells],
                                     [block_one, other_block, reduce2, mask], flops=4 * outer * wide * mid)
        near_one[3], sums = tie(near_one[3], sums)
        got = spread(sums, True)
        near_one[3] = send(near_one[3], count, 3)
        near_one[3], got = tie(near_one[3], got)
        other_four = swap(conv_four)
        act_four, conv_five, sums, moments_four = run_kernel(
            gridded(conv_five_kernel),
            [((outer, 2 * mid), bf16), ((outer, mid), f32), narrow_sums, narrow_moments], [core_at, cells],
            [got, all_cells, conv_four, other_four, both_four, mask, spatial2], flops=36 * outer * mid * mid,
            scratch=[pltpu.VMEM((outer, 2 * mid), f32)])
        (own_x, act_two), sums = tie((own_x, act_two), sums)
        got = spread(sums, True)
        own_two = slot(act_two, core, mid, 1)
        skip_two, got = tie(jnp.concatenate([own_x[:outer], own_two], axis=1), got)
        near_skip = gather_near(skip_two)
        other_five = swap(conv_five)
        act_five, conv_six, sums, moments_five = run_kernel(
            expand_kernel, [((outer, 2 * mid), bf16), ((outer, wide), f32), wide_sums, narrow_moments], [core_at, cells],
            [got, all_cells, conv_five, other_five, both_five, mask, expand2], flops=4 * outer * mid * wide,
            scratch=[pltpu.VMEM((outer, 2 * mid), f32)])
        act_four, sums = tie(act_four, sums)
        got = spread(sums, False)
        near_four = to_near([slot(act_four, at, share, 1) for at in near_order])
        near_four, got = tie(near_four, got)
        near_five = gather_near(slot(act_five, core, mid, 1))
        block_two, grad_join2, sums, moments_six = run_kernel(
            top_kernel, [((outer, wide), bf16), ((outer, wide), f32), wide_sums, wide_moments], [],
            [got, all_cells, conv_six, block_one, cotangent.reshape(outer, wide), norm_six, mask], flops=30 * outer * wide)
        got = spread(sums, False)

        norm_out = ((2, mid), f32)
        wide_norm_out = ((2, wide), f32)
        grad_six, norm_six_grad, part = run_kernel(
            functools.partial(back_dense_kernel, False), [((outer, wide), bf16), wide_norm_out, ((outer, mid), bf16)], [core_at],
            [got, grad_join2, conv_six, moments_six, norm_six, mask, expand2], flops=2 * outer * wide * mid)
        part = swap(part)
        grad_pre, sums = run_kernel(
            own_dense_kernel, [((outer, mid), f32), own_sums], [core_at],
            [grad_six, part, expand2, conv_five, moments_five, norm_five, mask], flops=2 * outer * wide * mid)
        grad_six, sums = tie(grad_six, sums)
        got = spread(sums, True)
        up_six = to_near([slot(grad_six, at, mid, 1) for at in near_order])
        up_six, got = tie(up_six, got)

        grad_five, norm_five_grad, part = run_kernel(
            gridded(back_five_kernel), [((outer, mid), bf16), norm_out, ((outer, mid), bf16)], [core_at],
            [got, grad_pre, conv_five, moments_five, norm_five, mask, spatial2], flops=18 * outer * mid * mid)
        part = swap(part)
        grad_pre, sums = run_kernel(
            gridded(own_five_kernel), [((outer, mid), f32), own_sums], [core_at],
            [grad_five, part, spatial2, conv_four, moments_four, norm_four, mask], flops=18 * outer * mid * mid)
        grad_five, sums = tie(grad_five, sums)
        got = spread(sums, True)
        up_five = to_near([grad_five] * near)
        (up_five, near_skip, near_five), got = tie((up_five, near_skip, near_five), got)
        other_near_skip = swap(near_skip)
        other_near_five = swap(near_five)

        grad_four, norm_four_grad, part = run_kernel(
            functools.partial(back_dense_kernel, True), [((outer, mid), bf16), norm_out, ((outer, wide), bf16)], [core_at],
            [got, grad_pre, conv_four, moments_four, norm_four, mask, reduce2], flops=2 * outer * wide * mid)
        part = swap(part)
        grad_join1, sums = run_kernel(
            own_four_kernel, [((outer, wide), f32), join_sums], [core_at],
            [grad_four, part, reduce2, grad_join2, conv_three, moments_three, norm_three, conv_skip, moments_skip, norm_skip,
             mask], flops=2 * outer * wide * mid)
        (grad_four, up_six, up_five, other_near_skip, other_near_five), sums = tie(
            (grad_four, up_six, up_five, other_near_skip, other_near_five), sums)
        got = spread(sums, False)
        reduce2_parts = run_kernel(
            functools.partial(weight_four_kernel, near), [((2 * mid, mid), bf16)] * near, [core_at, near_place],
            [block_one, other_block, grad_four], flops=4 * outer * wide * mid, scratch=[pltpu.VMEM((2 * wide, mid), f32)])
        reduce2_parts = to_near(reduce2_parts)
        rows_a = 2 * mid + 9 * share
        top_part, = run_kernel(
            functools.partial(weight_top_kernel, grid, width, near, far), [((rows_a, mid), bf16)], [core_at, near_place],
            [near_five, other_near_five, *up_six, *near_four, *up_five],
            scratch=[pltpu.VMEM((2 * mid, mid), f32), pltpu.VMEM((9, share, mid), f32)])
        top_part, got = tie(top_part, got)
        top_rows = lax.psum_scatter(top_part, "dp", scatter_dimension=0, tiled=True, axis_index_groups=far_groups)

        grad_three, grad_skip, norm_three_grad, norm_skip_grad, part = run_kernel(
            back_join_kernel,
            [((outer, wide), bf16), ((outer, wide), bf16), wide_norm_out, wide_norm_out, ((outer, mid), bf16)], [core_at],
            [got, grad_join1, conv_three, moments_three, norm_three, conv_skip, moments_skip, norm_skip, mask, expand1],
            flops=2 * outer * wide * mid)
        reduce2_parts, part = tie(reduce2_parts, swap(part))
        grad_pre, sums = run_kernel(
            own_dense_kernel, [((outer, mid), f32), own_sums], [core_at],
            [grad_three, part, expand1, conv_two, moments_two, norm_two, mask], flops=2 * outer * wide * mid)
        got = spread(sums, True)
        up_join = to_near([
            jnp.concatenate([slot(grad_three, at, mid, 1), slot(grad_skip, at, mid, 1)], axis=1) for at in near_order])

        rows_b = (4 * mid + 2 * cid) // far
        bucket_b = run_kernel(
            functools.partial(weight_bottom_kernel, near, far, cid), [((rows_b, mid), bf16)] * far,
            [core_at, near_place, far_place], [near_skip, other_near_skip, *reduce2_parts, *up_join],
            flops=2 * near * outer * (4 * mid + 2 * cid) * mid,
            scratch=[pltpu.VMEM((2 * mid, mid), f32), pltpu.VMEM((2 * mid, mid), f32), pltpu.VMEM((2 * cid, mid), f32)])
        bucket_b, got = tie(bucket_b, got)
        bucket_b = to_far(bucket_b)

        grad_two, norm_two_grad, part = run_kernel(
            gridded(back_two_kernel), [((outer, mid), bf16), norm_out, ((inner, mid), bf16)], [core_at],
            [got, grad_pre, conv_two, moments_two, norm_two, mask, spatial1], flops=18 * outer * mid * mid)
        part = swap(part)
        grad_pre, sums = run_kernel(
            gridded(own_two_kernel), [((inner, mid), f32), own_sums], [core_at],
            [grad_two, part, spatial1, conv_one, moments_one, norm_one, mask], flops=18 * outer * mid * mid)
        (grad_two, bucket_b[2], top_rows), sums = tie((grad_two, bucket_b[2], top_rows), sums)
        top_all = lax.all_gather(top_rows, "dp", axis=0, tiled=True)
        got = spread(sums, True)
        up_two = to_near([grad_two] * near)
        (up_two, bucket_b), got = tie((up_two, bucket_b), got)
        bucket_b = tell_far(total(bucket_b).astype(bf16))

        grad_one, norm_one_grad, part = run_kernel(
            back_one_kernel, [((inner, mid), bf16), norm_out, ((inner, cid), bf16)], [core_at],
            [got, grad_pre, conv_one, moments_one, norm_one, mask, reduce1, grad_skip, shortcut],
            flops=2 * inner * mid * cid)
        part = swap(part)
        reduce1_parts = run_kernel(
            functools.partial(weight_one_kernel, near), [((2 * cid // near, mid), bf16)] * near, [core_at, near_place],
            [own_x, other_x, grad_one], flops=4 * inner * cid * mid, scratch=[pltpu.VMEM((2 * cid, mid), f32)])
        (up_two, bucket_b[2]), reduce1_parts = tie((up_two, bucket_b[2]), reduce1_parts)
        reduce1_parts = to_near(reduce1_parts)
        bucket_c = run_kernel(
            functools.partial(weight_two_kernel, grid, width, near, far), [((9 * share // far, mid), bf16)] * far,
            [far_place], [*near_one, *up_two], flops=18 * near * outer * share * mid,
            scratch=[pltpu.VMEM((9, share, mid), f32)])
        reduce1_rows = total(reduce1_parts).astype(bf16)
        bucket_c = [jnp.concatenate([piece, slot(reduce1_rows, at, reduce1_rows.shape[0] // far, 0)])
                    for piece, at in zip(bucket_c, far_order)]
        bucket_b, bucket_c = tie(bucket_b, bucket_c)
        bucket_c = to_far(bucket_c)
        bucket_b = jnp.concatenate(bucket_b)
        rows_b = bucket_b.shape[0]
        bucket_b = [bucket_b, send(bucket_b, count, 1), send(bucket_b, count, 2)]
        bucket_b, bucket_c = tie(bucket_b, bucket_c)
        bucket_c = tell_far(total(bucket_c).astype(bf16))
        bucket_b.append(send(bucket_b[0], count, 3))
        bucket_b, bucket_c = tie(bucket_b, bucket_c)
        bucket_c = jnp.concatenate(bucket_c)
        rows_c = bucket_c.shape[0]
        bucket_c = to_near([bucket_c] * near)
        input_grad, = run_kernel(
            gridded(own_x_kernel), [((imgs, 4 * grid, cid), bf16)], [core_at],
            [grad_one, part, reduce1, grad_skip, shortcut, mask], flops=4 * inner * mid * cid)

        def lay(arrays, chunks, layouts):
            return laid_out(arrays, chunks, near, far, near_at, far_at, layouts)

        kernel_dims = (3, 3, 2 * mid, mid)
        wide_dims = (2 * mid, 4 * mid)
        chunk = rows_a // far
        top_chunks = [(0, (b * near + member) * chunk, member, False, b) for b in range(far) for member in range(near)]
        expand2_grad, spatial2_grad = lay([top_all], top_chunks, [("columns", wide_dims), ("kernel", kernel_dims)])
        reduce2_grad, expand1_grad, shortcut_grad = lay(
            bucket_b, near_chunks(rows_b),
            [("rows", reduce2.shape), ("columns", wide_dims), ("columns", shortcut.shape)])
        spatial1_grad, reduce1_grad = lay(
            bucket_c, near_chunks(rows_c), [("kernel", kernel_dims), ("rows", reduce1.shape)])
        grads = (reduce1_grad, spatial1_grad, expand1_grad, shortcut_grad, reduce2_grad, spatial2_grad, expand2_grad)
        return (block_one.reshape(cotangent.shape), block_two.reshape(cotangent.shape), input_grad.reshape(images.shape),
                *grads, norm_one_grad, norm_two_grad, norm_three_grad, norm_skip_grad, norm_four_grad, norm_five_grad,
                norm_six_grad)

    pixels = P("dp", None, None, "chan")
    weights = (P(None, "chan"), P(None, None, None, "chan")) + (P(None, "chan"),) * 3 + (P(None, None, None, "chan"), P(None, "chan"))
    norms = (P(None, "chan"),) * 7
    return jax.shard_map(
        local, mesh=mesh,
        in_specs=(pixels, P("dp", None), pixels) + weights + norms,
        out_specs=(pixels, pixels, pixels) + weights + norms,
        check_vma=False)
```

```python
import functools
import math

import jax
import jax.numpy as jnp
from jax import lax
from jax.experimental import pallas as pl
from jax.experimental.pallas import tpu as pltpu
from jax.sharding import PartitionSpec as P

epsilon = 1e-05
f32 = jnp.float32
bf16 = jnp.bfloat16
SWAP = [(0, 1), (1, 0)]


def swap(value):
    return lax.ppermute(value, "chan", SWAP)


def in_order(core, own, other, axis=-1):
    return jnp.where(
        core == 0,
        jnp.concatenate([own, other], axis),
        jnp.concatenate([other, own], axis),
    )


def tie(early, late):
    return lax.optimization_barrier((early, late))


def send(value, count, bits):
    return lax.ppermute(value, "dp", [(at, at ^ bits) for at in range(count)])


def slot(value, index, size, axis):
    return lax.dynamic_slice_in_dim(value, index * size, size, axis)


def lay_kernel(near, far, layouts, chunks, at_ref, *refs):
    ins, outs = refs[: len(refs) - len(layouts)], refs[len(refs) - len(layouts) :]
    near_at, far_at = at_ref[0], at_ref[1]
    for which, start, member, relative, b in chunks:
        owner = far_at ^ b
        if relative:
            member = near_at ^ member
        for (kind, dims), out in zip(layouts, outs):
            if kind == "kernel":
                size = dims[2] // near // far
                for tap in range(9):
                    first = pl.multiple_of(member * (size * far) + owner * size, size)
                    out[tap // 3, tap % 3, pl.ds(first, size), :] = ins[which][start : start + size, :].astype(f32)
                    start += size
            elif kind == "rows":
                size = dims[0] // near // far
                first = pl.multiple_of(member * (size * far) + owner * size, size)
                out[pl.ds(first, size), :] = ins[which][start : start + size, :].astype(f32)
                start += size
            else:
                size, lanes = dims[0] // far, dims[1] // near
                first = pl.multiple_of(owner * size, size)
                lane = pl.multiple_of(member * lanes, lanes)
                out[pl.ds(first, size), pl.ds(lane, lanes)] = ins[which][start : start + size, :].astype(f32)
                start += size


def laid_out(arrays, chunks, near, far, near_at, far_at, layouts):
    return pl.pallas_call(
        functools.partial(lay_kernel, near, far, layouts, chunks),
        out_shape=[jax.ShapeDtypeStruct(dims, f32) for _, dims in layouts],
        in_specs=[pl.BlockSpec(memory_space=pltpu.SMEM)] + [pl.BlockSpec(memory_space=pltpu.VMEM)] * len(arrays),
        out_specs=[pl.BlockSpec(memory_space=pltpu.VMEM)] * len(layouts),
        compiler_params=pltpu.CompilerParams(vmem_limit_bytes=40 * 2**20),
    )(jnp.stack([near_at, far_at]).astype(jnp.int32), *arrays)


def spec(kind):
    return pl.BlockSpec(memory_space=kind)


def staged(body, scalars, ins, outs, held, *refs):
    head, refs = refs[:scalars], refs[scalars:]
    given, results, refs = refs[:ins], refs[ins : ins + outs], refs[ins + outs :]
    moved = [at for at in range(ins) if at not in held]
    here, made, extra = refs[: len(moved)], refs[len(moved) : len(moved) + outs], refs[len(moved) + outs : -2]
    in_sems, out_sems = refs[-2:]
    arrivals = [pltpu.make_async_copy(given[at], here[k], in_sems.at[k]) for k, at in enumerate(moved)]
    for copy in arrivals:
        copy.start()
    for copy in arrivals:
        copy.wait()
    local = dict(zip(moved, here))
    body(*head, *[local.get(at, given[at]) for at in range(ins)], *made, *extra)
    leaving = [pltpu.make_async_copy(made[at], results[at], out_sems.at[at]) for at in range(outs)]
    for copy in leaving:
        copy.start()
    for copy in leaving:
        copy.wait()


def run_kernel(body, outs, scalars, arrays, flops=0, scratch=(), held=()):
    return pl.pallas_call(
        functools.partial(staged, body, len(scalars), len(arrays), len(outs), held),
        out_shape=[pltpu.HBM(shape, dtype) for shape, dtype in outs],
        in_specs=[spec(pltpu.SMEM)] * len(scalars)
        + [spec(pltpu.VMEM if at in held else pltpu.HBM) for at in range(len(arrays))],
        out_specs=[spec(pltpu.HBM)] * len(outs),
        scratch_shapes=[pltpu.VMEM(x.shape, x.dtype) for at, x in enumerate(arrays) if at not in held]
        + [pltpu.VMEM(shape, dtype) for shape, dtype in outs]
        + list(scratch) + [pltpu.SemaphoreType.DMA((len(arrays),)), pltpu.SemaphoreType.DMA((len(outs),))],
        cost_estimate=pl.CostEstimate(flops=1, bytes_accessed=1, transcendentals=0),
        compiler_params=pltpu.CompilerParams(vmem_limit_bytes=28 * 2**20),
    )(*scalars, *[x if at in held else pltpu.with_memory_space_constraint(x, pltpu.HBM) for at, x in enumerate(arrays)])


def widen(mask_ref, lanes):
    mask = mask_ref[...]
    return mask if lanes == 128 else jnp.concatenate([mask] * (lanes // 128), axis=1)


def dot(left, right):
    return lax.dot_general(left, right, (((1,), (0,)), ((), ())), preferred_element_type=f32)


def dot_nt(left, right):
    return lax.dot_general(left, right, (((1,), (1,)), ((), ())), preferred_element_type=f32)


def halves(ref, core, size):
    own = pl.ds(pl.multiple_of(core * size, size), size)
    other = pl.ds(pl.multiple_of((1 - core) * size, size), size)
    return own, other


def stats(values, mask, cells):
    total = jnp.sum(values * mask, axis=0, keepdims=True)
    centred = (values - total / cells) * mask
    return [total, jnp.sum(centred * centred, axis=0, keepdims=True)]


def put_rows(out_ref, rows):
    tile = jnp.concatenate(rows, axis=0)
    for at in range(out_ref.shape[0]):
        out_ref[at] = tile


def moments(tiles, cells_ref, scale=1.0, first=0):
    lanes = tiles[0].shape[1]
    cells = jnp.concatenate([cells_ref[...]] * (lanes // 128), axis=1) * scale
    pixels = jnp.sum(cells, axis=0, keepdims=True)
    totals = [tile[first : first + 1] for tile in tiles]
    mean = functools.reduce(jnp.add, totals) / pixels
    spread = functools.reduce(jnp.add, [tile[first + 1 : first + 2] for tile in tiles])
    offsets = jnp.concatenate(totals, axis=0) / cells - mean
    spread = spread + jnp.sum(cells * offsets * offsets, axis=0, keepdims=True)
    return mean, lax.rsqrt(spread / pixels + epsilon), pixels


def put_moments(out_ref, mean, inverse, pixels):
    lanes = mean.shape[1]
    out_ref[...] = jnp.concatenate([mean, inverse, pixels, jnp.zeros((5, lanes), f32)], axis=0)


def silu_slope(values):
    logistic = jax.nn.sigmoid(values)
    return logistic * (1.0 + values * (1.0 - logistic))


def shift_cols(values, by, width):
    rows = values.shape[0]
    column = lax.broadcasted_iota(jnp.int32, values.shape, 0) & (width - 1)
    moved = pltpu.roll(values, (-by) % rows, 0)
    return jnp.where(column == (0 if by < 0 else width - 1), 0.0, moved)


def shift_rows(values, by, width, grid):
    if by == 0:
        return values
    zeros = jnp.zeros((width, values.shape[1]), values.dtype)
    out = []
    for start in range(0, values.shape[0], grid):
        if by < 0:
            out += [zeros, values[start : start + grid - width]]
        else:
            out += [values[start + width : start + grid], zeros]
    return jnp.concatenate(out, axis=0)


def pixel_of(index, grid, width):
    plane = jnp.zeros_like(index)
    for at in range(1, 4):
        plane = plane + (index >= at * grid).astype(jnp.int32)
    inside = index - plane * grid
    line = inside >> (width.bit_length() - 1)
    column = inside & (width - 1)
    return (2 * line + (plane >> 1)) * (2 * width) + 2 * column + (plane & 1)


def sort_kernel(grid, width, images_ref, mask_ref, out_ref):
    size = 4 * grid
    target = lax.broadcasted_iota(jnp.int32, (size, size), 0)
    source = lax.broadcasted_iota(jnp.int32, (size, size), 1)
    pick = jnp.where(source == pixel_of(target, grid, width), 1.0, 0.0).astype(bf16)
    imgs = images_ref.shape[0]
    lanes = images_ref.shape[2]
    mask = widen(mask_ref, lanes)
    for n in range(imgs):
        ordered = dot(pick, images_ref[n])
        for plane in range(4):
            first = (plane * imgs + n) * grid
            rows = ordered[plane * grid : (plane + 1) * grid] * mask[n * grid : (n + 1) * grid]
            out_ref[first : first + grid, :] = rows.astype(bf16)


def conv_one_kernel(core_ref, cells_ref, own_ref, other_ref, weight_ref, mask_ref, out_ref, stats_ref):
    own, other = halves(weight_ref, core_ref[0], own_ref.shape[1])
    values = dot(own_ref[...], weight_ref[own, :]) + dot(other_ref[...], weight_ref[other, :])
    out_ref[...] = values
    mask = widen(mask_ref, values.shape[1])
    cells = jnp.full((1, values.shape[1]), cells_ref[0])
    put_rows(stats_ref, stats(values, jnp.concatenate([mask] * 4, axis=0), 4.0 * cells_ref[0]) + [cells, cells])


def conv_skip_kernel(core_ref, cells_ref, own_ref, other_ref, weight_ref, mask_ref, out_ref, stats_ref):
    rows = mask_ref.shape[0]
    own, other = halves(weight_ref, core_ref[0], own_ref.shape[1])
    values = dot(own_ref[:rows], weight_ref[own, :]) + dot(other_ref[:rows], weight_ref[other, :])
    out_ref[...] = values
    mask = widen(mask_ref, values.shape[1])
    stats_ref[...] = jnp.concatenate(stats(values, mask, cells_ref[0]), axis=0)


def norm_act(got_ref, all_cells_ref, scale, own_ref, other_ref, norm_ref, mask, core, raw_ref, act_ref, moments_ref):
    lanes = own_ref.shape[1]
    own, other = halves(None, core, lanes)
    raw_ref[:, own] = own_ref[...]
    raw_ref[:, other] = other_ref[...]
    count = got_ref.shape[0] // 2
    for half in range(2):
        mean, inverse, pixels = moments([got_ref[2 * at + half] for at in range(count)], all_cells_ref, scale)

        @pl.when(core == half)
        def _():
            put_moments(moments_ref, mean, inverse, pixels)

        at = slice(half * lanes, (half + 1) * lanes)
        pre = norm_ref[0:1, at] * ((raw_ref[:, at] - mean) * inverse) + norm_ref[1:2, at]
        act_ref[:, at] = (pre * jax.nn.sigmoid(pre) * mask).astype(bf16)


def conv_two_kernel(grid, width, core_ref, cells_ref, got_ref, own_ref, other_ref, norm_ref, mask_ref, weight_ref,
                    act_ref, out_ref, stats_ref, moments_ref, all_cells_ref, raw_ref):
    rows = mask_ref.shape[0]
    lanes = own_ref.shape[1]
    mask = widen(mask_ref, lanes)
    for at in range(got_ref.shape[0] // 2):
        all_cells_ref[at : at + 1, :] = got_ref[2 * at, 2:3, :128]
    norm_act(got_ref, all_cells_ref, 4.0, own_ref, other_ref, norm_ref, jnp.concatenate([mask] * 4, axis=0), core_ref[0],
             raw_ref, act_ref, moments_ref)
    values = jnp.zeros((rows, out_ref.shape[1]), f32)
    for plane in range(4):
        here = act_ref[plane * rows : (plane + 1) * rows, :]
        by_col = {1: here} if plane % 2 == 0 else {2: here, 0: shift_cols(here.astype(f32), -1, width).astype(bf16)}
        for s, moved in by_col.items():
            for r in ((1,) if plane < 2 else (0, 2)):
                values = values + dot(shift_rows(moved, -1 if r == 0 else 0, width, grid), weight_ref[r, s])
    out_ref[...] = values
    put_rows(stats_ref, stats(values, mask, cells_ref[0]))


def conv_five_kernel(grid, width, core_ref, cells_ref, got_ref, all_cells_ref, own_ref, other_ref, norm_ref, mask_ref, weight_ref,
                     act_ref, out_ref, stats_ref, moments_ref, raw_ref):
    rows = mask_ref.shape[0]
    mask = widen(mask_ref, own_ref.shape[1])
    norm_act(got_ref, all_cells_ref, 1.0, own_ref, other_ref, norm_ref, mask, core_ref[0], raw_ref, act_ref, moments_ref)
    values = jnp.zeros((rows, out_ref.shape[1]), f32)
    here = act_ref[...]
    for s in range(3):
        moved = here if s == 1 else shift_cols(here.astype(f32), s - 1, width).astype(bf16)
        for r in range(3):
            values = values + dot(shift_rows(moved, r - 1, width, grid), weight_ref[r, s])
    out_ref[...] = values
    put_rows(stats_ref, stats(values, mask, cells_ref[0]))


def expand_kernel(core_ref, cells_ref, got_ref, all_cells_ref, own_ref, other_ref, norm_ref, mask_ref, weight_ref, *refs):
    more_refs, (act_ref, out_ref, stats_ref, moments_ref, raw_ref) = refs[:-5], refs[-5:]
    norm_act(got_ref, all_cells_ref, 1.0, own_ref, other_ref, norm_ref, widen(mask_ref, own_ref.shape[1]), core_ref[0],
             raw_ref, act_ref, moments_ref)
    values = dot(act_ref[...], weight_ref[...])
    out_ref[...] = values
    more = [more_refs[0][...]] if more_refs else []
    put_rows(stats_ref, stats(values, widen(mask_ref, values.shape[1]), cells_ref[0]) + more)


def normed(raw_ref, moments_ref):
    return (raw_ref[...] - moments_ref[0:1]) * moments_ref[1:2]


def scaled(norm_ref, hat):
    return norm_ref[0:1] * hat + norm_ref[1:2]


def join_kernel(got_ref, all_cells_ref, three_ref, skip_ref, norm_three_ref, norm_skip_ref, mask_ref, out_ref, moments_three_ref,
                moments_skip_ref):
    tiles = [got_ref[at] for at in range(got_ref.shape[0])]
    put_moments(moments_three_ref, *moments(tiles, all_cells_ref))
    put_moments(moments_skip_ref, *moments(tiles, all_cells_ref, first=2))
    joined = scaled(norm_three_ref, normed(three_ref, moments_three_ref)) + scaled(
        norm_skip_ref, normed(skip_ref, moments_skip_ref))
    out_ref[...] = (joined * jax.nn.sigmoid(joined) * widen(mask_ref, joined.shape[1])).astype(bf16)


def conv_four_kernel(core_ref, cells_ref, own_ref, other_ref, weight_ref, mask_ref, out_ref, stats_ref):
    own, other = halves(weight_ref, core_ref[0], own_ref.shape[1])
    values = dot(own_ref[...], weight_ref[own, :]) + dot(other_ref[...], weight_ref[other, :])
    out_ref[...] = values
    put_rows(stats_ref, stats(values, widen(mask_ref, values.shape[1]), cells_ref[0]))


def put_sums(out_ref, grad, *hats):
    rows = [jnp.sum(grad, axis=0, keepdims=True)] + [jnp.sum(grad * hat, axis=0, keepdims=True) for hat in hats]
    put_rows(out_ref, rows + [rows[0]] * (out_ref.shape[1] - len(rows)))


def top_kernel(got_ref, all_cells_ref, six_ref, block_ref, cotangent_ref, norm_ref, mask_ref, out_ref, grad_ref, sums_ref, moments_ref):
    put_moments(moments_ref, *moments([got_ref[at] for at in range(got_ref.shape[0])], all_cells_ref))
    hat = normed(six_ref, moments_ref)
    joined = scaled(norm_ref, hat) + block_ref[...].astype(f32)
    mask = widen(mask_ref, joined.shape[1])
    logistic = jax.nn.sigmoid(joined)
    out_ref[...] = (joined * logistic * mask).astype(bf16)
    grad = cotangent_ref[...].astype(f32) * mask * (logistic * (1.0 + joined * (1.0 - logistic)))
    grad_ref[...] = grad
    put_sums(sums_ref, grad, hat)


def sums_of(got_ref, core=None):
    if core is None:
        return functools.reduce(jnp.add, [got_ref[at] for at in range(got_ref.shape[0])])
    return functools.reduce(jnp.add, [got_ref[2 * at + core] for at in range(got_ref.shape[0] // 2)])


def norm_back(grad, hat, moments_ref, norm_ref, beta, gamma, mask):
    inside = grad - (beta + hat * gamma) / moments_ref[2:3]
    return (mask * (norm_ref[0:1] * moments_ref[1:2]) * inside).astype(bf16)


def back_dense_kernel(both, core_ref, got_ref, grad_ref, raw_ref, moments_ref, norm_ref, mask_ref, weight_ref, out_ref,
                    norm_grad_ref, send_ref):
    sums = sums_of(got_ref, core_ref[0] if both else None)
    beta, gamma = sums[0:1], sums[1:2]
    norm_grad_ref[...] = jnp.concatenate([gamma, beta], axis=0)
    grad = norm_back(grad_ref[...], normed(raw_ref, moments_ref), moments_ref, norm_ref, beta, gamma,
                     widen(mask_ref, raw_ref.shape[1]))
    out_ref[...] = grad
    own, other = halves(weight_ref, core_ref[0], weight_ref.shape[0] // 2)
    send_ref[...] = dot_nt(grad, weight_ref[other, :]).astype(bf16)


def own_dense_kernel(core_ref, up_ref, got_ref, weight_ref, raw_ref, moments_ref, norm_ref, mask_ref, out_ref, sums_ref):
    own, other = halves(weight_ref, core_ref[0], weight_ref.shape[0] // 2)
    back = dot_nt(up_ref[...], weight_ref[own, :]) + got_ref[...].astype(f32)
    hat = normed(raw_ref, moments_ref)
    grad = back * widen(mask_ref, raw_ref.shape[1]) * silu_slope(scaled(norm_ref, hat))
    out_ref[...] = grad
    put_sums(sums_ref, grad, hat)


def moved_grads(grad, cols, rows, width, grid):
    wide = grad.astype(f32)
    out = {}
    for col in cols:
        moved = grad if col == 0 else shift_cols(wide, col, width).astype(bf16)
        for row in rows:
            out[row, col] = shift_rows(moved, row, width, grid)
    return out


def back_five_kernel(grid, width, core_ref, got_ref, grad_ref, raw_ref, moments_ref, norm_ref, mask_ref, weight_ref,
                     out_ref, norm_grad_ref, send_ref):
    sums = sums_of(got_ref, core_ref[0])
    beta, gamma = sums[0:1], sums[1:2]
    norm_grad_ref[...] = jnp.concatenate([gamma, beta], axis=0)
    grad = norm_back(grad_ref[...], normed(raw_ref, moments_ref), moments_ref, norm_ref, beta, gamma,
                     widen(mask_ref, raw_ref.shape[1]))
    out_ref[...] = grad
    own, other = halves(weight_ref, core_ref[0], weight_ref.shape[2] // 2)
    moved = moved_grads(grad, (-1, 0, 1), (-1, 0, 1), width, grid)
    back = functools.reduce(
        jnp.add, [dot_nt(moved[1 - r, 1 - s], weight_ref[r, s, other, :]) for r in range(3) for s in range(3)])
    send_ref[...] = back.astype(bf16)


def own_five_kernel(grid, width, core_ref, up_ref, got_ref, weight_ref, raw_ref, moments_ref, norm_ref, mask_ref, out_ref,
                    sums_ref):
    own, other = halves(weight_ref, core_ref[0], weight_ref.shape[2] // 2)
    moved = moved_grads(up_ref[...], (-1, 0, 1), (-1, 0, 1), width, grid)
    back = functools.reduce(
        jnp.add, [dot_nt(moved[1 - r, 1 - s], weight_ref[r, s, own, :]) for r in range(3) for s in range(3)])
    hat = normed(raw_ref, moments_ref)
    grad = (back + got_ref[...].astype(f32)) * widen(mask_ref, raw_ref.shape[1]) * silu_slope(scaled(norm_ref, hat))
    out_ref[...] = grad
    put_sums(sums_ref, grad, hat)


def own_four_kernel(core_ref, up_ref, got_ref, weight_ref, top_ref, three_ref, moments_three_ref, norm_three_ref, skip_ref,
                    moments_skip_ref, norm_skip_ref, mask_ref, out_ref, sums_ref):
    own, other = halves(weight_ref, core_ref[0], weight_ref.shape[0] // 2)
    back = dot_nt(up_ref[...], weight_ref[own, :]) + got_ref[...].astype(f32) + top_ref[...]
    hat_three = normed(three_ref, moments_three_ref)
    hat_skip = normed(skip_ref, moments_skip_ref)
    joined = scaled(norm_three_ref, hat_three) + scaled(norm_skip_ref, hat_skip)
    grad = back * widen(mask_ref, joined.shape[1]) * silu_slope(joined)
    out_ref[...] = grad
    put_sums(sums_ref, grad, hat_three, hat_skip)


def back_join_kernel(core_ref, got_ref, grad_ref, three_ref, moments_three_ref, norm_three_ref, skip_ref, moments_skip_ref,
                     norm_skip_ref, mask_ref, weight_ref, out_three_ref, out_skip_ref, norm_three_grad_ref,
                     norm_skip_grad_ref, send_ref):
    sums = sums_of(got_ref)
    beta, gamma_three, gamma_skip = sums[0:1], sums[1:2], sums[2:3]
    norm_three_grad_ref[...] = jnp.concatenate([gamma_three, beta], axis=0)
    norm_skip_grad_ref[...] = jnp.concatenate([gamma_skip, beta], axis=0)
    mask = widen(mask_ref, three_ref.shape[1])
    grad = norm_back(grad_ref[...], normed(three_ref, moments_three_ref), moments_three_ref, norm_three_ref, beta,
                     gamma_three, mask)
    out_three_ref[...] = grad
    own, other = halves(weight_ref, core_ref[0], weight_ref.shape[0] // 2)
    send_ref[...] = dot_nt(grad, weight_ref[other, :]).astype(bf16)
    out_skip_ref[...] = norm_back(grad_ref[...], normed(skip_ref, moments_skip_ref), moments_skip_ref, norm_skip_ref, beta,
                                  gamma_skip, mask)


def planes_back(moved, weight_ref, at):
    def term(r, s, row, col):
        return dot_nt(moved[row, col], weight_ref[r, s, at, :])

    return [
        term(1, 1, 0, 0),
        term(1, 2, 0, 0) + term(1, 0, 0, 1),
        term(2, 1, 0, 0) + term(0, 1, 1, 0),
        term(2, 2, 0, 0) + term(2, 0, 0, 1) + term(0, 2, 1, 0) + term(0, 0, 1, 1),
    ]


def back_two_kernel(grid, width, core_ref, got_ref, grad_ref, raw_ref, moments_ref, norm_ref, mask_ref, weight_ref, out_ref,
                    norm_grad_ref, send_ref):
    sums = sums_of(got_ref, core_ref[0])
    beta, gamma = sums[0:1], sums[1:2]
    norm_grad_ref[...] = jnp.concatenate([gamma, beta], axis=0)
    grad = norm_back(grad_ref[...], normed(raw_ref, moments_ref), moments_ref, norm_ref, beta, gamma,
                     widen(mask_ref, raw_ref.shape[1]))
    out_ref[...] = grad
    own, other = halves(weight_ref, core_ref[0], weight_ref.shape[2] // 2)
    rows = grad.shape[0]
    for plane, back in enumerate(planes_back(moved_grads(grad, (0, 1), (0, 1), width, grid), weight_ref, other)):
        send_ref[plane * rows : (plane + 1) * rows, :] = back.astype(bf16)


def own_two_kernel(grid, width, core_ref, up_ref, got_ref, weight_ref, raw_ref, moments_ref, norm_ref, mask_ref, out_ref,
                   sums_ref):
    own, other = halves(weight_ref, core_ref[0], weight_ref.shape[2] // 2)
    rows = up_ref.shape[0]
    mask = widen(mask_ref, raw_ref.shape[1])
    beta = jnp.zeros((1, raw_ref.shape[1]), f32)
    gamma = beta
    for plane, back in enumerate(planes_back(moved_grads(up_ref[...], (0, 1), (0, 1), width, grid), weight_ref, own)):
        at = slice(plane * rows, (plane + 1) * rows)
        hat = (raw_ref[at, :] - moments_ref[0:1]) * moments_ref[1:2]
        grad = (back + got_ref[at, :].astype(f32)) * mask * silu_slope(scaled(norm_ref, hat))
        out_ref[at, :] = grad
        beta = beta + jnp.sum(grad, axis=0, keepdims=True)
        gamma = gamma + jnp.sum(grad * hat, axis=0, keepdims=True)
    put_rows(sums_ref, [beta, gamma])


def back_one_kernel(core_ref, got_ref, grad_ref, raw_ref, moments_ref, norm_ref, mask_ref, weight_ref, up_skip_ref,
                    shortcut_ref, out_ref, norm_grad_ref, send_ref):
    sums = sums_of(got_ref, core_ref[0])
    beta, gamma = sums[0:1], sums[1:2]
    norm_grad_ref[...] = jnp.concatenate([gamma, beta], axis=0)
    mask = jnp.concatenate([widen(mask_ref, raw_ref.shape[1])] * 4, axis=0)
    grad = norm_back(grad_ref[...], normed(raw_ref, moments_ref), moments_ref, norm_ref, beta, gamma, mask)
    out_ref[...] = grad
    own, other = halves(weight_ref, core_ref[0], weight_ref.shape[0] // 2)
    rows = mask_ref.shape[0]
    skip = dot_nt(up_skip_ref[...], shortcut_ref[other, :])
    send_ref[:rows, :] = (dot_nt(grad[:rows], weight_ref[other, :]) + skip).astype(bf16)
    send_ref[rows:, :] = dot_nt(grad[rows:], weight_ref[other, :]).astype(bf16)


def own_x_kernel(grid, width, core_ref, up_ref, got_ref, weight_ref, up_skip_ref, shortcut_ref, mask_ref, out_ref):
    own, other = halves(weight_ref, core_ref[0], weight_ref.shape[0] // 2)
    rows = mask_ref.shape[0]
    imgs = out_ref.shape[0]
    back = dot_nt(up_ref[...], weight_ref[own, :]) + got_ref[...].astype(f32)
    skip = dot_nt(up_skip_ref[...], shortcut_ref[own, :])
    mask = widen(mask_ref, back.shape[1])
    planes = [back[:rows] + skip] + [back[at * rows : (at + 1) * rows] for at in range(1, 4)]
    planes = [(plane * mask).astype(bf16) for plane in planes]
    size = 4 * grid
    target = lax.broadcasted_iota(jnp.int32, (size, size), 1)
    source = lax.broadcasted_iota(jnp.int32, (size, size), 0)
    place = jnp.where(source == pixel_of(target, grid, width), 1.0, 0.0).astype(bf16)
    for n in range(imgs):
        ordered = jnp.concatenate([plane[n * grid : (n + 1) * grid] for plane in planes], axis=0)
        out_ref[n] = dot(place, ordered).astype(bf16)


def turn(value):
    return value.astype(f32).T.astype(bf16)


def put_parts(outs, start, total_ref, far_at):
    size = total_ref.shape[0] // len(outs)
    for b, out in enumerate(outs):
        first = pl.multiple_of((far_at ^ b) * size, size)
        out[start : start + size, :] = total_ref[pl.ds(first, size), :].astype(bf16)
    return start + size


def put_tap_parts(outs, start, total_ref, far_at):
    size = total_ref.shape[1] // len(outs)
    for b, out in enumerate(outs):
        first = pl.multiple_of((far_at ^ b) * size, size)
        for tap in range(9):
            at = start + tap * size
            out[at : at + size, :] = total_ref[tap, pl.ds(first, size), :].astype(bf16)
    return start + 9 * size


def add_into(ref, at, part, block):
    ref[at] = part if block == 0 else ref[at] + part


def weight_top_kernel(grid, width, near, far, core_ref, near_at_ref, own_five_ref, other_five_ref, *refs):
    up_six, act_four, up_five = refs[:near], refs[near : 2 * near], refs[2 * near : 3 * near]
    out_ref, dense_ref, taps_ref = refs[3 * near :]
    depth = own_five_ref.shape[2]
    for half, act_ref in zip(halves(None, core_ref[0], depth), (own_five_ref, other_five_ref)):
        for block in range(near):
            add_into(dense_ref, half, dot(turn(act_ref[block]), up_six[block][...]), block)
    for block in range(near):
        turned = turn(act_four[block][...])
        moved = moved_grads(up_five[block][...], (-1, 0, 1), (-1, 0, 1), width, grid)
        for r in range(3):
            for s in range(3):
                add_into(taps_ref, 3 * r + s, dot(turned, moved[1 - r, 1 - s]), block)
    start = 0
    for owner in range(far):
        size = dense_ref.shape[0] // far
        out_ref[start : start + size, :] = dense_ref[owner * size : (owner + 1) * size, :].astype(bf16)
        start += size
        size = taps_ref.shape[1] // far
        for tap in range(9):
            out_ref[start : start + size, :] = taps_ref[tap, owner * size : (owner + 1) * size, :].astype(bf16)
            start += size


def weight_four_kernel(near, core_ref, near_at_ref, own_ref, other_ref, up_ref, *refs):
    outs, sum_ref = refs[:near], refs[near]
    own, other = halves(None, core_ref[0], own_ref.shape[1])
    sum_ref[own, :] = dot(turn(own_ref[...]), up_ref[...])
    sum_ref[other, :] = dot(turn(other_ref[...]), up_ref[...])
    put_parts(outs, 0, sum_ref, near_at_ref[0])


def weight_bottom_kernel(near, far, split, core_ref, near_at_ref, far_at_ref, own_ref, other_ref, *refs):
    parts, up_join = refs[:near], refs[near : 2 * near]
    outs, (reduce_ref, expand_ref, shortcut_ref) = refs[2 * near : 2 * near + far], refs[2 * near + far :]
    rows, lanes = up_join[0].shape[0], up_join[0].shape[1] // 2
    depth = own_ref.shape[1] - split
    reduce_ref[...] = functools.reduce(jnp.add, [part[...].astype(f32) for part in parts])
    for half, act_ref in zip(halves(None, core_ref[0], split), (own_ref, other_ref)):
        for block in range(near):
            first = pl.multiple_of((near_at_ref[0] ^ block) * rows, rows)
            turned = turn(act_ref[pl.ds(first, rows), :])
            add_into(shortcut_ref, half, dot(turned[:split], up_join[block][:, lanes:]), block)
    for half, act_ref in zip(halves(None, core_ref[0], depth), (own_ref, other_ref)):
        for block in range(near):
            first = pl.multiple_of((near_at_ref[0] ^ block) * rows, rows)
            turned = turn(act_ref[pl.ds(first, rows), split:])
            add_into(expand_ref, half, dot(turned, up_join[block][:, :lanes]), block)
    start = put_parts(outs, 0, reduce_ref, far_at_ref[0])
    start = put_parts(outs, start, expand_ref, far_at_ref[0])
    put_parts(outs, start, shortcut_ref, far_at_ref[0])


def weight_two_kernel(grid, width, near, far, far_at_ref, *refs):
    acts, ups, outs, taps_ref = refs[:near], refs[near : 2 * near], refs[2 * near : 2 * near + far], refs[2 * near + far]
    rows = ups[0].shape[0]
    for block in range(near):
        moved = moved_grads(ups[block][...], (0, 1), (0, 1), width, grid)
        for plane in range(4):
            turned = turn(acts[block][plane * rows : (plane + 1) * rows, :])
            for r in ((1,) if plane < 2 else (0, 2)):
                for s in ((1,) if plane % 2 == 0 else (0, 2)):
                    add_into(taps_ref, 3 * r + s, dot(turned, moved[int(r == 0), int(s == 0)]), block)
    put_tap_parts(outs, 0, taps_ref, far_at_ref[0])


def weight_one_kernel(near, core_ref, near_at_ref, own_ref, other_ref, up_ref, *refs):
    outs, sum_ref = refs[:near], refs[near]
    own, other = halves(None, core_ref[0], own_ref.shape[1])
    sum_ref[own, :] = dot(turn(own_ref[...]), up_ref[...])
    sum_ref[other, :] = dot(turn(other_ref[...]), up_ref[...])
    put_parts(outs, 0, sum_ref, near_at_ref[0])


def solution(mesh):
    count = mesh.shape["dp"]
    near = 4
    far = count // near
    def to_near(pieces):
        return [pieces[0]] + [send(pieces[b], count, b) for b in range(1, near)]

    def to_far(pieces):
        return [pieces[0]] + [send(pieces[b].astype(bf16), count, b * near) for b in range(1, far)]

    def tell_far(value):
        return [value] + [send(value, count, b * near) for b in range(1, far)]

    far_groups = [[at * near + b for at in range(far)] for b in range(near)]
    near_groups = [[at * near + b for b in range(near)] for at in range(far)]

    def gather_near(value):
        return lax.all_gather(value, "dp", axis=0, tiled=True, axis_index_groups=near_groups)

    def tell_near_first(value):
        rows = value.shape[0] // 2
        first, second = value[:rows], value[rows:]
        return [first, send(first, count, 1), second, send(second, count, 2)]

    def tell_near_then(halves_of):
        first = jnp.concatenate(halves_of[:2])
        second = jnp.concatenate(halves_of[2:])
        return [first, send(first, count, 2), second, send(second, count, 1)]

    def told_chunks(rows):
        half = far // 2
        out = []
        for which, members in enumerate([(0, 1), (2, 3), (0, 2), (1, 3)]):
            for at, member in enumerate(members):
                for b in range(half):
                    out.append((which, (at * half + b) * (rows // far), member, True, (which // 2) * half + b))
        return out

    def total(pieces):
        return functools.reduce(jnp.add, [piece.astype(f32) for piece in pieces])

    def local(images, extents, cotangent, reduce1, spatial1, expand1, shortcut, reduce2, spatial2, expand2,
              norm_one, norm_two, norm_three, norm_skip, norm_four, norm_five, norm_six):
        core = lax.axis_index("chan")
        place = lax.axis_index("dp")
        near_at, far_at = place % near, place // near
        near_order = [near_at ^ b for b in range(near)]
        far_order = [far_at ^ b for b in range(far)]
        imgs, height, width = cotangent.shape[:3]
        grid = height * width
        outer = imgs * grid
        cid = images.shape[3]
        mid = reduce1.shape[1]
        wide = cotangent.shape[3]
        share = 2 * mid // near
        near_place = near_at.reshape(1).astype(jnp.int32)
        far_place = far_at.reshape(1).astype(jnp.int32)
        core_at = core.reshape(1).astype(jnp.int32)

        cell = lax.broadcasted_iota(jnp.int32, (imgs, grid), 1)
        valid = (cell // width < extents[:, 0:1]) & (cell % width < extents[:, 1:2])
        mask = jnp.broadcast_to(valid.astype(f32).reshape(outer, 1), (outer, 128))
        cells = jnp.sum(extents[:, 0] * extents[:, 1]).astype(f32).reshape(1)

        def gridded(body):
            return functools.partial(body, grid, width)

        def spread(local_sums, both):
            return lax.all_to_all(local_sums, ("dp", "chan") if both else "dp", 0, 0, tiled=True)

        first_sums = ((2 * count, 4, mid), f32)
        narrow_sums = ((2 * count, 2, mid), f32)
        own_sums = ((2 * count, 2, mid), f32)
        wide_sums = ((count, 2, wide), f32)
        join_sums = ((count, 4, wide), f32)
        all_cells_out = ((count, 128), f32)
        narrow_moments = ((8, mid), f32)
        wide_moments = ((8, wide), f32)
        inner = 4 * outer

        norms = jnp.concatenate([norm_one, norm_two, norm_four, norm_five])
        norms = in_order(core, norms, swap(norms))
        both_one, both_two, both_four, both_five = norms[0:2], norms[2:4], norms[4:6], norms[6:8]

        own_x, = run_kernel(gridded(sort_kernel), [((inner, cid), bf16)], [],
                            [images.reshape(imgs, 4 * grid, cid), mask], flops=2 * imgs * 16 * grid * grid * cid, held=(1,))
        other_x = swap(own_x)
        conv_one, sums = run_kernel(conv_one_kernel, [((inner, mid), f32), first_sums], [core_at, cells],
                                    [own_x, other_x, reduce1, mask], flops=4 * inner * cid * mid, held=(2, 3,))
        got = spread(sums, True)
        other_one = swap(conv_one)
        conv_skip, skip_stats = run_kernel(conv_skip_kernel, [((outer, wide), f32), ((2, wide), f32)], [core_at, cells],
                                           [own_x, other_x, shortcut, mask], flops=4 * outer * cid * wide, held=(2, 3,))
        act_one, conv_two, sums, moments_one, all_cells = run_kernel(
            gridded(conv_two_kernel),
            [((inner, 2 * mid), bf16), ((outer, mid), f32), narrow_sums, narrow_moments, all_cells_out], [core_at, cells],
            [got, conv_one, other_one, both_one, mask, spatial1], flops=36 * outer * mid * mid,
            scratch=[pltpu.VMEM((inner, 2 * mid), f32)], held=(0, 4, 5,))
        act_one, sums = tie(act_one, sums)
        got = spread(sums, True)
        other_two = swap(conv_two)
        near_one = [slot(act_one, at, share, 1) for at in near_order]
        near_one[1] = send(near_one[1], count, 1)
        near_one[1], got = tie(near_one[1], got)
        act_two, conv_three, sums, moments_two = run_kernel(
            expand_kernel, [((outer, 2 * mid), bf16), ((outer, wide), f32), join_sums, narrow_moments], [core_at, cells],
            [got, all_cells, conv_two, other_two, both_two, mask, expand1, skip_stats], flops=4 * outer * mid * wide,
            scratch=[pltpu.VMEM((outer, 2 * mid), f32)], held=(0, 1, 5, 6,))
        near_one[2], sums = tie(near_one[2], sums)
        got = spread(sums, False)
        near_one[2] = send(near_one[2], count, 2)
        near_one[2], got = tie(near_one[2], got)
        block_one, moments_three, moments_skip = run_kernel(
            join_kernel, [((outer, wide), bf16), wide_moments, wide_moments], [],
            [got, all_cells, conv_three, conv_skip, norm_three, norm_skip, mask], flops=20 * outer * wide, held=(0, 1, 6,))
        other_block = swap(block_one)
        conv_four, sums = run_kernel(conv_four_kernel, [((outer, mid), f32), narrow_sums], [core_at, cells],
                                     [block_one, other_block, reduce2, mask], flops=4 * outer * wide * mid, held=(2, 3,))
        near_one[3], sums = tie(near_one[3], sums)
        got = spread(sums, True)
        near_one[3] = send(near_one[3], count, 3)
        near_one[3], got = tie(near_one[3], got)
        other_four = swap(conv_four)
        act_four, conv_five, sums, moments_four = run_kernel(
            gridded(conv_five_kernel),
            [((outer, 2 * mid), bf16), ((outer, mid), f32), narrow_sums, narrow_moments], [core_at, cells],
            [got, all_cells, conv_four, other_four, both_four, mask, spatial2], flops=36 * outer * mid * mid,
            scratch=[pltpu.VMEM((outer, 2 * mid), f32)], held=(0, 1, 5, 6,))
        (own_x, act_two), sums = tie((own_x, act_two), sums)
        got = spread(sums, True)
        own_two = slot(act_two, core, mid, 1)
        skip_two, got = tie(jnp.concatenate([own_x[:outer], own_two], axis=1), got)
        near_skip = gather_near(skip_two)
        other_five = swap(conv_five)
        act_five, conv_six, sums, moments_five = run_kernel(
            expand_kernel, [((outer, 2 * mid), bf16), ((outer, wide), f32), wide_sums, narrow_moments], [core_at, cells],
            [got, all_cells, conv_five, other_five, both_five, mask, expand2], flops=4 * outer * mid * wide,
            scratch=[pltpu.VMEM((outer, 2 * mid), f32)], held=(0, 1, 5, 6,))
        act_four, sums = tie(act_four, sums)
        got = spread(sums, False)
        near_four = to_near([slot(act_four, at, share, 1) for at in near_order])
        near_four, got = tie(near_four, got)
        block_two, grad_join2, sums, moments_six = run_kernel(
            top_kernel, [((outer, wide), bf16), ((outer, wide), f32), wide_sums, wide_moments], [],
            [got, all_cells, conv_six, block_one, cotangent.reshape(outer, wide), norm_six, mask], flops=30 * outer * wide, held=(0, 1, 6,))
        own_five, sums = tie(slot(act_five, core, mid, 1), sums)
        got = spread(sums, False)
        near_five = to_near([own_five] * near)
        near_five, got = tie(near_five, got)

        norm_out = ((2, mid), f32)
        wide_norm_out = ((2, wide), f32)
        grad_six, norm_six_grad, part = run_kernel(
            functools.partial(back_dense_kernel, False), [((outer, wide), bf16), wide_norm_out, ((outer, mid), bf16)], [core_at],
            [got, grad_join2, conv_six, moments_six, norm_six, mask, expand2], flops=2 * outer * wide * mid, held=(0, 5, 6,))
        part = swap(part)
        grad_pre, sums = run_kernel(
            own_dense_kernel, [((outer, mid), f32), own_sums], [core_at],
            [grad_six, part, expand2, conv_five, moments_five, norm_five, mask], flops=2 * outer * wide * mid, held=(1, 2, 6,))
        grad_six, sums = tie(grad_six, sums)
        near_five, sums = tie(near_five, sums)
        got = spread(sums, True)
        up_six = to_near([slot(grad_six, at, mid, 1) for at in near_order])
        near_five = jnp.stack(near_five)
        other_near_five = swap(near_five)
        (up_six, near_five, other_near_five), got = tie((up_six, near_five, other_near_five), got)

        grad_five, norm_five_grad, part = run_kernel(
            gridded(back_five_kernel), [((outer, mid), bf16), norm_out, ((outer, mid), bf16)], [core_at],
            [got, grad_pre, conv_five, moments_five, norm_five, mask, spatial2], flops=18 * outer * mid * mid, held=(0, 5, 6,))
        part = swap(part)
        up_five = to_near([grad_five] * near)
        grad_pre, sums = run_kernel(
            gridded(own_five_kernel), [((outer, mid), f32), own_sums], [core_at],
            [grad_five, part, spatial2, conv_four, moments_four, norm_four, mask], flops=18 * outer * mid * mid, held=(1, 2, 6,))
        up_five, sums = tie(up_five, sums)
        got = spread(sums, True)
        rows_a = 2 * mid + 9 * share
        top_part, = run_kernel(
            functools.partial(weight_top_kernel, grid, width, near, far), [((rows_a, mid), bf16)], [core_at, near_place],
            [near_five, other_near_five, *up_six, *near_four, *up_five],
            scratch=[pltpu.VMEM((2 * mid, mid), f32), pltpu.VMEM((9, share, mid), f32)])
        (top_part, near_skip), got = tie((top_part, near_skip), got)
        top_rows = lax.psum_scatter(top_part, "dp", scatter_dimension=0, tiled=True, axis_index_groups=far_groups)
        other_near_skip = swap(near_skip)

        grad_four, norm_four_grad, part = run_kernel(
            functools.partial(back_dense_kernel, True), [((outer, mid), bf16), norm_out, ((outer, wide), bf16)], [core_at],
            [got, grad_pre, conv_four, moments_four, norm_four, mask, reduce2], flops=2 * outer * wide * mid, held=(0, 5, 6,))
        part = swap(part)
        grad_join1, sums = run_kernel(
            own_four_kernel, [((outer, wide), f32), join_sums], [core_at],
            [grad_four, part, reduce2, grad_join2, conv_three, moments_three, norm_three, conv_skip, moments_skip, norm_skip,
             mask], flops=2 * outer * wide * mid, held=(1, 2, 10,))
        (grad_four, other_near_skip), sums = tie((grad_four, other_near_skip), sums)
        got = spread(sums, False)
        reduce2_parts = run_kernel(
            functools.partial(weight_four_kernel, near), [((2 * mid, mid), bf16)] * near, [core_at, near_place],
            [block_one, other_block, grad_four], flops=4 * outer * wide * mid, scratch=[pltpu.VMEM((2 * wide, mid), f32)])
        reduce2_parts = to_near(reduce2_parts)

        top_rows, got = tie(top_rows, got)
        grad_three, grad_skip, norm_three_grad, norm_skip_grad, part = run_kernel(
            back_join_kernel,
            [((outer, wide), bf16), ((outer, wide), bf16), wide_norm_out, wide_norm_out, ((outer, mid), bf16)], [core_at],
            [got, grad_join1, conv_three, moments_three, norm_three, conv_skip, moments_skip, norm_skip, mask, expand1],
            flops=2 * outer * wide * mid, held=(0, 8, 9,))
        reduce2_parts, part = tie(reduce2_parts, swap(part))
        grad_pre, sums = run_kernel(
            own_dense_kernel, [((outer, mid), f32), own_sums], [core_at],
            [grad_three, part, expand1, conv_two, moments_two, norm_two, mask], flops=2 * outer * wide * mid, held=(1, 2, 6,))
        top_rows, sums = tie(top_rows, sums)
        got = spread(sums, True)
        up_join = to_near([
            jnp.concatenate([slot(grad_three, at, mid, 1), slot(grad_skip, at, mid, 1)], axis=1) for at in near_order])

        rows_b = (4 * mid + 2 * cid) // far
        bucket_b = run_kernel(
            functools.partial(weight_bottom_kernel, near, far, cid), [((rows_b, mid), bf16)] * far,
            [core_at, near_place, far_place], [near_skip, other_near_skip, *reduce2_parts, *up_join],
            flops=2 * near * outer * (4 * mid + 2 * cid) * mid,
            scratch=[pltpu.VMEM((2 * mid, mid), f32), pltpu.VMEM((2 * mid, mid), f32), pltpu.VMEM((2 * cid, mid), f32)])
        top_rows = tell_far(top_rows)
        top_rows, got = tie(top_rows, got)
        top_all = gather_near(jnp.concatenate(top_rows))
        bucket_b, got = tie(bucket_b, got)
        bucket_b = to_far(bucket_b)

        grad_two, norm_two_grad, part = run_kernel(
            gridded(back_two_kernel), [((outer, mid), bf16), norm_out, ((inner, mid), bf16)], [core_at],
            [got, grad_pre, conv_two, moments_two, norm_two, mask, spatial1], flops=18 * outer * mid * mid, held=(0, 5, 6,))
        part = swap(part)
        up_two = to_near([grad_two] * near)
        grad_pre, sums = run_kernel(
            gridded(own_two_kernel), [((inner, mid), f32), own_sums], [core_at],
            [grad_two, part, spatial1, conv_one, moments_one, norm_one, mask], flops=18 * outer * mid * mid, held=(1, 2, 6,))
        (up_two, bucket_b[2]), sums = tie((up_two, bucket_b[2]), sums)
        got = spread(sums, True)
        bucket_c = run_kernel(
            functools.partial(weight_two_kernel, grid, width, near, far), [((9 * share // far, mid), bf16)] * far,
            [far_place], [*near_one, *up_two], flops=18 * near * outer * share * mid,
            scratch=[pltpu.VMEM((9, share, mid), f32)])
        (bucket_c, bucket_b), got = tie((bucket_c, bucket_b), got)
        bucket_b = tell_far(total(bucket_b).astype(bf16))

        grad_one, norm_one_grad, part = run_kernel(
            back_one_kernel, [((inner, mid), bf16), norm_out, ((inner, cid), bf16)], [core_at],
            [got, grad_pre, conv_one, moments_one, norm_one, mask, reduce1, grad_skip, shortcut],
            flops=2 * inner * mid * cid, held=(0, 5, 6, 8,))
        part = swap(part)
        reduce1_parts = run_kernel(
            functools.partial(weight_one_kernel, near), [((2 * cid // near, mid), bf16)] * near, [core_at, near_place],
            [own_x, other_x, grad_one], flops=4 * inner * cid * mid, scratch=[pltpu.VMEM((2 * cid, mid), f32)])
        bucket_b[far // 2 + 1 :], reduce1_parts = tie(bucket_b[far // 2 + 1 :], reduce1_parts)
        reduce1_parts = to_near(reduce1_parts)
        reduce1_rows = total(reduce1_parts).astype(bf16)
        bucket_c = [jnp.concatenate([piece, slot(reduce1_rows, at, reduce1_rows.shape[0] // far, 0)])
                    for piece, at in zip(bucket_c, far_order)]
        bucket_b, bucket_c = tie(bucket_b, bucket_c)
        bucket_b = jnp.concatenate(bucket_b)
        rows_b = bucket_b.shape[0]
        bucket_b = tell_near_first(bucket_b)
        bucket_c = to_far(bucket_c)
        bucket_b, bucket_c = tie(bucket_b, bucket_c)
        def lay(arrays, chunks, layouts):
            return laid_out(arrays, chunks, near, far, near_at, far_at, layouts)

        kernel_dims = (3, 3, 2 * mid, mid)
        wide_dims = (2 * mid, 4 * mid)
        chunk = rows_a // far
        top_chunks = [(0, (member * far + b) * chunk, member, False, b) for member in range(near) for b in range(far)]
        expand2_grad, spatial2_grad = lay([top_all], top_chunks, [("columns", wide_dims), ("kernel", kernel_dims)])
        input_grad, = run_kernel(
            gridded(own_x_kernel), [((imgs, 4 * grid, cid), bf16)], [core_at],
            [grad_one, part, reduce1, grad_skip, shortcut, mask], flops=4 * inner * mid * cid, held=(1, 2, 4, 5,))
        bucket_b, sums_c = tie(bucket_b, total(bucket_c).astype(bf16))
        bucket_c = tell_far(sums_c)
        bucket_b = tell_near_then(bucket_b)
        (bucket_b, expand2_grad, spatial2_grad, input_grad), bucket_c = tie(
            (bucket_b, expand2_grad, spatial2_grad, input_grad), bucket_c)
        bucket_c = jnp.concatenate(bucket_c)
        rows_c = bucket_c.shape[0]
        bucket_c = tell_near_first(bucket_c)
        reduce2_grad, expand1_grad, shortcut_grad = lay(
            bucket_b, told_chunks(rows_b),
            [("rows", reduce2.shape), ("columns", wide_dims), ("columns", shortcut.shape)])
        (reduce2_grad, expand1_grad, shortcut_grad), bucket_c = tie((reduce2_grad, expand1_grad, shortcut_grad), bucket_c)
        bucket_c = tell_near_then(bucket_c)
        spatial1_grad, reduce1_grad = lay(
            bucket_c, told_chunks(rows_c), [("kernel", kernel_dims), ("rows", reduce1.shape)])
        grads = (reduce1_grad, spatial1_grad, expand1_grad, shortcut_grad, reduce2_grad, spatial2_grad, expand2_grad)
        return (block_one.reshape(cotangent.shape), block_two.reshape(cotangent.shape), input_grad.reshape(images.shape),
                *grads, norm_one_grad, norm_two_grad, norm_three_grad, norm_skip_grad, norm_four_grad, norm_five_grad,
                norm_six_grad)

    pixels = P("dp", None, None, "chan")
    weights = (P(None, "chan"), P(None, None, None, "chan")) + (P(None, "chan"),) * 3 + (P(None, None, None, "chan"), P(None, "chan"))
    norms = (P(None, "chan"),) * 7
    return jax.shard_map(
        local, mesh=mesh,
        in_specs=(pixels, P("dp", None), pixels) + weights + norms,
        out_specs=(pixels, pixels, pixels) + weights + norms,
        check_vma=False)
```

```python
import functools
import math

import jax
import jax.numpy as jnp
from jax import lax
from jax.experimental import pallas as pl
from jax.experimental.pallas import tpu as pltpu
from jax.sharding import PartitionSpec as P

epsilon = 1e-05
f32 = jnp.float32
bf16 = jnp.bfloat16
SWAP = [(0, 1), (1, 0)]


def swap(value):
    return lax.ppermute(value, "chan", SWAP)


def in_order(core, own, other, axis=-1):
    return jnp.where(
        core == 0,
        jnp.concatenate([own, other], axis),
        jnp.concatenate([other, own], axis),
    )


def tie(early, late):
    return lax.optimization_barrier((early, late))


def send(value, count, bits):
    return lax.ppermute(value, "dp", [(at, at ^ bits) for at in range(count)])


def slot(value, index, size, axis):
    return lax.dynamic_slice_in_dim(value, index * size, size, axis)


def lay_kernel(near, far, layouts, chunks, at_ref, *refs):
    ins, outs = refs[: len(refs) - len(layouts)], refs[len(refs) - len(layouts) :]
    near_at, far_at = at_ref[0], at_ref[1]
    for which, start, member, relative, b in chunks:
        owner = far_at ^ b
        if relative:
            member = near_at ^ member
        for (kind, dims), out in zip(layouts, outs):
            if kind == "kernel":
                size = dims[2] // near // far
                for tap in range(9):
                    first = pl.multiple_of(member * (size * far) + owner * size, size)
                    out[tap // 3, tap % 3, pl.ds(first, size), :] = ins[which][start : start + size, :].astype(f32)
                    start += size
            elif kind == "rows":
                size = dims[0] // near // far
                first = pl.multiple_of(member * (size * far) + owner * size, size)
                out[pl.ds(first, size), :] = ins[which][start : start + size, :].astype(f32)
                start += size
            else:
                size, lanes = dims[0] // far, dims[1] // near
                first = pl.multiple_of(owner * size, size)
                lane = pl.multiple_of(member * lanes, lanes)
                out[pl.ds(first, size), pl.ds(lane, lanes)] = ins[which][start : start + size, :].astype(f32)
                start += size


def laid_out(arrays, chunks, near, far, near_at, far_at, layouts):
    return pl.pallas_call(
        functools.partial(lay_kernel, near, far, layouts, chunks),
        out_shape=[jax.ShapeDtypeStruct(dims, f32) for _, dims in layouts],
        in_specs=[pl.BlockSpec(memory_space=pltpu.SMEM)] + [pl.BlockSpec(memory_space=pltpu.VMEM)] * len(arrays),
        out_specs=[pl.BlockSpec(memory_space=pltpu.VMEM)] * len(layouts),
        compiler_params=pltpu.CompilerParams(vmem_limit_bytes=40 * 2**20),
    )(jnp.stack([near_at, far_at]).astype(jnp.int32), *arrays)


def spec(kind):
    return pl.BlockSpec(memory_space=kind)


def staged(body, scalars, ins, outs, held, *refs):
    head, refs = refs[:scalars], refs[scalars:]
    given, results, refs = refs[:ins], refs[ins : ins + outs], refs[ins + outs :]
    moved = [at for at in range(ins) if at not in held]
    here, made, extra = refs[: len(moved)], refs[len(moved) : len(moved) + outs], refs[len(moved) + outs : -2]
    in_sems, out_sems = refs[-2:]
    arrivals = [pltpu.make_async_copy(given[at], here[k], in_sems.at[k]) for k, at in enumerate(moved)]
    for copy in arrivals:
        copy.start()
    for copy in arrivals:
        copy.wait()
    local = dict(zip(moved, here))
    body(*head, *[local.get(at, given[at]) for at in range(ins)], *made, *extra)
    leaving = [pltpu.make_async_copy(made[at], results[at], out_sems.at[at]) for at in range(outs)]
    for copy in leaving:
        copy.start()
    for copy in leaving:
        copy.wait()


def run_kernel(body, outs, scalars, arrays, flops=0, scratch=(), held=()):
    return pl.pallas_call(
        functools.partial(staged, body, len(scalars), len(arrays), len(outs), held),
        out_shape=[pltpu.HBM(shape, dtype) for shape, dtype in outs],
        in_specs=[spec(pltpu.SMEM)] * len(scalars)
        + [spec(pltpu.VMEM if at in held else pltpu.HBM) for at in range(len(arrays))],
        out_specs=[spec(pltpu.HBM)] * len(outs),
        scratch_shapes=[pltpu.VMEM(x.shape, x.dtype) for at, x in enumerate(arrays) if at not in held]
        + [pltpu.VMEM(shape, dtype) for shape, dtype in outs]
        + list(scratch) + [pltpu.SemaphoreType.DMA((len(arrays),)), pltpu.SemaphoreType.DMA((len(outs),))],
        cost_estimate=pl.CostEstimate(flops=1, bytes_accessed=1, transcendentals=0),
        compiler_params=pltpu.CompilerParams(vmem_limit_bytes=28 * 2**20),
    )(*scalars, *[x if at in held else pltpu.with_memory_space_constraint(x, pltpu.HBM) for at, x in enumerate(arrays)])


def widen(mask_ref, lanes):
    mask = mask_ref[...]
    return mask if lanes == 128 else jnp.concatenate([mask] * (lanes // 128), axis=1)


def dot(left, right):
    return lax.dot_general(left, right, (((1,), (0,)), ((), ())), preferred_element_type=f32)


def dot_nt(left, right):
    return lax.dot_general(left, right, (((1,), (1,)), ((), ())), preferred_element_type=f32)


def halves(ref, core, size):
    own = pl.ds(pl.multiple_of(core * size, size), size)
    other = pl.ds(pl.multiple_of((1 - core) * size, size), size)
    return own, other


def stats(values, mask, cells):
    total = jnp.sum(values * mask, axis=0, keepdims=True)
    centred = (values - total / cells) * mask
    return [total, jnp.sum(centred * centred, axis=0, keepdims=True)]


def put_rows(out_ref, rows):
    tile = jnp.concatenate(rows, axis=0)
    for at in range(out_ref.shape[0]):
        out_ref[at] = tile


def moments(tiles, cells_ref, scale=1.0, first=0):
    lanes = tiles[0].shape[1]
    cells = jnp.concatenate([cells_ref[...]] * (lanes // 128), axis=1) * scale
    pixels = jnp.sum(cells, axis=0, keepdims=True)
    totals = [tile[first : first + 1] for tile in tiles]
    mean = functools.reduce(jnp.add, totals) / pixels
    spread = functools.reduce(jnp.add, [tile[first + 1 : first + 2] for tile in tiles])
    offsets = jnp.concatenate(totals, axis=0) / cells - mean
    spread = spread + jnp.sum(cells * offsets * offsets, axis=0, keepdims=True)
    return mean, lax.rsqrt(spread / pixels + epsilon), pixels


def put_moments(out_ref, mean, inverse, pixels):
    lanes = mean.shape[1]
    out_ref[...] = jnp.concatenate([mean, inverse, pixels, jnp.zeros((5, lanes), f32)], axis=0)


def silu_slope(values):
    logistic = jax.nn.sigmoid(values)
    return logistic * (1.0 + values * (1.0 - logistic))


def shift_cols(values, by, width):
    rows = values.shape[0]
    column = lax.broadcasted_iota(jnp.int32, values.shape, 0) & (width - 1)
    moved = pltpu.roll(values, (-by) % rows, 0)
    return jnp.where(column == (0 if by < 0 else width - 1), 0.0, moved)


def shift_rows(values, by, width, grid):
    if by == 0:
        return values
    zeros = jnp.zeros((width, values.shape[1]), values.dtype)
    out = []
    for start in range(0, values.shape[0], grid):
        if by < 0:
            out += [zeros, values[start : start + grid - width]]
        else:
            out += [values[start + width : start + grid], zeros]
    return jnp.concatenate(out, axis=0)


def pixel_of(index, grid, width):
    plane = jnp.zeros_like(index)
    for at in range(1, 4):
        plane = plane + (index >= at * grid).astype(jnp.int32)
    inside = index - plane * grid
    line = inside >> (width.bit_length() - 1)
    column = inside & (width - 1)
    return (2 * line + (plane >> 1)) * (2 * width) + 2 * column + (plane & 1)


def sort_kernel(grid, width, images_ref, mask_ref, out_ref):
    size = 4 * grid
    target = lax.broadcasted_iota(jnp.int32, (size, size), 0)
    source = lax.broadcasted_iota(jnp.int32, (size, size), 1)
    pick = jnp.where(source == pixel_of(target, grid, width), 1.0, 0.0).astype(bf16)
    imgs = images_ref.shape[0]
    lanes = images_ref.shape[2]
    mask = widen(mask_ref, lanes)
    for n in range(imgs):
        ordered = dot(pick, images_ref[n])
        for plane in range(4):
            first = (plane * imgs + n) * grid
            rows = ordered[plane * grid : (plane + 1) * grid] * mask[n * grid : (n + 1) * grid]
            out_ref[first : first + grid, :] = rows.astype(bf16)


def conv_one_kernel(core_ref, cells_ref, own_ref, other_ref, weight_ref, mask_ref, out_ref, stats_ref):
    own, other = halves(weight_ref, core_ref[0], own_ref.shape[1])
    values = dot(own_ref[...], weight_ref[own, :]) + dot(other_ref[...], weight_ref[other, :])
    out_ref[...] = values
    mask = widen(mask_ref, values.shape[1])
    cells = jnp.full((1, values.shape[1]), cells_ref[0])
    put_rows(stats_ref, stats(values, jnp.concatenate([mask] * 4, axis=0), 4.0 * cells_ref[0]) + [cells, cells])


def conv_skip_kernel(core_ref, cells_ref, own_ref, other_ref, weight_ref, mask_ref, out_ref, stats_ref):
    rows = mask_ref.shape[0]
    own, other = halves(weight_ref, core_ref[0], own_ref.shape[1])
    values = dot(own_ref[:rows], weight_ref[own, :]) + dot(other_ref[:rows], weight_ref[other, :])
    out_ref[...] = values
    mask = widen(mask_ref, values.shape[1])
    stats_ref[...] = jnp.concatenate(stats(values, mask, cells_ref[0]), axis=0)


def norm_act(got_ref, all_cells_ref, scale, own_ref, other_ref, norm_ref, mask, core, raw_ref, act_ref, moments_ref):
    lanes = own_ref.shape[1]
    own, other = halves(None, core, lanes)
    raw_ref[:, own] = own_ref[...]
    raw_ref[:, other] = other_ref[...]
    count = got_ref.shape[0] // 2
    for half in range(2):
        mean, inverse, pixels = moments([got_ref[2 * at + half] for at in range(count)], all_cells_ref, scale)

        @pl.when(core == half)
        def _():
            put_moments(moments_ref, mean, inverse, pixels)

        at = slice(half * lanes, (half + 1) * lanes)
        pre = norm_ref[0:1, at] * ((raw_ref[:, at] - mean) * inverse) + norm_ref[1:2, at]
        act_ref[:, at] = (pre * jax.nn.sigmoid(pre) * mask).astype(bf16)


def conv_two_kernel(grid, width, core_ref, cells_ref, got_ref, own_ref, other_ref, norm_ref, mask_ref, weight_ref,
                    act_ref, out_ref, stats_ref, moments_ref, all_cells_ref, raw_ref):
    rows = mask_ref.shape[0]
    lanes = own_ref.shape[1]
    mask = widen(mask_ref, lanes)
    for at in range(got_ref.shape[0] // 2):
        all_cells_ref[at : at + 1, :] = got_ref[2 * at, 2:3, :128]
    norm_act(got_ref, all_cells_ref, 4.0, own_ref, other_ref, norm_ref, jnp.concatenate([mask] * 4, axis=0), core_ref[0],
             raw_ref, act_ref, moments_ref)
    values = jnp.zeros((rows, out_ref.shape[1]), f32)
    for plane in range(4):
        here = act_ref[plane * rows : (plane + 1) * rows, :]
        by_col = {1: here} if plane % 2 == 0 else {2: here, 0: shift_cols(here.astype(f32), -1, width).astype(bf16)}
        for s, moved in by_col.items():
            for r in ((1,) if plane < 2 else (0, 2)):
                values = values + dot(shift_rows(moved, -1 if r == 0 else 0, width, grid), weight_ref[r, s])
    out_ref[...] = values
    put_rows(stats_ref, stats(values, mask, cells_ref[0]))


def conv_five_kernel(grid, width, core_ref, cells_ref, got_ref, all_cells_ref, own_ref, other_ref, norm_ref, mask_ref, weight_ref,
                     act_ref, out_ref, stats_ref, moments_ref, raw_ref):
    rows = mask_ref.shape[0]
    mask = widen(mask_ref, own_ref.shape[1])
    norm_act(got_ref, all_cells_ref, 1.0, own_ref, other_ref, norm_ref, mask, core_ref[0], raw_ref, act_ref, moments_ref)
    values = jnp.zeros((rows, out_ref.shape[1]), f32)
    here = act_ref[...]
    for s in range(3):
        moved = here if s == 1 else shift_cols(here.astype(f32), s - 1, width).astype(bf16)
        for r in range(3):
            values = values + dot(shift_rows(moved, r - 1, width, grid), weight_ref[r, s])
    out_ref[...] = values
    put_rows(stats_ref, stats(values, mask, cells_ref[0]))


def expand_kernel(core_ref, cells_ref, got_ref, all_cells_ref, own_ref, other_ref, norm_ref, mask_ref, weight_ref, *refs):
    more_refs, (act_ref, out_ref, stats_ref, moments_ref, raw_ref) = refs[:-5], refs[-5:]
    norm_act(got_ref, all_cells_ref, 1.0, own_ref, other_ref, norm_ref, widen(mask_ref, own_ref.shape[1]), core_ref[0],
             raw_ref, act_ref, moments_ref)
    values = dot(act_ref[...], weight_ref[...])
    out_ref[...] = values
    more = [more_refs[0][...]] if more_refs else []
    put_rows(stats_ref, stats(values, widen(mask_ref, values.shape[1]), cells_ref[0]) + more)


def normed(raw_ref, moments_ref):
    return (raw_ref[...] - moments_ref[0:1]) * moments_ref[1:2]


def scaled(norm_ref, hat):
    return norm_ref[0:1] * hat + norm_ref[1:2]


def join_kernel(got_ref, all_cells_ref, three_ref, skip_ref, norm_three_ref, norm_skip_ref, mask_ref, out_ref, moments_three_ref,
                moments_skip_ref):
    tiles = [got_ref[at] for at in range(got_ref.shape[0])]
    put_moments(moments_three_ref, *moments(tiles, all_cells_ref))
    put_moments(moments_skip_ref, *moments(tiles, all_cells_ref, first=2))
    joined = scaled(norm_three_ref, normed(three_ref, moments_three_ref)) + scaled(
        norm_skip_ref, normed(skip_ref, moments_skip_ref))
    out_ref[...] = (joined * jax.nn.sigmoid(joined) * widen(mask_ref, joined.shape[1])).astype(bf16)


def conv_four_kernel(core_ref, cells_ref, own_ref, other_ref, weight_ref, mask_ref, out_ref, stats_ref):
    own, other = halves(weight_ref, core_ref[0], own_ref.shape[1])
    values = dot(own_ref[...], weight_ref[own, :]) + dot(other_ref[...], weight_ref[other, :])
    out_ref[...] = values
    put_rows(stats_ref, stats(values, widen(mask_ref, values.shape[1]), cells_ref[0]))


def put_sums(out_ref, grad, *hats):
    rows = [jnp.sum(grad, axis=0, keepdims=True)] + [jnp.sum(grad * hat, axis=0, keepdims=True) for hat in hats]
    put_rows(out_ref, rows + [rows[0]] * (out_ref.shape[1] - len(rows)))


def top_kernel(got_ref, all_cells_ref, six_ref, block_ref, cotangent_ref, norm_ref, mask_ref, out_ref, grad_ref, sums_ref, moments_ref):
    put_moments(moments_ref, *moments([got_ref[at] for at in range(got_ref.shape[0])], all_cells_ref))
    hat = normed(six_ref, moments_ref)
    joined = scaled(norm_ref, hat) + block_ref[...].astype(f32)
    mask = widen(mask_ref, joined.shape[1])
    logistic = jax.nn.sigmoid(joined)
    out_ref[...] = (joined * logistic * mask).astype(bf16)
    grad = cotangent_ref[...].astype(f32) * mask * (logistic * (1.0 + joined * (1.0 - logistic)))
    grad_ref[...] = grad
    put_sums(sums_ref, grad, hat)


def sums_of(got_ref, core=None):
    if core is None:
        return functools.reduce(jnp.add, [got_ref[at] for at in range(got_ref.shape[0])])
    return functools.reduce(jnp.add, [got_ref[2 * at + core] for at in range(got_ref.shape[0] // 2)])


def norm_back(grad, hat, moments_ref, norm_ref, beta, gamma, mask):
    inside = grad - (beta + hat * gamma) / moments_ref[2:3]
    return (mask * (norm_ref[0:1] * moments_ref[1:2]) * inside).astype(bf16)


def back_dense_kernel(both, core_ref, got_ref, grad_ref, raw_ref, moments_ref, norm_ref, mask_ref, weight_ref, out_ref,
                    norm_grad_ref, send_ref):
    sums = sums_of(got_ref, core_ref[0] if both else None)
    beta, gamma = sums[0:1], sums[1:2]
    norm_grad_ref[...] = jnp.concatenate([gamma, beta], axis=0)
    grad = norm_back(grad_ref[...], normed(raw_ref, moments_ref), moments_ref, norm_ref, beta, gamma,
                     widen(mask_ref, raw_ref.shape[1]))
    out_ref[...] = grad
    own, other = halves(weight_ref, core_ref[0], weight_ref.shape[0] // 2)
    send_ref[...] = dot_nt(grad, weight_ref[other, :]).astype(bf16)


def own_dense_kernel(core_ref, up_ref, got_ref, weight_ref, raw_ref, moments_ref, norm_ref, mask_ref, out_ref, sums_ref):
    own, other = halves(weight_ref, core_ref[0], weight_ref.shape[0] // 2)
    back = dot_nt(up_ref[...], weight_ref[own, :]) + got_ref[...].astype(f32)
    hat = normed(raw_ref, moments_ref)
    grad = back * widen(mask_ref, raw_ref.shape[1]) * silu_slope(scaled(norm_ref, hat))
    out_ref[...] = grad
    put_sums(sums_ref, grad, hat)


def moved_grads(grad, cols, rows, width, grid):
    wide = grad.astype(f32)
    out = {}
    for col in cols:
        moved = grad if col == 0 else shift_cols(wide, col, width).astype(bf16)
        for row in rows:
            out[row, col] = shift_rows(moved, row, width, grid)
    return out


def back_five_kernel(grid, width, core_ref, got_ref, grad_ref, raw_ref, moments_ref, norm_ref, mask_ref, weight_ref,
                     out_ref, norm_grad_ref, send_ref):
    sums = sums_of(got_ref, core_ref[0])
    beta, gamma = sums[0:1], sums[1:2]
    norm_grad_ref[...] = jnp.concatenate([gamma, beta], axis=0)
    grad = norm_back(grad_ref[...], normed(raw_ref, moments_ref), moments_ref, norm_ref, beta, gamma,
                     widen(mask_ref, raw_ref.shape[1]))
    out_ref[...] = grad
    own, other = halves(weight_ref, core_ref[0], weight_ref.shape[2] // 2)
    moved = moved_grads(grad, (-1, 0, 1), (-1, 0, 1), width, grid)
    back = functools.reduce(
        jnp.add, [dot_nt(moved[1 - r, 1 - s], weight_ref[r, s, other, :]) for r in range(3) for s in range(3)])
    send_ref[...] = back.astype(bf16)


def own_five_kernel(grid, width, core_ref, up_ref, got_ref, weight_ref, raw_ref, moments_ref, norm_ref, mask_ref, out_ref,
                    sums_ref):
    own, other = halves(weight_ref, core_ref[0], weight_ref.shape[2] // 2)
    moved = moved_grads(up_ref[...], (-1, 0, 1), (-1, 0, 1), width, grid)
    back = functools.reduce(
        jnp.add, [dot_nt(moved[1 - r, 1 - s], weight_ref[r, s, own, :]) for r in range(3) for s in range(3)])
    hat = normed(raw_ref, moments_ref)
    grad = (back + got_ref[...].astype(f32)) * widen(mask_ref, raw_ref.shape[1]) * silu_slope(scaled(norm_ref, hat))
    out_ref[...] = grad
    put_sums(sums_ref, grad, hat)


def own_four_kernel(core_ref, up_ref, got_ref, weight_ref, top_ref, three_ref, moments_three_ref, norm_three_ref, skip_ref,
                    moments_skip_ref, norm_skip_ref, mask_ref, out_ref, sums_ref):
    own, other = halves(weight_ref, core_ref[0], weight_ref.shape[0] // 2)
    back = dot_nt(up_ref[...], weight_ref[own, :]) + got_ref[...].astype(f32) + top_ref[...]
    hat_three = normed(three_ref, moments_three_ref)
    hat_skip = normed(skip_ref, moments_skip_ref)
    joined = scaled(norm_three_ref, hat_three) + scaled(norm_skip_ref, hat_skip)
    grad = back * widen(mask_ref, joined.shape[1]) * silu_slope(joined)
    out_ref[...] = grad
    put_sums(sums_ref, grad, hat_three, hat_skip)


def back_join_kernel(core_ref, got_ref, grad_ref, three_ref, moments_three_ref, norm_three_ref, skip_ref, moments_skip_ref,
                     norm_skip_ref, mask_ref, weight_ref, out_three_ref, out_skip_ref, norm_three_grad_ref,
                     norm_skip_grad_ref, send_ref):
    sums = sums_of(got_ref)
    beta, gamma_three, gamma_skip = sums[0:1], sums[1:2], sums[2:3]
    norm_three_grad_ref[...] = jnp.concatenate([gamma_three, beta], axis=0)
    norm_skip_grad_ref[...] = jnp.concatenate([gamma_skip, beta], axis=0)
    mask = widen(mask_ref, three_ref.shape[1])
    grad = norm_back(grad_ref[...], normed(three_ref, moments_three_ref), moments_three_ref, norm_three_ref, beta,
                     gamma_three, mask)
    out_three_ref[...] = grad
    own, other = halves(weight_ref, core_ref[0], weight_ref.shape[0] // 2)
    send_ref[...] = dot_nt(grad, weight_ref[other, :]).astype(bf16)
    out_skip_ref[...] = norm_back(grad_ref[...], normed(skip_ref, moments_skip_ref), moments_skip_ref, norm_skip_ref, beta,
                                  gamma_skip, mask)


def planes_back(moved, weight_ref, at):
    def term(r, s, row, col):
        return dot_nt(moved[row, col], weight_ref[r, s, at, :])

    return [
        term(1, 1, 0, 0),
        term(1, 2, 0, 0) + term(1, 0, 0, 1),
        term(2, 1, 0, 0) + term(0, 1, 1, 0),
        term(2, 2, 0, 0) + term(2, 0, 0, 1) + term(0, 2, 1, 0) + term(0, 0, 1, 1),
    ]


def back_two_kernel(grid, width, core_ref, got_ref, grad_ref, raw_ref, moments_ref, norm_ref, mask_ref, weight_ref, out_ref,
                    norm_grad_ref, send_ref):
    sums = sums_of(got_ref, core_ref[0])
    beta, gamma = sums[0:1], sums[1:2]
    norm_grad_ref[...] = jnp.concatenate([gamma, beta], axis=0)
    grad = norm_back(grad_ref[...], normed(raw_ref, moments_ref), moments_ref, norm_ref, beta, gamma,
                     widen(mask_ref, raw_ref.shape[1]))
    out_ref[...] = grad
    own, other = halves(weight_ref, core_ref[0], weight_ref.shape[2] // 2)
    rows = grad.shape[0]
    for plane, back in enumerate(planes_back(moved_grads(grad, (0, 1), (0, 1), width, grid), weight_ref, other)):
        send_ref[plane * rows : (plane + 1) * rows, :] = back.astype(bf16)


def own_two_kernel(grid, width, core_ref, up_ref, got_ref, weight_ref, raw_ref, moments_ref, norm_ref, mask_ref, out_ref,
                   sums_ref):
    own, other = halves(weight_ref, core_ref[0], weight_ref.shape[2] // 2)
    rows = up_ref.shape[0]
    mask = widen(mask_ref, raw_ref.shape[1])
    beta = jnp.zeros((1, raw_ref.shape[1]), f32)
    gamma = beta
    for plane, back in enumerate(planes_back(moved_grads(up_ref[...], (0, 1), (0, 1), width, grid), weight_ref, own)):
        at = slice(plane * rows, (plane + 1) * rows)
        hat = (raw_ref[at, :] - moments_ref[0:1]) * moments_ref[1:2]
        grad = (back + got_ref[at, :].astype(f32)) * mask * silu_slope(scaled(norm_ref, hat))
        out_ref[at, :] = grad
        beta = beta + jnp.sum(grad, axis=0, keepdims=True)
        gamma = gamma + jnp.sum(grad * hat, axis=0, keepdims=True)
    put_rows(sums_ref, [beta, gamma])


def back_one_kernel(core_ref, got_ref, grad_ref, raw_ref, moments_ref, norm_ref, mask_ref, weight_ref, up_skip_ref,
                    shortcut_ref, out_ref, norm_grad_ref, send_ref):
    sums = sums_of(got_ref, core_ref[0])
    beta, gamma = sums[0:1], sums[1:2]
    norm_grad_ref[...] = jnp.concatenate([gamma, beta], axis=0)
    mask = jnp.concatenate([widen(mask_ref, raw_ref.shape[1])] * 4, axis=0)
    grad = norm_back(grad_ref[...], normed(raw_ref, moments_ref), moments_ref, norm_ref, beta, gamma, mask)
    out_ref[...] = grad
    own, other = halves(weight_ref, core_ref[0], weight_ref.shape[0] // 2)
    rows = mask_ref.shape[0]
    skip = dot_nt(up_skip_ref[...], shortcut_ref[other, :])
    send_ref[:rows, :] = (dot_nt(grad[:rows], weight_ref[other, :]) + skip).astype(bf16)
    send_ref[rows:, :] = dot_nt(grad[rows:], weight_ref[other, :]).astype(bf16)


def own_x_kernel(grid, width, core_ref, up_ref, got_ref, weight_ref, up_skip_ref, shortcut_ref, mask_ref, out_ref):
    own, other = halves(weight_ref, core_ref[0], weight_ref.shape[0] // 2)
    rows = mask_ref.shape[0]
    imgs = out_ref.shape[0]
    back = dot_nt(up_ref[...], weight_ref[own, :]) + got_ref[...].astype(f32)
    skip = dot_nt(up_skip_ref[...], shortcut_ref[own, :])
    mask = widen(mask_ref, back.shape[1])
    planes = [back[:rows] + skip] + [back[at * rows : (at + 1) * rows] for at in range(1, 4)]
    planes = [(plane * mask).astype(bf16) for plane in planes]
    size = 4 * grid
    target = lax.broadcasted_iota(jnp.int32, (size, size), 1)
    source = lax.broadcasted_iota(jnp.int32, (size, size), 0)
    place = jnp.where(source == pixel_of(target, grid, width), 1.0, 0.0).astype(bf16)
    for n in range(imgs):
        ordered = jnp.concatenate([plane[n * grid : (n + 1) * grid] for plane in planes], axis=0)
        out_ref[n] = dot(place, ordered).astype(bf16)


def turn(value):
    return value.astype(f32).T.astype(bf16)


def put_parts(outs, start, total_ref, far_at):
    size = total_ref.shape[0] // len(outs)
    for b, out in enumerate(outs):
        first = pl.multiple_of((far_at ^ b) * size, size)
        out[start : start + size, :] = total_ref[pl.ds(first, size), :].astype(bf16)
    return start + size


def put_tap_parts(outs, start, total_ref, far_at):
    size = total_ref.shape[1] // len(outs)
    for b, out in enumerate(outs):
        first = pl.multiple_of((far_at ^ b) * size, size)
        for tap in range(9):
            at = start + tap * size
            out[at : at + size, :] = total_ref[tap, pl.ds(first, size), :].astype(bf16)
    return start + 9 * size


def add_into(ref, at, part, block):
    ref[at] = part if block == 0 else ref[at] + part


def weight_top_kernel(grid, width, near, far, core_ref, near_at_ref, own_ref, other_ref, *refs):
    up_six, up_five = refs[:near], refs[near : 2 * near]
    out_ref, dense_ref, taps_ref = refs[2 * near :]
    rows = up_six[0].shape[0]
    depth = own_ref.shape[1] // 2
    near_at = near_at_ref[0]
    share = taps_ref.shape[1]
    lane = pl.multiple_of((near_at & 1) * share, share)
    for half, act_ref in zip(halves(None, core_ref[0], depth), (own_ref, other_ref)):
        for block in range(near):
            first = pl.multiple_of((near_at ^ block) * rows, rows)
            add_into(dense_ref, half, dot(turn(act_ref[pl.ds(first, rows), depth:]), up_six[block][...]), block)
    for block in range(near):
        at = (pl.ds(pl.multiple_of((near_at ^ block) * rows, rows), rows), pl.ds(lane, share))
        act = jnp.where(core_ref[0] == (near_at >> 1), own_ref[at].astype(f32), other_ref[at].astype(f32))
        turned = act.T.astype(bf16)
        moved = moved_grads(up_five[block][...], (-1, 0, 1), (-1, 0, 1), width, grid)
        for r in range(3):
            for s in range(3):
                add_into(taps_ref, 3 * r + s, dot(turned, moved[1 - r, 1 - s]), block)
    start = 0
    for owner in range(far):
        size = dense_ref.shape[0] // far
        out_ref[start : start + size, :] = dense_ref[owner * size : (owner + 1) * size, :].astype(bf16)
        start += size
        size = taps_ref.shape[1] // far
        for tap in range(9):
            out_ref[start : start + size, :] = taps_ref[tap, owner * size : (owner + 1) * size, :].astype(bf16)
            start += size


def weight_four_kernel(near, core_ref, near_at_ref, own_ref, other_ref, up_ref, *refs):
    outs, sum_ref = refs[:near], refs[near]
    own, other = halves(None, core_ref[0], own_ref.shape[1])
    sum_ref[own, :] = dot(turn(own_ref[...]), up_ref[...])
    sum_ref[other, :] = dot(turn(other_ref[...]), up_ref[...])
    put_parts(outs, 0, sum_ref, near_at_ref[0])


def weight_bottom_kernel(near, far, split, core_ref, near_at_ref, far_at_ref, own_ref, other_ref, *refs):
    parts, up_join = refs[:near], refs[near : 2 * near]
    outs, (reduce_ref, expand_ref, shortcut_ref) = refs[2 * near : 2 * near + far], refs[2 * near + far :]
    rows, lanes = up_join[0].shape[0], up_join[0].shape[1] // 2
    depth = own_ref.shape[1] - split
    reduce_ref[...] = functools.reduce(jnp.add, [part[...].astype(f32) for part in parts])
    for half, act_ref in zip(halves(None, core_ref[0], split), (own_ref, other_ref)):
        for block in range(near):
            first = pl.multiple_of((near_at_ref[0] ^ block) * rows, rows)
            turned = turn(act_ref[pl.ds(first, rows), :])
            add_into(shortcut_ref, half, dot(turned[:split], up_join[block][:, lanes:]), block)
    for half, act_ref in zip(halves(None, core_ref[0], depth), (own_ref, other_ref)):
        for block in range(near):
            first = pl.multiple_of((near_at_ref[0] ^ block) * rows, rows)
            turned = turn(act_ref[pl.ds(first, rows), split:])
            add_into(expand_ref, half, dot(turned, up_join[block][:, :lanes]), block)
    start = put_parts(outs, 0, reduce_ref, far_at_ref[0])
    start = put_parts(outs, start, expand_ref, far_at_ref[0])
    put_parts(outs, start, shortcut_ref, far_at_ref[0])


def weight_two_kernel(grid, width, near, far, near_at_ref, far_at_ref, act_ref, *refs):
    ups, outs, taps_ref = refs[:near], refs[near : near + far], refs[near + far]
    rows = ups[0].shape[0]
    for block in range(near):
        moved = moved_grads(ups[block][...], (0, 1), (0, 1), width, grid)
        for plane in range(4):
            first = pl.multiple_of((near_at_ref[0] ^ block) * (4 * rows) + plane * rows, rows)
            turned = turn(act_ref[pl.ds(first, rows), :])
            for r in ((1,) if plane < 2 else (0, 2)):
                for s in ((1,) if plane % 2 == 0 else (0, 2)):
                    add_into(taps_ref, 3 * r + s, dot(turned, moved[int(r == 0), int(s == 0)]), block)
    put_tap_parts(outs, 0, taps_ref, far_at_ref[0])


def weight_one_kernel(near, core_ref, near_at_ref, own_ref, other_ref, up_ref, *refs):
    outs, sum_ref = refs[:near], refs[near]
    own, other = halves(None, core_ref[0], own_ref.shape[1])
    sum_ref[own, :] = dot(turn(own_ref[...]), up_ref[...])
    sum_ref[other, :] = dot(turn(other_ref[...]), up_ref[...])
    put_parts(outs, 0, sum_ref, near_at_ref[0])


def solution(mesh):
    count = mesh.shape["dp"]
    near = 4
    far = count // near
    def to_near(pieces):
        return [pieces[0]] + [send(pieces[b], count, b) for b in range(1, near)]

    def to_far(pieces):
        return [pieces[0]] + [send(pieces[b].astype(bf16), count, b * near) for b in range(1, far)]

    def tell_far(value):
        return [value] + [send(value, count, b * near) for b in range(1, far)]

    far_groups = [[at * near + b for at in range(far)] for b in range(near)]
    near_groups = [[at * near + b for b in range(near)] for at in range(far)]

    def gather_near(value):
        return lax.all_gather(value, "dp", axis=0, tiled=True, axis_index_groups=near_groups)

    def tell_near_first(value):
        rows = value.shape[0] // 2
        first, second = value[:rows], value[rows:]
        return [first, send(first, count, 1), second, send(second, count, 2)]

    def tell_near_then(halves_of):
        first = jnp.concatenate(halves_of[:2])
        second = jnp.concatenate(halves_of[2:])
        return [first, send(first, count, 2), second, send(second, count, 1)]

    def told_chunks(rows):
        half = far // 2
        out = []
        for which, members in enumerate([(0, 1), (2, 3), (0, 2), (1, 3)]):
            for at, member in enumerate(members):
                for b in range(half):
                    out.append((which, (at * half + b) * (rows // far), member, True, (which // 2) * half + b))
        return out

    def total(pieces):
        return functools.reduce(jnp.add, [piece.astype(f32) for piece in pieces])

    def local(images, extents, cotangent, reduce1, spatial1, expand1, shortcut, reduce2, spatial2, expand2,
              norm_one, norm_two, norm_three, norm_skip, norm_four, norm_five, norm_six):
        core = lax.axis_index("chan")
        place = lax.axis_index("dp")
        near_at, far_at = place % near, place // near
        near_order = [near_at ^ b for b in range(near)]
        far_order = [far_at ^ b for b in range(far)]
        imgs, height, width = cotangent.shape[:3]
        grid = height * width
        outer = imgs * grid
        cid = images.shape[3]
        mid = reduce1.shape[1]
        wide = cotangent.shape[3]
        share = 2 * mid // near
        near_place = near_at.reshape(1).astype(jnp.int32)
        far_place = far_at.reshape(1).astype(jnp.int32)
        core_at = core.reshape(1).astype(jnp.int32)

        cell = lax.broadcasted_iota(jnp.int32, (imgs, grid), 1)
        valid = (cell // width < extents[:, 0:1]) & (cell % width < extents[:, 1:2])
        mask = jnp.broadcast_to(valid.astype(f32).reshape(outer, 1), (outer, 128))
        cells = jnp.sum(extents[:, 0] * extents[:, 1]).astype(f32).reshape(1)

        def gridded(body):
            return functools.partial(body, grid, width)

        def spread(local_sums, both):
            return lax.all_to_all(local_sums, ("dp", "chan") if both else "dp", 0, 0, tiled=True)

        first_sums = ((2 * count, 4, mid), f32)
        narrow_sums = ((2 * count, 2, mid), f32)
        own_sums = ((2 * count, 2, mid), f32)
        wide_sums = ((count, 2, wide), f32)
        join_sums = ((count, 4, wide), f32)
        all_cells_out = ((count, 128), f32)
        narrow_moments = ((8, mid), f32)
        wide_moments = ((8, wide), f32)
        inner = 4 * outer

        norms = jnp.concatenate([norm_one, norm_two, norm_four, norm_five])
        norms = in_order(core, norms, swap(norms))
        both_one, both_two, both_four, both_five = norms[0:2], norms[2:4], norms[4:6], norms[6:8]

        own_x, = run_kernel(gridded(sort_kernel), [((inner, cid), bf16)], [],
                            [images.reshape(imgs, 4 * grid, cid), mask], flops=2 * imgs * 16 * grid * grid * cid, held=(1,))
        other_x = swap(own_x)
        conv_one, sums = run_kernel(conv_one_kernel, [((inner, mid), f32), first_sums], [core_at, cells],
                                    [own_x, other_x, reduce1, mask], flops=4 * inner * cid * mid, held=(2, 3,))
        got = spread(sums, True)
        other_one = swap(conv_one)
        conv_skip, skip_stats = run_kernel(conv_skip_kernel, [((outer, wide), f32), ((2, wide), f32)], [core_at, cells],
                                           [own_x, other_x, shortcut, mask], flops=4 * outer * cid * wide, held=(2, 3,))
        act_one, conv_two, sums, moments_one, all_cells = run_kernel(
            gridded(conv_two_kernel),
            [((inner, 2 * mid), bf16), ((outer, mid), f32), narrow_sums, narrow_moments, all_cells_out], [core_at, cells],
            [got, conv_one, other_one, both_one, mask, spatial1], flops=36 * outer * mid * mid,
            scratch=[pltpu.VMEM((inner, 2 * mid), f32)], held=(0, 4, 5,))
        got = spread(sums, True)
        other_two = swap(conv_two)
        near_one = gather_near(slot(act_one, core, mid, 1))
        act_two, conv_three, sums, moments_two = run_kernel(
            expand_kernel, [((outer, 2 * mid), bf16), ((outer, wide), f32), join_sums, narrow_moments], [core_at, cells],
            [got, all_cells, conv_two, other_two, both_two, mask, expand1, skip_stats], flops=4 * outer * mid * wide,
            scratch=[pltpu.VMEM((outer, 2 * mid), f32)], held=(0, 1, 5, 6,))
        (own_x, act_two), sums = tie((own_x, act_two), sums)
        got = spread(sums, False)
        own_two = slot(act_two, core, mid, 1)
        skip_two = jnp.concatenate([own_x[:outer], own_two], axis=1)
        skip_two, got = tie(skip_two, got)
        near_skip = gather_near(skip_two)
        block_one, moments_three, moments_skip = run_kernel(
            join_kernel, [((outer, wide), bf16), wide_moments, wide_moments], [],
            [got, all_cells, conv_three, conv_skip, norm_three, norm_skip, mask], flops=20 * outer * wide, held=(0, 1, 6,))
        other_block = swap(block_one)
        conv_four, sums = run_kernel(conv_four_kernel, [((outer, mid), f32), narrow_sums], [core_at, cells],
                                     [block_one, other_block, reduce2, mask], flops=4 * outer * wide * mid, held=(2, 3,))
        near_one, sums = tie(near_one, sums)
        got = spread(sums, True)
        other_four = swap(conv_four)
        act_four, conv_five, sums, moments_four = run_kernel(
            gridded(conv_five_kernel),
            [((outer, 2 * mid), bf16), ((outer, mid), f32), narrow_sums, narrow_moments], [core_at, cells],
            [got, all_cells, conv_four, other_four, both_four, mask, spatial2], flops=36 * outer * mid * mid,
            scratch=[pltpu.VMEM((outer, 2 * mid), f32)], held=(0, 1, 5, 6,))
        got = spread(sums, True)
        other_five = swap(conv_five)
        act_five, conv_six, sums, moments_five = run_kernel(
            expand_kernel, [((outer, 2 * mid), bf16), ((outer, wide), f32), wide_sums, narrow_moments], [core_at, cells],
            [got, all_cells, conv_five, other_five, both_five, mask, expand2], flops=4 * outer * mid * wide,
            scratch=[pltpu.VMEM((outer, 2 * mid), f32)], held=(0, 1, 5, 6,))
        near_skip, got = tie(near_skip, spread(sums, False))
        near_act = gather_near(jnp.concatenate([slot(act_four, core, mid, 1), slot(act_five, core, mid, 1)], axis=1))
        block_two, grad_join2, sums, moments_six = run_kernel(
            top_kernel, [((outer, wide), bf16), ((outer, wide), f32), wide_sums, wide_moments], [],
            [got, all_cells, conv_six, block_one, cotangent.reshape(outer, wide), norm_six, mask], flops=30 * outer * wide, held=(0, 1, 6,))
        near_one, sums = tie(near_one, sums)
        got = spread(sums, False)
        own_one = slot(near_one, near_at % 2, share, 1)
        own_one, got = tie(own_one, got)
        other_one = swap(own_one)

        norm_out = ((2, mid), f32)
        wide_norm_out = ((2, wide), f32)
        grad_six, norm_six_grad, part = run_kernel(
            functools.partial(back_dense_kernel, False), [((outer, wide), bf16), wide_norm_out, ((outer, mid), bf16)], [core_at],
            [got, grad_join2, conv_six, moments_six, norm_six, mask, expand2], flops=2 * outer * wide * mid, held=(0, 5, 6,))
        part = swap(part)
        grad_pre, sums = run_kernel(
            own_dense_kernel, [((outer, mid), f32), own_sums], [core_at],
            [grad_six, part, expand2, conv_five, moments_five, norm_five, mask], flops=2 * outer * wide * mid, held=(1, 2, 6,))
        grad_six, sums = tie(grad_six, sums)
        (near_act, own_one, other_one), sums = tie((near_act, own_one, other_one), sums)
        got = spread(sums, True)
        up_six = to_near([slot(grad_six, at, mid, 1) for at in near_order])
        other_near_act = swap(near_act)
        near_one = jnp.where(core == near_at // 2, own_one, other_one)
        (up_six, near_one, other_near_act), got = tie((up_six, near_one, other_near_act), got)

        grad_five, norm_five_grad, part = run_kernel(
            gridded(back_five_kernel), [((outer, mid), bf16), norm_out, ((outer, mid), bf16)], [core_at],
            [got, grad_pre, conv_five, moments_five, norm_five, mask, spatial2], flops=18 * outer * mid * mid, held=(0, 5, 6,))
        part = swap(part)
        up_five = to_near([grad_five] * near)
        grad_pre, sums = run_kernel(
            gridded(own_five_kernel), [((outer, mid), f32), own_sums], [core_at],
            [grad_five, part, spatial2, conv_four, moments_four, norm_four, mask], flops=18 * outer * mid * mid, held=(1, 2, 6,))
        up_five, sums = tie(up_five, sums)
        got = spread(sums, True)
        rows_a = 2 * mid + 9 * share
        top_part, = run_kernel(
            functools.partial(weight_top_kernel, grid, width, near, far), [((rows_a, mid), bf16)], [core_at, near_place],
            [near_act, other_near_act, *up_six, *up_five],
            scratch=[pltpu.VMEM((2 * mid, mid), f32), pltpu.VMEM((9, share, mid), f32)])
        (top_part, near_skip), got = tie((top_part, near_skip), got)
        top_rows = lax.psum_scatter(top_part, "dp", scatter_dimension=0, tiled=True, axis_index_groups=far_groups)
        other_near_skip = swap(near_skip)

        grad_four, norm_four_grad, part = run_kernel(
            functools.partial(back_dense_kernel, True), [((outer, mid), bf16), norm_out, ((outer, wide), bf16)], [core_at],
            [got, grad_pre, conv_four, moments_four, norm_four, mask, reduce2], flops=2 * outer * wide * mid, held=(0, 5, 6,))
        part = swap(part)
        grad_join1, sums = run_kernel(
            own_four_kernel, [((outer, wide), f32), join_sums], [core_at],
            [grad_four, part, reduce2, grad_join2, conv_three, moments_three, norm_three, conv_skip, moments_skip, norm_skip,
             mask], flops=2 * outer * wide * mid, held=(1, 2, 10,))
        (grad_four, other_near_skip), sums = tie((grad_four, other_near_skip), sums)
        got = spread(sums, False)
        reduce2_parts = run_kernel(
            functools.partial(weight_four_kernel, near), [((2 * mid, mid), bf16)] * near, [core_at, near_place],
            [block_one, other_block, grad_four], flops=4 * outer * wide * mid, scratch=[pltpu.VMEM((2 * wide, mid), f32)])
        reduce2_parts = to_near(reduce2_parts)

        top_rows, got = tie(top_rows, got)
        grad_three, grad_skip, norm_three_grad, norm_skip_grad, part = run_kernel(
            back_join_kernel,
            [((outer, wide), bf16), ((outer, wide), bf16), wide_norm_out, wide_norm_out, ((outer, mid), bf16)], [core_at],
            [got, grad_join1, conv_three, moments_three, norm_three, conv_skip, moments_skip, norm_skip, mask, expand1],
            flops=2 * outer * wide * mid, held=(0, 8, 9,))
        reduce2_parts, part = tie(reduce2_parts, swap(part))
        grad_pre, sums = run_kernel(
            own_dense_kernel, [((outer, mid), f32), own_sums], [core_at],
            [grad_three, part, expand1, conv_two, moments_two, norm_two, mask], flops=2 * outer * wide * mid, held=(1, 2, 6,))
        top_rows, sums = tie(top_rows, sums)
        got = spread(sums, True)
        up_join = to_near([
            jnp.concatenate([slot(grad_three, at, mid, 1), slot(grad_skip, at, mid, 1)], axis=1) for at in near_order])

        rows_b = (4 * mid + 2 * cid) // far
        bucket_b = run_kernel(
            functools.partial(weight_bottom_kernel, near, far, cid), [((rows_b, mid), bf16)] * far,
            [core_at, near_place, far_place], [near_skip, other_near_skip, *reduce2_parts, *up_join],
            flops=2 * near * outer * (4 * mid + 2 * cid) * mid,
            scratch=[pltpu.VMEM((2 * mid, mid), f32), pltpu.VMEM((2 * mid, mid), f32), pltpu.VMEM((2 * cid, mid), f32)])
        top_rows = tell_far(top_rows)
        top_rows, got = tie(top_rows, got)
        top_all = gather_near(jnp.concatenate(top_rows))
        bucket_b, got = tie(bucket_b, got)
        bucket_b = to_far(bucket_b)

        grad_two, norm_two_grad, part = run_kernel(
            gridded(back_two_kernel), [((outer, mid), bf16), norm_out, ((inner, mid), bf16)], [core_at],
            [got, grad_pre, conv_two, moments_two, norm_two, mask, spatial1], flops=18 * outer * mid * mid, held=(0, 5, 6,))
        part = swap(part)
        up_two = to_near([grad_two] * near)
        grad_pre, sums = run_kernel(
            gridded(own_two_kernel), [((inner, mid), f32), own_sums], [core_at],
            [grad_two, part, spatial1, conv_one, moments_one, norm_one, mask], flops=18 * outer * mid * mid, held=(1, 2, 6,))
        (up_two, bucket_b[2]), sums = tie((up_two, bucket_b[2]), sums)
        got = spread(sums, True)
        bucket_c = run_kernel(
            functools.partial(weight_two_kernel, grid, width, near, far), [((9 * share // far, mid), bf16)] * far,
            [near_place, far_place], [near_one, *up_two], flops=18 * near * outer * share * mid,
            scratch=[pltpu.VMEM((9, share, mid), f32)])
        (bucket_c, bucket_b), got = tie((bucket_c, bucket_b), got)
        bucket_b = tell_far(total(bucket_b).astype(bf16))

        grad_one, norm_one_grad, part = run_kernel(
            back_one_kernel, [((inner, mid), bf16), norm_out, ((inner, cid), bf16)], [core_at],
            [got, grad_pre, conv_one, moments_one, norm_one, mask, reduce1, grad_skip, shortcut],
            flops=2 * inner * mid * cid, held=(0, 5, 6, 8,))
        part = swap(part)
        reduce1_parts = run_kernel(
            functools.partial(weight_one_kernel, near), [((2 * cid // near, mid), bf16)] * near, [core_at, near_place],
            [own_x, other_x, grad_one], flops=4 * inner * cid * mid, scratch=[pltpu.VMEM((2 * cid, mid), f32)])
        bucket_b[far // 2 + 1 :], reduce1_parts = tie(bucket_b[far // 2 + 1 :], reduce1_parts)
        reduce1_parts = to_near(reduce1_parts)
        reduce1_rows = total(reduce1_parts).astype(bf16)
        bucket_c = [jnp.concatenate([piece, slot(reduce1_rows, at, reduce1_rows.shape[0] // far, 0)])
                    for piece, at in zip(bucket_c, far_order)]
        bucket_b, bucket_c = tie(bucket_b, bucket_c)
        bucket_b = jnp.concatenate(bucket_b)
        rows_b = bucket_b.shape[0]
        bucket_b = tell_near_first(bucket_b)
        bucket_c = to_far(bucket_c)
        bucket_b, bucket_c = tie(bucket_b, bucket_c)
        def lay(arrays, chunks, layouts):
            return laid_out(arrays, chunks, near, far, near_at, far_at, layouts)

        kernel_dims = (3, 3, 2 * mid, mid)
        wide_dims = (2 * mid, 4 * mid)
        chunk = rows_a // far
        top_chunks = [(0, (member * far + b) * chunk, member, False, b) for member in range(near) for b in range(far)]
        expand2_grad, spatial2_grad = lay([top_all], top_chunks, [("columns", wide_dims), ("kernel", kernel_dims)])
        input_grad, = run_kernel(
            gridded(own_x_kernel), [((imgs, 4 * grid, cid), bf16)], [core_at],
            [grad_one, part, reduce1, grad_skip, shortcut, mask], flops=4 * inner * mid * cid, held=(1, 2, 4, 5,))
        bucket_b, sums_c = tie(bucket_b, total(bucket_c).astype(bf16))
        bucket_c = tell_far(sums_c)
        bucket_b = tell_near_then(bucket_b)
        (bucket_b, expand2_grad, spatial2_grad, input_grad), bucket_c = tie(
            (bucket_b, expand2_grad, spatial2_grad, input_grad), bucket_c)
        bucket_c = jnp.concatenate(bucket_c)
        rows_c = bucket_c.shape[0]
        bucket_c = tell_near_first(bucket_c)
        reduce2_grad, expand1_grad, shortcut_grad = lay(
            bucket_b, told_chunks(rows_b),
            [("rows", reduce2.shape), ("columns", wide_dims), ("columns", shortcut.shape)])
        (reduce2_grad, expand1_grad, shortcut_grad), bucket_c = tie((reduce2_grad, expand1_grad, shortcut_grad), bucket_c)
        bucket_c = tell_near_then(bucket_c)
        spatial1_grad, reduce1_grad = lay(
            bucket_c, told_chunks(rows_c), [("kernel", kernel_dims), ("rows", reduce1.shape)])
        grads = (reduce1_grad, spatial1_grad, expand1_grad, shortcut_grad, reduce2_grad, spatial2_grad, expand2_grad)
        return (block_one.reshape(cotangent.shape), block_two.reshape(cotangent.shape), input_grad.reshape(images.shape),
                *grads, norm_one_grad, norm_two_grad, norm_three_grad, norm_skip_grad, norm_four_grad, norm_five_grad,
                norm_six_grad)

    pixels = P("dp", None, None, "chan")
    weights = (P(None, "chan"), P(None, None, None, "chan")) + (P(None, "chan"),) * 3 + (P(None, None, None, "chan"), P(None, "chan"))
    norms = (P(None, "chan"),) * 7
    return jax.shard_map(
        local, mesh=mesh,
        in_specs=(pixels, P("dp", None), pixels) + weights + norms,
        out_specs=(pixels, pixels, pixels) + weights + norms,
        check_vma=False)
```

```python
import functools
import math

import jax
import jax.numpy as jnp
from jax import lax
from jax.experimental import pallas as pl
from jax.experimental.pallas import tpu as pltpu
from jax.sharding import PartitionSpec as P

epsilon = 1e-05
f32 = jnp.float32
bf16 = jnp.bfloat16
SWAP = [(0, 1), (1, 0)]


def swap(value):
    return lax.ppermute(value, "chan", SWAP)


def in_order(core, own, other, axis=-1):
    return jnp.where(
        core == 0,
        jnp.concatenate([own, other], axis),
        jnp.concatenate([other, own], axis),
    )


def tie(early, late):
    return lax.optimization_barrier((early, late))


def send(value, count, bits):
    return lax.ppermute(value, "dp", [(at, at ^ bits) for at in range(count)])


def slot(value, index, size, axis):
    return lax.dynamic_slice_in_dim(value, index * size, size, axis)


def lay_kernel(near, far, layouts, chunks, at_ref, *refs):
    ins, outs = refs[: len(refs) - len(layouts)], refs[len(refs) - len(layouts) :]
    near_at, far_at = at_ref[0], at_ref[1]
    for which, start, member, relative, b in chunks:
        owner = far_at ^ b
        if relative:
            member = near_at ^ member
        for (kind, dims), out in zip(layouts, outs):
            if kind == "kernel":
                size = dims[2] // near // far
                for tap in range(9):
                    first = pl.multiple_of(member * (size * far) + owner * size, size)
                    out[tap // 3, tap % 3, pl.ds(first, size), :] = ins[which][start : start + size, :].astype(f32)
                    start += size
            elif kind == "rows":
                size = dims[0] // near // far
                first = pl.multiple_of(member * (size * far) + owner * size, size)
                out[pl.ds(first, size), :] = ins[which][start : start + size, :].astype(f32)
                start += size
            else:
                size, lanes = dims[0] // far, dims[1] // near
                first = pl.multiple_of(owner * size, size)
                lane = pl.multiple_of(member * lanes, lanes)
                out[pl.ds(first, size), pl.ds(lane, lanes)] = ins[which][start : start + size, :].astype(f32)
                start += size


def laid_out(arrays, chunks, near, far, near_at, far_at, layouts):
    return pl.pallas_call(
        functools.partial(lay_kernel, near, far, layouts, chunks),
        out_shape=[jax.ShapeDtypeStruct(dims, f32) for _, dims in layouts],
        in_specs=[pl.BlockSpec(memory_space=pltpu.SMEM)] + [pl.BlockSpec(memory_space=pltpu.VMEM)] * len(arrays),
        out_specs=[pl.BlockSpec(memory_space=pltpu.VMEM)] * len(layouts),
        compiler_params=pltpu.CompilerParams(vmem_limit_bytes=40 * 2**20),
    )(jnp.stack([near_at, far_at]).astype(jnp.int32), *arrays)


def spec(kind):
    return pl.BlockSpec(memory_space=kind)


def staged(body, scalars, ins, outs, held, *refs):
    head, refs = refs[:scalars], refs[scalars:]
    given, results, refs = refs[:ins], refs[ins : ins + outs], refs[ins + outs :]
    moved = [at for at in range(ins) if at not in held]
    here, made, extra = refs[: len(moved)], refs[len(moved) : len(moved) + outs], refs[len(moved) + outs : -2]
    in_sems, out_sems = refs[-2:]
    arrivals = [pltpu.make_async_copy(given[at], here[k], in_sems.at[k]) for k, at in enumerate(moved)]
    for copy in arrivals:
        copy.start()
    for copy in arrivals:
        copy.wait()
    local = dict(zip(moved, here))
    body(*head, *[local.get(at, given[at]) for at in range(ins)], *made, *extra)
    leaving = [pltpu.make_async_copy(made[at], results[at], out_sems.at[at]) for at in range(outs)]
    for copy in leaving:
        copy.start()
    for copy in leaving:
        copy.wait()


def run_kernel(body, outs, scalars, arrays, flops=0, scratch=(), held=()):
    return pl.pallas_call(
        functools.partial(staged, body, len(scalars), len(arrays), len(outs), held),
        out_shape=[pltpu.HBM(shape, dtype) for shape, dtype in outs],
        in_specs=[spec(pltpu.SMEM)] * len(scalars)
        + [spec(pltpu.VMEM if at in held else pltpu.HBM) for at in range(len(arrays))],
        out_specs=[spec(pltpu.HBM)] * len(outs),
        scratch_shapes=[pltpu.VMEM(x.shape, x.dtype) for at, x in enumerate(arrays) if at not in held]
        + [pltpu.VMEM(shape, dtype) for shape, dtype in outs]
        + list(scratch) + [pltpu.SemaphoreType.DMA((len(arrays),)), pltpu.SemaphoreType.DMA((len(outs),))],
        cost_estimate=pl.CostEstimate(flops=1, bytes_accessed=1, transcendentals=0),
        compiler_params=pltpu.CompilerParams(vmem_limit_bytes=28 * 2**20),
    )(*scalars, *[x if at in held else pltpu.with_memory_space_constraint(x, pltpu.HBM) for at, x in enumerate(arrays)])


def widen(mask_ref, lanes):
    mask = mask_ref[...]
    return mask if lanes == 128 else jnp.concatenate([mask] * (lanes // 128), axis=1)


def dot(left, right):
    return lax.dot_general(left, right, (((1,), (0,)), ((), ())), preferred_element_type=f32)


def dot_nt(left, right):
    return lax.dot_general(left, right, (((1,), (1,)), ((), ())), preferred_element_type=f32)


def halves(ref, core, size):
    own = pl.ds(pl.multiple_of(core * size, size), size)
    other = pl.ds(pl.multiple_of((1 - core) * size, size), size)
    return own, other


def stats(values, mask, cells):
    total = jnp.sum(values * mask, axis=0, keepdims=True)
    centred = (values - total / cells) * mask
    return [total, jnp.sum(centred * centred, axis=0, keepdims=True)]


def put_rows(out_ref, rows):
    tile = jnp.concatenate(rows, axis=0)
    for at in range(out_ref.shape[0]):
        out_ref[at] = tile


def moments(tiles, cells_ref, scale=1.0, first=0):
    lanes = tiles[0].shape[1]
    cells = jnp.concatenate([cells_ref[...]] * (lanes // 128), axis=1) * scale
    pixels = jnp.sum(cells, axis=0, keepdims=True)
    totals = [tile[first : first + 1] for tile in tiles]
    mean = functools.reduce(jnp.add, totals) / pixels
    spread = functools.reduce(jnp.add, [tile[first + 1 : first + 2] for tile in tiles])
    offsets = jnp.concatenate(totals, axis=0) / cells - mean
    spread = spread + jnp.sum(cells * offsets * offsets, axis=0, keepdims=True)
    return mean, lax.rsqrt(spread / pixels + epsilon), pixels


def put_moments(out_ref, mean, inverse, pixels):
    lanes = mean.shape[1]
    out_ref[...] = jnp.concatenate([mean, inverse, pixels, jnp.zeros((5, lanes), f32)], axis=0)


def silu_slope(values):
    logistic = jax.nn.sigmoid(values)
    return logistic * (1.0 + values * (1.0 - logistic))


def shift_cols(values, by, width):
    rows = values.shape[0]
    column = lax.broadcasted_iota(jnp.int32, values.shape, 0) & (width - 1)
    moved = pltpu.roll(values, (-by) % rows, 0)
    return jnp.where(column == (0 if by < 0 else width - 1), 0.0, moved)


def shift_rows(values, by, width, grid):
    if by == 0:
        return values
    zeros = jnp.zeros((width, values.shape[1]), values.dtype)
    out = []
    for start in range(0, values.shape[0], grid):
        if by < 0:
            out += [zeros, values[start : start + grid - width]]
        else:
            out += [values[start + width : start + grid], zeros]
    return jnp.concatenate(out, axis=0)


def pixel_of(index, grid, width):
    plane = jnp.zeros_like(index)
    for at in range(1, 4):
        plane = plane + (index >= at * grid).astype(jnp.int32)
    inside = index - plane * grid
    line = inside >> (width.bit_length() - 1)
    column = inside & (width - 1)
    return (2 * line + (plane >> 1)) * (2 * width) + 2 * column + (plane & 1)


def sort_kernel(grid, width, images_ref, mask_ref, out_ref):
    size = 4 * grid
    target = lax.broadcasted_iota(jnp.int32, (size, size), 0)
    source = lax.broadcasted_iota(jnp.int32, (size, size), 1)
    pick = jnp.where(source == pixel_of(target, grid, width), 1.0, 0.0).astype(bf16)
    imgs = images_ref.shape[0]
    lanes = images_ref.shape[2]
    mask = widen(mask_ref, lanes)
    for n in range(imgs):
        ordered = dot(pick, images_ref[n])
        for plane in range(4):
            first = (plane * imgs + n) * grid
            rows = ordered[plane * grid : (plane + 1) * grid] * mask[n * grid : (n + 1) * grid]
            out_ref[first : first + grid, :] = rows.astype(bf16)


def conv_one_kernel(core_ref, cells_ref, own_ref, other_ref, weight_ref, mask_ref, out_ref, stats_ref):
    own, other = halves(weight_ref, core_ref[0], own_ref.shape[1])
    values = dot(own_ref[...], weight_ref[own, :]) + dot(other_ref[...], weight_ref[other, :])
    out_ref[...] = values
    mask = widen(mask_ref, values.shape[1])
    cells = jnp.full((1, values.shape[1]), cells_ref[0])
    put_rows(stats_ref, stats(values, jnp.concatenate([mask] * 4, axis=0), 4.0 * cells_ref[0]) + [cells, cells])


def conv_skip_kernel(core_ref, cells_ref, own_ref, other_ref, weight_ref, mask_ref, out_ref, stats_ref):
    rows = mask_ref.shape[0]
    own, other = halves(weight_ref, core_ref[0], own_ref.shape[1])
    values = dot(own_ref[:rows], weight_ref[own, :]) + dot(other_ref[:rows], weight_ref[other, :])
    out_ref[...] = values
    mask = widen(mask_ref, values.shape[1])
    stats_ref[...] = jnp.concatenate(stats(values, mask, cells_ref[0]), axis=0)


def norm_act(got_ref, all_cells_ref, scale, own_ref, other_ref, norm_ref, mask, core, raw_ref, act_ref, moments_ref):
    lanes = own_ref.shape[1]
    own, other = halves(None, core, lanes)
    raw_ref[:, own] = own_ref[...]
    raw_ref[:, other] = other_ref[...]
    count = got_ref.shape[0] // 2
    for half in range(2):
        mean, inverse, pixels = moments([got_ref[2 * at + half] for at in range(count)], all_cells_ref, scale)

        @pl.when(core == half)
        def _():
            put_moments(moments_ref, mean, inverse, pixels)

        at = slice(half * lanes, (half + 1) * lanes)
        pre = norm_ref[0:1, at] * ((raw_ref[:, at] - mean) * inverse) + norm_ref[1:2, at]
        act_ref[:, at] = (pre * jax.nn.sigmoid(pre) * mask).astype(bf16)


def conv_two_kernel(grid, width, core_ref, cells_ref, got_ref, own_ref, other_ref, norm_ref, mask_ref, weight_ref,
                    act_ref, out_ref, stats_ref, moments_ref, all_cells_ref, raw_ref):
    rows = mask_ref.shape[0]
    lanes = own_ref.shape[1]
    mask = widen(mask_ref, lanes)
    for at in range(got_ref.shape[0] // 2):
        all_cells_ref[at : at + 1, :] = got_ref[2 * at, 2:3, :128]
    norm_act(got_ref, all_cells_ref, 4.0, own_ref, other_ref, norm_ref, jnp.concatenate([mask] * 4, axis=0), core_ref[0],
             raw_ref, act_ref, moments_ref)
    values = jnp.zeros((rows, out_ref.shape[1]), f32)
    for plane in range(4):
        here = act_ref[plane * rows : (plane + 1) * rows, :]
        by_col = {1: here} if plane % 2 == 0 else {2: here, 0: shift_cols(here.astype(f32), -1, width).astype(bf16)}
        for s, moved in by_col.items():
            for r in ((1,) if plane < 2 else (0, 2)):
                values = values + dot(shift_rows(moved, -1 if r == 0 else 0, width, grid), weight_ref[r, s])
    out_ref[...] = values
    put_rows(stats_ref, stats(values, mask, cells_ref[0]))


def conv_five_kernel(grid, width, core_ref, cells_ref, got_ref, all_cells_ref, own_ref, other_ref, norm_ref, mask_ref, weight_ref,
                     act_ref, out_ref, stats_ref, moments_ref, raw_ref):
    rows = mask_ref.shape[0]
    mask = widen(mask_ref, own_ref.shape[1])
    norm_act(got_ref, all_cells_ref, 1.0, own_ref, other_ref, norm_ref, mask, core_ref[0], raw_ref, act_ref, moments_ref)
    values = jnp.zeros((rows, out_ref.shape[1]), f32)
    here = act_ref[...]
    for s in range(3):
        moved = here if s == 1 else shift_cols(here.astype(f32), s - 1, width).astype(bf16)
        for r in range(3):
            values = values + dot(shift_rows(moved, r - 1, width, grid), weight_ref[r, s])
    out_ref[...] = values
    put_rows(stats_ref, stats(values, mask, cells_ref[0]))


def expand_kernel(core_ref, cells_ref, got_ref, all_cells_ref, own_ref, other_ref, norm_ref, mask_ref, weight_ref, *refs):
    more_refs, (act_ref, out_ref, stats_ref, moments_ref, raw_ref) = refs[:-5], refs[-5:]
    norm_act(got_ref, all_cells_ref, 1.0, own_ref, other_ref, norm_ref, widen(mask_ref, own_ref.shape[1]), core_ref[0],
             raw_ref, act_ref, moments_ref)
    values = dot(act_ref[...], weight_ref[...])
    out_ref[...] = values
    more = [more_refs[0][...]] if more_refs else []
    put_rows(stats_ref, stats(values, widen(mask_ref, values.shape[1]), cells_ref[0]) + more)


def normed(raw_ref, moments_ref):
    return (raw_ref[...] - moments_ref[0:1]) * moments_ref[1:2]


def scaled(norm_ref, hat):
    return norm_ref[0:1] * hat + norm_ref[1:2]


def join_kernel(got_ref, all_cells_ref, three_ref, skip_ref, norm_three_ref, norm_skip_ref, mask_ref, out_ref, moments_three_ref,
                moments_skip_ref):
    tiles = [got_ref[at] for at in range(got_ref.shape[0])]
    put_moments(moments_three_ref, *moments(tiles, all_cells_ref))
    put_moments(moments_skip_ref, *moments(tiles, all_cells_ref, first=2))
    joined = scaled(norm_three_ref, normed(three_ref, moments_three_ref)) + scaled(
        norm_skip_ref, normed(skip_ref, moments_skip_ref))
    out_ref[...] = (joined * jax.nn.sigmoid(joined) * widen(mask_ref, joined.shape[1])).astype(bf16)


def conv_four_kernel(core_ref, cells_ref, own_ref, other_ref, weight_ref, mask_ref, out_ref, stats_ref):
    own, other = halves(weight_ref, core_ref[0], own_ref.shape[1])
    values = dot(own_ref[...], weight_ref[own, :]) + dot(other_ref[...], weight_ref[other, :])
    out_ref[...] = values
    put_rows(stats_ref, stats(values, widen(mask_ref, values.shape[1]), cells_ref[0]))


def put_sums(out_ref, grad, *hats):
    rows = [jnp.sum(grad, axis=0, keepdims=True)] + [jnp.sum(grad * hat, axis=0, keepdims=True) for hat in hats]
    put_rows(out_ref, rows + [rows[0]] * (out_ref.shape[1] - len(rows)))


def top_kernel(got_ref, all_cells_ref, six_ref, block_ref, cotangent_ref, norm_ref, mask_ref, out_ref, grad_ref, sums_ref, moments_ref):
    put_moments(moments_ref, *moments([got_ref[at] for at in range(got_ref.shape[0])], all_cells_ref))
    hat = normed(six_ref, moments_ref)
    joined = scaled(norm_ref, hat) + block_ref[...].astype(f32)
    mask = widen(mask_ref, joined.shape[1])
    logistic = jax.nn.sigmoid(joined)
    out_ref[...] = (joined * logistic * mask).astype(bf16)
    grad = cotangent_ref[...].astype(f32) * mask * (logistic * (1.0 + joined * (1.0 - logistic)))
    grad_ref[...] = grad
    put_sums(sums_ref, grad, hat)


def sums_of(got_ref, core=None):
    if core is None:
        return functools.reduce(jnp.add, [got_ref[at] for at in range(got_ref.shape[0])])
    return functools.reduce(jnp.add, [got_ref[2 * at + core] for at in range(got_ref.shape[0] // 2)])


def norm_back(grad, hat, moments_ref, norm_ref, beta, gamma, mask):
    inside = grad - (beta + hat * gamma) / moments_ref[2:3]
    return (mask * (norm_ref[0:1] * moments_ref[1:2]) * inside).astype(bf16)


def back_dense_kernel(both, core_ref, got_ref, grad_ref, raw_ref, moments_ref, norm_ref, mask_ref, weight_ref, out_ref,
                    norm_grad_ref, send_ref):
    sums = sums_of(got_ref, core_ref[0] if both else None)
    beta, gamma = sums[0:1], sums[1:2]
    norm_grad_ref[...] = jnp.concatenate([gamma, beta], axis=0)
    grad = norm_back(grad_ref[...], normed(raw_ref, moments_ref), moments_ref, norm_ref, beta, gamma,
                     widen(mask_ref, raw_ref.shape[1]))
    out_ref[...] = grad
    own, other = halves(weight_ref, core_ref[0], weight_ref.shape[0] // 2)
    send_ref[...] = dot_nt(grad, weight_ref[other, :]).astype(bf16)


def own_dense_kernel(core_ref, up_ref, got_ref, weight_ref, raw_ref, moments_ref, norm_ref, mask_ref, out_ref, sums_ref):
    own, other = halves(weight_ref, core_ref[0], weight_ref.shape[0] // 2)
    back = dot_nt(up_ref[...], weight_ref[own, :]) + got_ref[...].astype(f32)
    hat = normed(raw_ref, moments_ref)
    grad = back * widen(mask_ref, raw_ref.shape[1]) * silu_slope(scaled(norm_ref, hat))
    out_ref[...] = grad
    put_sums(sums_ref, grad, hat)


def moved_grads(grad, cols, rows, width, grid):
    wide = grad.astype(f32)
    out = {}
    for col in cols:
        moved = grad if col == 0 else shift_cols(wide, col, width).astype(bf16)
        for row in rows:
            out[row, col] = shift_rows(moved, row, width, grid)
    return out


def back_five_kernel(grid, width, core_ref, got_ref, grad_ref, raw_ref, moments_ref, norm_ref, mask_ref, weight_ref,
                     out_ref, norm_grad_ref, send_ref):
    sums = sums_of(got_ref, core_ref[0])
    beta, gamma = sums[0:1], sums[1:2]
    norm_grad_ref[...] = jnp.concatenate([gamma, beta], axis=0)
    grad = norm_back(grad_ref[...], normed(raw_ref, moments_ref), moments_ref, norm_ref, beta, gamma,
                     widen(mask_ref, raw_ref.shape[1]))
    out_ref[...] = grad
    own, other = halves(weight_ref, core_ref[0], weight_ref.shape[2] // 2)
    moved = moved_grads(grad, (-1, 0, 1), (-1, 0, 1), width, grid)
    back = functools.reduce(
        jnp.add, [dot_nt(moved[1 - r, 1 - s], weight_ref[r, s, other, :]) for r in range(3) for s in range(3)])
    send_ref[...] = back.astype(bf16)


def own_five_kernel(grid, width, core_ref, up_ref, got_ref, weight_ref, raw_ref, moments_ref, norm_ref, mask_ref, out_ref,
                    sums_ref):
    own, other = halves(weight_ref, core_ref[0], weight_ref.shape[2] // 2)
    moved = moved_grads(up_ref[...], (-1, 0, 1), (-1, 0, 1), width, grid)
    back = functools.reduce(
        jnp.add, [dot_nt(moved[1 - r, 1 - s], weight_ref[r, s, own, :]) for r in range(3) for s in range(3)])
    hat = normed(raw_ref, moments_ref)
    grad = (back + got_ref[...].astype(f32)) * widen(mask_ref, raw_ref.shape[1]) * silu_slope(scaled(norm_ref, hat))
    out_ref[...] = grad
    put_sums(sums_ref, grad, hat)


def own_four_kernel(core_ref, up_ref, got_ref, weight_ref, top_ref, three_ref, moments_three_ref, norm_three_ref, skip_ref,
                    moments_skip_ref, norm_skip_ref, mask_ref, out_ref, sums_ref):
    own, other = halves(weight_ref, core_ref[0], weight_ref.shape[0] // 2)
    back = dot_nt(up_ref[...], weight_ref[own, :]) + got_ref[...].astype(f32) + top_ref[...]
    hat_three = normed(three_ref, moments_three_ref)
    hat_skip = normed(skip_ref, moments_skip_ref)
    joined = scaled(norm_three_ref, hat_three) + scaled(norm_skip_ref, hat_skip)
    grad = back * widen(mask_ref, joined.shape[1]) * silu_slope(joined)
    out_ref[...] = grad
    put_sums(sums_ref, grad, hat_three, hat_skip)


def back_join_kernel(core_ref, got_ref, grad_ref, three_ref, moments_three_ref, norm_three_ref, skip_ref, moments_skip_ref,
                     norm_skip_ref, mask_ref, weight_ref, out_three_ref, out_skip_ref, norm_three_grad_ref,
                     norm_skip_grad_ref, send_ref):
    sums = sums_of(got_ref)
    beta, gamma_three, gamma_skip = sums[0:1], sums[1:2], sums[2:3]
    norm_three_grad_ref[...] = jnp.concatenate([gamma_three, beta], axis=0)
    norm_skip_grad_ref[...] = jnp.concatenate([gamma_skip, beta], axis=0)
    mask = widen(mask_ref, three_ref.shape[1])
    grad = norm_back(grad_ref[...], normed(three_ref, moments_three_ref), moments_three_ref, norm_three_ref, beta,
                     gamma_three, mask)
    out_three_ref[...] = grad
    own, other = halves(weight_ref, core_ref[0], weight_ref.shape[0] // 2)
    send_ref[...] = dot_nt(grad, weight_ref[other, :]).astype(bf16)
    out_skip_ref[...] = norm_back(grad_ref[...], normed(skip_ref, moments_skip_ref), moments_skip_ref, norm_skip_ref, beta,
                                  gamma_skip, mask)


def planes_back(moved, weight_ref, at):
    def term(r, s, row, col):
        return dot_nt(moved[row, col], weight_ref[r, s, at, :])

    return [
        term(1, 1, 0, 0),
        term(1, 2, 0, 0) + term(1, 0, 0, 1),
        term(2, 1, 0, 0) + term(0, 1, 1, 0),
        term(2, 2, 0, 0) + term(2, 0, 0, 1) + term(0, 2, 1, 0) + term(0, 0, 1, 1),
    ]


def back_two_kernel(grid, width, core_ref, got_ref, grad_ref, raw_ref, moments_ref, norm_ref, mask_ref, weight_ref, out_ref,
                    norm_grad_ref, send_ref):
    sums = sums_of(got_ref, core_ref[0])
    beta, gamma = sums[0:1], sums[1:2]
    norm_grad_ref[...] = jnp.concatenate([gamma, beta], axis=0)
    grad = norm_back(grad_ref[...], normed(raw_ref, moments_ref), moments_ref, norm_ref, beta, gamma,
                     widen(mask_ref, raw_ref.shape[1]))
    out_ref[...] = grad
    own, other = halves(weight_ref, core_ref[0], weight_ref.shape[2] // 2)
    rows = grad.shape[0]
    for plane, back in enumerate(planes_back(moved_grads(grad, (0, 1), (0, 1), width, grid), weight_ref, other)):
        send_ref[plane * rows : (plane + 1) * rows, :] = back.astype(bf16)


def own_two_kernel(grid, width, core_ref, up_ref, got_ref, weight_ref, raw_ref, moments_ref, norm_ref, mask_ref, out_ref,
                   sums_ref):
    own, other = halves(weight_ref, core_ref[0], weight_ref.shape[2] // 2)
    rows = up_ref.shape[0]
    mask = widen(mask_ref, raw_ref.shape[1])
    beta = jnp.zeros((1, raw_ref.shape[1]), f32)
    gamma = beta
    for plane, back in enumerate(planes_back(moved_grads(up_ref[...], (0, 1), (0, 1), width, grid), weight_ref, own)):
        at = slice(plane * rows, (plane + 1) * rows)
        hat = (raw_ref[at, :] - moments_ref[0:1]) * moments_ref[1:2]
        grad = (back + got_ref[at, :].astype(f32)) * mask * silu_slope(scaled(norm_ref, hat))
        out_ref[at, :] = grad
        beta = beta + jnp.sum(grad, axis=0, keepdims=True)
        gamma = gamma + jnp.sum(grad * hat, axis=0, keepdims=True)
    put_rows(sums_ref, [beta, gamma])


def back_one_kernel(core_ref, got_ref, grad_ref, raw_ref, moments_ref, norm_ref, mask_ref, weight_ref, up_skip_ref,
                    shortcut_ref, out_ref, norm_grad_ref, send_ref):
    sums = sums_of(got_ref, core_ref[0])
    beta, gamma = sums[0:1], sums[1:2]
    norm_grad_ref[...] = jnp.concatenate([gamma, beta], axis=0)
    mask = jnp.concatenate([widen(mask_ref, raw_ref.shape[1])] * 4, axis=0)
    grad = norm_back(grad_ref[...], normed(raw_ref, moments_ref), moments_ref, norm_ref, beta, gamma, mask)
    out_ref[...] = grad
    own, other = halves(weight_ref, core_ref[0], weight_ref.shape[0] // 2)
    rows = mask_ref.shape[0]
    skip = dot_nt(up_skip_ref[...], shortcut_ref[other, :])
    send_ref[:rows, :] = (dot_nt(grad[:rows], weight_ref[other, :]) + skip).astype(bf16)
    send_ref[rows:, :] = dot_nt(grad[rows:], weight_ref[other, :]).astype(bf16)


def own_x_kernel(grid, width, core_ref, up_ref, got_ref, weight_ref, up_skip_ref, shortcut_ref, mask_ref, out_ref):
    own, other = halves(weight_ref, core_ref[0], weight_ref.shape[0] // 2)
    rows = mask_ref.shape[0]
    imgs = out_ref.shape[0]
    back = dot_nt(up_ref[...], weight_ref[own, :]) + got_ref[...].astype(f32)
    skip = dot_nt(up_skip_ref[...], shortcut_ref[own, :])
    mask = widen(mask_ref, back.shape[1])
    planes = [back[:rows] + skip] + [back[at * rows : (at + 1) * rows] for at in range(1, 4)]
    planes = [(plane * mask).astype(bf16) for plane in planes]
    size = 4 * grid
    target = lax.broadcasted_iota(jnp.int32, (size, size), 1)
    source = lax.broadcasted_iota(jnp.int32, (size, size), 0)
    place = jnp.where(source == pixel_of(target, grid, width), 1.0, 0.0).astype(bf16)
    for n in range(imgs):
        ordered = jnp.concatenate([plane[n * grid : (n + 1) * grid] for plane in planes], axis=0)
        out_ref[n] = dot(place, ordered).astype(bf16)


def turn(value):
    return value.astype(f32).T.astype(bf16)


def put_parts(outs, start, total_ref, far_at):
    size = total_ref.shape[0] // len(outs)
    for b, out in enumerate(outs):
        first = pl.multiple_of((far_at ^ b) * size, size)
        out[start : start + size, :] = total_ref[pl.ds(first, size), :].astype(bf16)
    return start + size


def put_tap_parts(outs, start, total_ref, far_at):
    size = total_ref.shape[1] // len(outs)
    for b, out in enumerate(outs):
        first = pl.multiple_of((far_at ^ b) * size, size)
        for tap in range(9):
            at = start + tap * size
            out[at : at + size, :] = total_ref[tap, pl.ds(first, size), :].astype(bf16)
    return start + 9 * size


def add_into(ref, at, part, block):
    ref[at] = part if block == 0 else ref[at] + part


def weight_top_kernel(grid, width, near, far, core_ref, near_at_ref, own_ref, other_ref, *refs):
    up_six, up_five = refs[:near], refs[near : 2 * near]
    out_ref, dense_ref, taps_ref = refs[2 * near :]
    rows = up_six[0].shape[0]
    depth = own_ref.shape[1] // 2
    near_at = near_at_ref[0]
    share = taps_ref.shape[1]
    lane = pl.multiple_of((near_at & 1) * share, share)
    for half, act_ref in zip(halves(None, core_ref[0], depth), (own_ref, other_ref)):
        for block in range(near):
            first = pl.multiple_of((near_at ^ block) * rows, rows)
            add_into(dense_ref, half, dot(turn(act_ref[pl.ds(first, rows), depth:]), up_six[block][...]), block)
    for block in range(near):
        at = (pl.ds(pl.multiple_of((near_at ^ block) * rows, rows), rows), pl.ds(lane, share))
        act = jnp.where(core_ref[0] == (near_at >> 1), own_ref[at].astype(f32), other_ref[at].astype(f32))
        turned = act.T.astype(bf16)
        moved = moved_grads(up_five[block][...], (-1, 0, 1), (-1, 0, 1), width, grid)
        for r in range(3):
            for s in range(3):
                add_into(taps_ref, 3 * r + s, dot(turned, moved[1 - r, 1 - s]), block)
    start = 0
    for owner in range(far):
        size = dense_ref.shape[0] // far
        out_ref[start : start + size, :] = dense_ref[owner * size : (owner + 1) * size, :].astype(bf16)
        start += size
        size = taps_ref.shape[1] // far
        for tap in range(9):
            out_ref[start : start + size, :] = taps_ref[tap, owner * size : (owner + 1) * size, :].astype(bf16)
            start += size


def weight_four_kernel(near, core_ref, near_at_ref, own_ref, other_ref, up_ref, *refs):
    outs, sum_ref = refs[:near], refs[near]
    own, other = halves(None, core_ref[0], own_ref.shape[1])
    sum_ref[own, :] = dot(turn(own_ref[...]), up_ref[...])
    sum_ref[other, :] = dot(turn(other_ref[...]), up_ref[...])
    put_parts(outs, 0, sum_ref, near_at_ref[0])


def weight_bottom_kernel(near, far, split, core_ref, near_at_ref, far_at_ref, own_ref, other_ref, *refs):
    parts, up_join = refs[:near], refs[near : 2 * near]
    outs, (reduce_ref, expand_ref, shortcut_ref) = refs[2 * near : 2 * near + far], refs[2 * near + far :]
    rows, lanes = up_join[0].shape[0], up_join[0].shape[1] // 2
    depth = own_ref.shape[1] - split
    reduce_ref[...] = functools.reduce(jnp.add, [part[...].astype(f32) for part in parts])
    for half, act_ref in zip(halves(None, core_ref[0], split), (own_ref, other_ref)):
        for block in range(near):
            first = pl.multiple_of((near_at_ref[0] ^ block) * rows, rows)
            turned = turn(act_ref[pl.ds(first, rows), :])
            add_into(shortcut_ref, half, dot(turned[:split], up_join[block][:, lanes:]), block)
    for half, act_ref in zip(halves(None, core_ref[0], depth), (own_ref, other_ref)):
        for block in range(near):
            first = pl.multiple_of((near_at_ref[0] ^ block) * rows, rows)
            turned = turn(act_ref[pl.ds(first, rows), split:])
            add_into(expand_ref, half, dot(turned, up_join[block][:, :lanes]), block)
    start = put_parts(outs, 0, reduce_ref, far_at_ref[0])
    start = put_parts(outs, start, expand_ref, far_at_ref[0])
    put_parts(outs, start, shortcut_ref, far_at_ref[0])


def weight_two_kernel(grid, width, near, far, near_at_ref, far_at_ref, act_ref, *refs):
    ups, outs, taps_ref = refs[:near], refs[near : near + far], refs[near + far]
    rows = ups[0].shape[0]
    for block in range(near):
        moved = moved_grads(ups[block][...], (0, 1), (0, 1), width, grid)
        for plane in range(4):
            first = pl.multiple_of((near_at_ref[0] ^ block) * (4 * rows) + plane * rows, rows)
            turned = turn(act_ref[pl.ds(first, rows), :])
            for r in ((1,) if plane < 2 else (0, 2)):
                for s in ((1,) if plane % 2 == 0 else (0, 2)):
                    add_into(taps_ref, 3 * r + s, dot(turned, moved[int(r == 0), int(s == 0)]), block)
    put_tap_parts(outs, 0, taps_ref, far_at_ref[0])


def weight_one_kernel(near, core_ref, near_at_ref, own_ref, other_ref, up_ref, *refs):
    outs, sum_ref = refs[:near], refs[near]
    own, other = halves(None, core_ref[0], own_ref.shape[1])
    sum_ref[own, :] = dot(turn(own_ref[...]), up_ref[...])
    sum_ref[other, :] = dot(turn(other_ref[...]), up_ref[...])
    put_parts(outs, 0, sum_ref, near_at_ref[0])


def solution(mesh):
    count = mesh.shape["dp"]
    near = 4
    far = count // near
    def to_near(pieces):
        return [pieces[0]] + [send(pieces[b], count, b) for b in range(1, near)]

    def to_far(pieces):
        return [pieces[0]] + [send(pieces[b].astype(bf16), count, b * near) for b in range(1, far)]

    def tell_far(value):
        return [value] + [send(value, count, b * near) for b in range(1, far)]

    far_groups = [[at * near + b for at in range(far)] for b in range(near)]
    near_groups = [[at * near + b for b in range(near)] for at in range(far)]

    def gather_near(value):
        return lax.all_gather(value, "dp", axis=0, tiled=True, axis_index_groups=near_groups)

    def tell_near_first(value):
        rows = value.shape[0] // 2
        first, second = value[:rows], value[rows:]
        return [first, send(first, count, 1), second, send(second, count, 2)]

    def tell_near_then(halves_of):
        first = jnp.concatenate(halves_of[:2])
        second = jnp.concatenate(halves_of[2:])
        return [first, send(first, count, 2), second, send(second, count, 1)]

    def told_chunks(rows):
        half = far // 2
        out = []
        for which, members in enumerate([(0, 1), (2, 3), (0, 2), (1, 3)]):
            for at, member in enumerate(members):
                for b in range(half):
                    out.append((which, (at * half + b) * (rows // far), member, True, (which // 2) * half + b))
        return out

    def total(pieces):
        return functools.reduce(jnp.add, [piece.astype(f32) for piece in pieces])

    def local(images, extents, cotangent, reduce1, spatial1, expand1, shortcut, reduce2, spatial2, expand2,
              norm_one, norm_two, norm_three, norm_skip, norm_four, norm_five, norm_six):
        core = lax.axis_index("chan")
        place = lax.axis_index("dp")
        near_at, far_at = place % near, place // near
        near_order = [near_at ^ b for b in range(near)]
        far_order = [far_at ^ b for b in range(far)]
        imgs, height, width = cotangent.shape[:3]
        grid = height * width
        outer = imgs * grid
        cid = images.shape[3]
        mid = reduce1.shape[1]
        wide = cotangent.shape[3]
        share = 2 * mid // near
        near_place = near_at.reshape(1).astype(jnp.int32)
        far_place = far_at.reshape(1).astype(jnp.int32)
        core_at = core.reshape(1).astype(jnp.int32)

        cell = lax.broadcasted_iota(jnp.int32, (imgs, grid), 1)
        valid = (cell // width < extents[:, 0:1]) & (cell % width < extents[:, 1:2])
        mask = jnp.broadcast_to(valid.astype(f32).reshape(outer, 1), (outer, 128))
        cells = jnp.sum(extents[:, 0] * extents[:, 1]).astype(f32).reshape(1)

        def gridded(body):
            return functools.partial(body, grid, width)

        def spread(local_sums, both):
            return lax.all_to_all(local_sums, ("dp", "chan") if both else "dp", 0, 0, tiled=True)

        first_sums = ((2 * count, 4, mid), f32)
        narrow_sums = ((2 * count, 2, mid), f32)
        own_sums = ((2 * count, 2, mid), f32)
        wide_sums = ((count, 2, wide), f32)
        join_sums = ((count, 4, wide), f32)
        all_cells_out = ((count, 128), f32)
        narrow_moments = ((8, mid), f32)
        wide_moments = ((8, wide), f32)
        inner = 4 * outer

        norms = jnp.concatenate([norm_one, norm_two, norm_four, norm_five])
        norms = in_order(core, norms, swap(norms))
        both_one, both_two, both_four, both_five = norms[0:2], norms[2:4], norms[4:6], norms[6:8]

        own_x, = run_kernel(gridded(sort_kernel), [((inner, cid), bf16)], [],
                            [images.reshape(imgs, 4 * grid, cid), mask], flops=2 * imgs * 16 * grid * grid * cid, held=(1,))
        other_x = swap(own_x)
        conv_one, sums = run_kernel(conv_one_kernel, [((inner, mid), f32), first_sums], [core_at, cells],
                                    [own_x, other_x, reduce1, mask], flops=4 * inner * cid * mid, held=(2, 3,))
        got = spread(sums, True)
        other_one = swap(conv_one)
        conv_skip, skip_stats = run_kernel(conv_skip_kernel, [((outer, wide), f32), ((2, wide), f32)], [core_at, cells],
                                           [own_x, other_x, shortcut, mask], flops=4 * outer * cid * wide, held=(2, 3,))
        act_one, conv_two, sums, moments_one, all_cells = run_kernel(
            gridded(conv_two_kernel),
            [((inner, 2 * mid), bf16), ((outer, mid), f32), narrow_sums, narrow_moments, all_cells_out], [core_at, cells],
            [got, conv_one, other_one, both_one, mask, spatial1], flops=36 * outer * mid * mid,
            scratch=[pltpu.VMEM((inner, 2 * mid), f32)], held=(0, 4, 5,))
        got = spread(sums, True)
        other_two = swap(conv_two)
        near_one = gather_near(slot(act_one, core, mid, 1))
        act_two, conv_three, sums, moments_two = run_kernel(
            expand_kernel, [((outer, 2 * mid), bf16), ((outer, wide), f32), join_sums, narrow_moments], [core_at, cells],
            [got, all_cells, conv_two, other_two, both_two, mask, expand1, skip_stats], flops=4 * outer * mid * wide,
            scratch=[pltpu.VMEM((outer, 2 * mid), f32)], held=(0, 1, 5, 6,))
        (own_x, act_two), sums = tie((own_x, act_two), sums)
        got = spread(sums, False)
        own_two = slot(act_two, core, mid, 1)
        skip_two = jnp.concatenate([own_x[:outer], own_two], axis=1)
        skip_two, got = tie(skip_two, got)
        near_skip = gather_near(skip_two)
        block_one, moments_three, moments_skip = run_kernel(
            join_kernel, [((outer, wide), bf16), wide_moments, wide_moments], [],
            [got, all_cells, conv_three, conv_skip, norm_three, norm_skip, mask], flops=20 * outer * wide, held=(0, 1, 6,))
        other_block = swap(block_one)
        conv_four, sums = run_kernel(conv_four_kernel, [((outer, mid), f32), narrow_sums], [core_at, cells],
                                     [block_one, other_block, reduce2, mask], flops=4 * outer * wide * mid, held=(2, 3,))
        near_one, sums = tie(near_one, sums)
        got = spread(sums, True)
        other_four = swap(conv_four)
        act_four, conv_five, sums, moments_four = run_kernel(
            gridded(conv_five_kernel),
            [((outer, 2 * mid), bf16), ((outer, mid), f32), narrow_sums, narrow_moments], [core_at, cells],
            [got, all_cells, conv_four, other_four, both_four, mask, spatial2], flops=36 * outer * mid * mid,
            scratch=[pltpu.VMEM((outer, 2 * mid), f32)], held=(0, 1, 5, 6,))
        got = spread(sums, True)
        other_five = swap(conv_five)
        act_five, conv_six, sums, moments_five = run_kernel(
            expand_kernel, [((outer, 2 * mid), bf16), ((outer, wide), f32), wide_sums, narrow_moments], [core_at, cells],
            [got, all_cells, conv_five, other_five, both_five, mask, expand2], flops=4 * outer * mid * wide,
            scratch=[pltpu.VMEM((outer, 2 * mid), f32)], held=(0, 1, 5, 6,))
        near_skip, got = tie(near_skip, spread(sums, False))
        near_act = gather_near(jnp.concatenate([slot(act_four, core, mid, 1), slot(act_five, core, mid, 1)], axis=1))
        block_two, grad_join2, sums, moments_six = run_kernel(
            top_kernel, [((outer, wide), bf16), ((outer, wide), f32), wide_sums, wide_moments], [],
            [got, all_cells, conv_six, block_one, cotangent.reshape(outer, wide), norm_six, mask], flops=30 * outer * wide, held=(0, 1, 6,))
        near_one, sums = tie(near_one, sums)
        got = spread(sums, False)
        own_one = slot(near_one, near_at % 2, share, 1)
        own_one, got = tie(own_one, got)
        other_one = swap(own_one)

        norm_out = ((2, mid), f32)
        wide_norm_out = ((2, wide), f32)
        grad_six, norm_six_grad, part = run_kernel(
            functools.partial(back_dense_kernel, False), [((outer, wide), bf16), wide_norm_out, ((outer, mid), bf16)], [core_at],
            [got, grad_join2, conv_six, moments_six, norm_six, mask, expand2], flops=2 * outer * wide * mid, held=(0, 5, 6,))
        part = swap(part)
        grad_pre, sums = run_kernel(
            own_dense_kernel, [((outer, mid), f32), own_sums], [core_at],
            [grad_six, part, expand2, conv_five, moments_five, norm_five, mask], flops=2 * outer * wide * mid, held=(1, 2, 6,))
        grad_six, sums = tie(grad_six, sums)
        (near_act, own_one, other_one), sums = tie((near_act, own_one, other_one), sums)
        got = spread(sums, True)
        up_six = to_near([slot(grad_six, at, mid, 1) for at in near_order])
        other_near_act = swap(near_act)
        near_one = jnp.where(core == near_at // 2, own_one, other_one)
        (up_six, near_one, other_near_act), got = tie((up_six, near_one, other_near_act), got)

        grad_five, norm_five_grad, part = run_kernel(
            gridded(back_five_kernel), [((outer, mid), bf16), norm_out, ((outer, mid), bf16)], [core_at],
            [got, grad_pre, conv_five, moments_five, norm_five, mask, spatial2], flops=18 * outer * mid * mid, held=(0, 5, 6,))
        part = swap(part)
        up_five = to_near([grad_five] * near)
        grad_pre, sums = run_kernel(
            gridded(own_five_kernel), [((outer, mid), f32), own_sums], [core_at],
            [grad_five, part, spatial2, conv_four, moments_four, norm_four, mask], flops=18 * outer * mid * mid, held=(1, 2, 6,))
        up_five, sums = tie(up_five, sums)
        got = spread(sums, True)
        rows_a = 2 * mid + 9 * share
        top_part, = run_kernel(
            functools.partial(weight_top_kernel, grid, width, near, far), [((rows_a, mid), bf16)], [core_at, near_place],
            [near_act, other_near_act, *up_six, *up_five],
            scratch=[pltpu.VMEM((2 * mid, mid), f32), pltpu.VMEM((9, share, mid), f32)])
        (top_part, near_skip), got = tie((top_part, near_skip), got)
        top_rows = lax.psum_scatter(top_part, "dp", scatter_dimension=0, tiled=True, axis_index_groups=far_groups)
        other_near_skip = swap(near_skip)

        grad_four, norm_four_grad, part = run_kernel(
            functools.partial(back_dense_kernel, True), [((outer, mid), bf16), norm_out, ((outer, wide), bf16)], [core_at],
            [got, grad_pre, conv_four, moments_four, norm_four, mask, reduce2], flops=2 * outer * wide * mid, held=(0, 5, 6,))
        part = swap(part)
        grad_join1, sums = run_kernel(
            own_four_kernel, [((outer, wide), f32), join_sums], [core_at],
            [grad_four, part, reduce2, grad_join2, conv_three, moments_three, norm_three, conv_skip, moments_skip, norm_skip,
             mask], flops=2 * outer * wide * mid, held=(1, 2, 10,))
        (grad_four, other_near_skip), sums = tie((grad_four, other_near_skip), sums)
        got = spread(sums, False)
        reduce2_parts = run_kernel(
            functools.partial(weight_four_kernel, near), [((2 * mid, mid), bf16)] * near, [core_at, near_place],
            [block_one, other_block, grad_four], flops=4 * outer * wide * mid, scratch=[pltpu.VMEM((2 * wide, mid), f32)])
        reduce2_parts = to_near(reduce2_parts)

        top_rows, got = tie(top_rows, got)
        grad_three, grad_skip, norm_three_grad, norm_skip_grad, part = run_kernel(
            back_join_kernel,
            [((outer, wide), bf16), ((outer, wide), bf16), wide_norm_out, wide_norm_out, ((outer, mid), bf16)], [core_at],
            [got, grad_join1, conv_three, moments_three, norm_three, conv_skip, moments_skip, norm_skip, mask, expand1],
            flops=2 * outer * wide * mid, held=(0, 8, 9,))
        reduce2_parts, part = tie(reduce2_parts, swap(part))
        grad_pre, sums = run_kernel(
            own_dense_kernel, [((outer, mid), f32), own_sums], [core_at],
            [grad_three, part, expand1, conv_two, moments_two, norm_two, mask], flops=2 * outer * wide * mid, held=(1, 2, 6,))
        top_rows, sums = tie(top_rows, sums)
        got = spread(sums, True)
        up_join = to_near([
            jnp.concatenate([slot(grad_three, at, mid, 1), slot(grad_skip, at, mid, 1)], axis=1) for at in near_order])

        rows_b = (4 * mid + 2 * cid) // far
        bucket_b = run_kernel(
            functools.partial(weight_bottom_kernel, near, far, cid), [((rows_b, mid), bf16)] * far,
            [core_at, near_place, far_place], [near_skip, other_near_skip, *reduce2_parts, *up_join],
            flops=2 * near * outer * (4 * mid + 2 * cid) * mid,
            scratch=[pltpu.VMEM((2 * mid, mid), f32), pltpu.VMEM((2 * mid, mid), f32), pltpu.VMEM((2 * cid, mid), f32)])
        top_rows = tell_far(top_rows)
        top_rows, got = tie(top_rows, got)
        top_all = gather_near(jnp.concatenate(top_rows))
        bucket_b, got = tie(bucket_b, got)
        bucket_b = to_far(bucket_b)

        grad_two, norm_two_grad, part = run_kernel(
            gridded(back_two_kernel), [((outer, mid), bf16), norm_out, ((inner, mid), bf16)], [core_at],
            [got, grad_pre, conv_two, moments_two, norm_two, mask, spatial1], flops=18 * outer * mid * mid, held=(0, 5, 6,))
        part = swap(part)
        up_two = to_near([grad_two] * near)
        grad_pre, sums = run_kernel(
            gridded(own_two_kernel), [((inner, mid), f32), own_sums], [core_at],
            [grad_two, part, spatial1, conv_one, moments_one, norm_one, mask], flops=18 * outer * mid * mid, held=(1, 2, 6,))
        (up_two, bucket_b[3]), sums = tie((up_two, bucket_b[3]), sums)
        got = spread(sums, True)
        bucket_c = run_kernel(
            functools.partial(weight_two_kernel, grid, width, near, far), [((9 * share // far, mid), bf16)] * far,
            [near_place, far_place], [near_one, *up_two], flops=18 * near * outer * share * mid,
            scratch=[pltpu.VMEM((9, share, mid), f32)])
        (bucket_c, bucket_b), got = tie((bucket_c, bucket_b), got)
        bucket_b = tell_far(total(bucket_b).astype(bf16))

        grad_one, norm_one_grad, part = run_kernel(
            back_one_kernel, [((inner, mid), bf16), norm_out, ((inner, cid), bf16)], [core_at],
            [got, grad_pre, conv_one, moments_one, norm_one, mask, reduce1, grad_skip, shortcut],
            flops=2 * inner * mid * cid, held=(0, 5, 6, 8,))
        part = swap(part)
        reduce1_parts = run_kernel(
            functools.partial(weight_one_kernel, near), [((2 * cid // near, mid), bf16)] * near, [core_at, near_place],
            [own_x, other_x, grad_one], flops=4 * inner * cid * mid, scratch=[pltpu.VMEM((2 * cid, mid), f32)])
        bucket_b[far // 2 + 1 :], reduce1_parts = tie(bucket_b[far // 2 + 1 :], reduce1_parts)
        reduce1_parts = to_near(reduce1_parts)
        reduce1_rows = total(reduce1_parts).astype(bf16)
        bucket_c = [jnp.concatenate([piece, slot(reduce1_rows, at, reduce1_rows.shape[0] // far, 0)])
                    for piece, at in zip(bucket_c, far_order)]
        bucket_b, bucket_c = tie(bucket_b, bucket_c)
        bucket_b = jnp.concatenate(bucket_b)
        rows_b = bucket_b.shape[0]
        bucket_b = tell_near_first(bucket_b)
        bucket_c = to_far(bucket_c)
        bucket_b, bucket_c = tie(bucket_b, bucket_c)
        def lay(arrays, chunks, layouts):
            return laid_out(arrays, chunks, near, far, near_at, far_at, layouts)

        kernel_dims = (3, 3, 2 * mid, mid)
        wide_dims = (2 * mid, 4 * mid)
        chunk = rows_a // far
        top_chunks = [(0, (member * far + b) * chunk, member, False, b) for member in range(near) for b in range(far)]
        expand2_grad, spatial2_grad = lay([top_all], top_chunks, [("columns", wide_dims), ("kernel", kernel_dims)])
        input_grad, = run_kernel(
            gridded(own_x_kernel), [((imgs, 4 * grid, cid), bf16)], [core_at],
            [grad_one, part, reduce1, grad_skip, shortcut, mask], flops=4 * inner * mid * cid, held=(1, 2, 4, 5,))
        bucket_b, sums_c = tie(bucket_b, total(bucket_c).astype(bf16))
        bucket_c = tell_far(sums_c)
        bucket_b = tell_near_then(bucket_b)
        (bucket_b, expand2_grad, spatial2_grad, input_grad), bucket_c = tie(
            (bucket_b, expand2_grad, spatial2_grad, input_grad), bucket_c)
        bucket_c = jnp.concatenate(bucket_c)
        rows_c = bucket_c.shape[0]
        bucket_c = tell_near_first(bucket_c)
        reduce2_grad, expand1_grad, shortcut_grad = lay(
            bucket_b, told_chunks(rows_b),
            [("rows", reduce2.shape), ("columns", wide_dims), ("columns", shortcut.shape)])
        (reduce2_grad, expand1_grad, shortcut_grad), bucket_c = tie((reduce2_grad, expand1_grad, shortcut_grad), bucket_c)
        bucket_c = tell_near_then(bucket_c)
        spatial1_grad, reduce1_grad = lay(
            bucket_c, told_chunks(rows_c), [("kernel", kernel_dims), ("rows", reduce1.shape)])
        grads = (reduce1_grad, spatial1_grad, expand1_grad, shortcut_grad, reduce2_grad, spatial2_grad, expand2_grad)
        return (block_one.reshape(cotangent.shape), block_two.reshape(cotangent.shape), input_grad.reshape(images.shape),
                *grads, norm_one_grad, norm_two_grad, norm_three_grad, norm_skip_grad, norm_four_grad, norm_five_grad,
                norm_six_grad)

    pixels = P("dp", None, None, "chan")
    weights = (P(None, "chan"), P(None, None, None, "chan")) + (P(None, "chan"),) * 3 + (P(None, None, None, "chan"), P(None, "chan"))
    norms = (P(None, "chan"),) * 7
    return jax.shard_map(
        local, mesh=mesh,
        in_specs=(pixels, P("dp", None), pixels) + weights + norms,
        out_specs=(pixels, pixels, pixels) + weights + norms,
        check_vma=False)
```

```python
import functools
import math

import jax
import jax.numpy as jnp
from jax import lax
from jax.experimental import pallas as pl
from jax.experimental.pallas import tpu as pltpu
from jax.sharding import PartitionSpec as P

epsilon = 1e-05
f32 = jnp.float32
bf16 = jnp.bfloat16
SWAP = [(0, 1), (1, 0)]


def swap(value):
    return lax.ppermute(value, "chan", SWAP)


def in_order(core, own, other, axis=-1):
    return jnp.where(
        core == 0,
        jnp.concatenate([own, other], axis),
        jnp.concatenate([other, own], axis),
    )


def tie(early, late):
    return lax.optimization_barrier((early, late))


def send(value, count, bits):
    return lax.ppermute(value, "dp", [(at, at ^ bits) for at in range(count)])


def slot(value, index, size, axis):
    return lax.dynamic_slice_in_dim(value, index * size, size, axis)


def lay_kernel(near, far, layouts, chunks, at_ref, *refs):
    ins, outs = refs[: len(refs) - len(layouts)], refs[len(refs) - len(layouts) :]
    near_at, far_at = at_ref[0], at_ref[1]
    for which, start, member, relative, b in chunks:
        owner = far_at ^ b
        if relative:
            member = near_at ^ member
        for (kind, dims), out in zip(layouts, outs):
            if kind == "kernel":
                size = dims[2] // near // far
                for tap in range(9):
                    first = pl.multiple_of(member * (size * far) + owner * size, size)
                    out[tap // 3, tap % 3, pl.ds(first, size), :] = ins[which][start : start + size, :].astype(f32)
                    start += size
            elif kind == "rows":
                size = dims[0] // near // far
                first = pl.multiple_of(member * (size * far) + owner * size, size)
                out[pl.ds(first, size), :] = ins[which][start : start + size, :].astype(f32)
                start += size
            else:
                size, lanes = dims[0] // far, dims[1] // near
                first = pl.multiple_of(owner * size, size)
                lane = pl.multiple_of(member * lanes, lanes)
                out[pl.ds(first, size), pl.ds(lane, lanes)] = ins[which][start : start + size, :].astype(f32)
                start += size


def laid_out(arrays, chunks, near, far, near_at, far_at, layouts):
    return pl.pallas_call(
        functools.partial(lay_kernel, near, far, layouts, chunks),
        out_shape=[jax.ShapeDtypeStruct(dims, f32) for _, dims in layouts],
        in_specs=[pl.BlockSpec(memory_space=pltpu.SMEM)] + [pl.BlockSpec(memory_space=pltpu.VMEM)] * len(arrays),
        out_specs=[pl.BlockSpec(memory_space=pltpu.VMEM)] * len(layouts),
        compiler_params=pltpu.CompilerParams(vmem_limit_bytes=40 * 2**20),
    )(jnp.stack([near_at, far_at]).astype(jnp.int32), *arrays)


def spec(kind):
    return pl.BlockSpec(memory_space=kind)


def staged(body, scalars, ins, outs, held, *refs):
    head, refs = refs[:scalars], refs[scalars:]
    given, results, refs = refs[:ins], refs[ins : ins + outs], refs[ins + outs :]
    moved = [at for at in range(ins) if at not in held]
    here, made, extra = refs[: len(moved)], refs[len(moved) : len(moved) + outs], refs[len(moved) + outs : -2]
    in_sems, out_sems = refs[-2:]
    arrivals = [pltpu.make_async_copy(given[at], here[k], in_sems.at[k]) for k, at in enumerate(moved)]
    for copy in arrivals:
        copy.start()
    for copy in arrivals:
        copy.wait()
    local = dict(zip(moved, here))
    body(*head, *[local.get(at, given[at]) for at in range(ins)], *made, *extra)
    leaving = [pltpu.make_async_copy(made[at], results[at], out_sems.at[at]) for at in range(outs)]
    for copy in leaving:
        copy.start()
    for copy in leaving:
        copy.wait()


def run_kernel(body, outs, scalars, arrays, flops=0, scratch=(), held=()):
    return pl.pallas_call(
        functools.partial(staged, body, len(scalars), len(arrays), len(outs), held),
        out_shape=[pltpu.HBM(shape, dtype) for shape, dtype in outs],
        in_specs=[spec(pltpu.SMEM)] * len(scalars)
        + [spec(pltpu.VMEM if at in held else pltpu.HBM) for at in range(len(arrays))],
        out_specs=[spec(pltpu.HBM)] * len(outs),
        scratch_shapes=[pltpu.VMEM(x.shape, x.dtype) for at, x in enumerate(arrays) if at not in held]
        + [pltpu.VMEM(shape, dtype) for shape, dtype in outs]
        + list(scratch) + [pltpu.SemaphoreType.DMA((len(arrays),)), pltpu.SemaphoreType.DMA((len(outs),))],
        cost_estimate=pl.CostEstimate(flops=1, bytes_accessed=1, transcendentals=0),
        compiler_params=pltpu.CompilerParams(vmem_limit_bytes=28 * 2**20),
    )(*scalars, *[x if at in held else pltpu.with_memory_space_constraint(x, pltpu.HBM) for at, x in enumerate(arrays)])


def widen(mask_ref, lanes):
    mask = mask_ref[...]
    return mask if lanes == 128 else jnp.concatenate([mask] * (lanes // 128), axis=1)


def dot(left, right):
    return lax.dot_general(left, right, (((1,), (0,)), ((), ())), preferred_element_type=f32)


def dot_nt(left, right):
    return lax.dot_general(left, right, (((1,), (1,)), ((), ())), preferred_element_type=f32)


def halves(ref, core, size):
    own = pl.ds(pl.multiple_of(core * size, size), size)
    other = pl.ds(pl.multiple_of((1 - core) * size, size), size)
    return own, other


def stats(values, mask, cells):
    total = jnp.sum(values * mask, axis=0, keepdims=True)
    centred = (values - total / cells) * mask
    return [total, jnp.sum(centred * centred, axis=0, keepdims=True)]


def put_rows(out_ref, rows):
    tile = jnp.concatenate(rows, axis=0)
    for at in range(out_ref.shape[0]):
        out_ref[at] = tile


def moments(tiles, cells_ref, scale=1.0, first=0):
    lanes = tiles[0].shape[1]
    cells = jnp.concatenate([cells_ref[...]] * (lanes // 128), axis=1) * scale
    pixels = jnp.sum(cells, axis=0, keepdims=True)
    totals = [tile[first : first + 1] for tile in tiles]
    mean = functools.reduce(jnp.add, totals) / pixels
    spread = functools.reduce(jnp.add, [tile[first + 1 : first + 2] for tile in tiles])
    offsets = jnp.concatenate(totals, axis=0) / cells - mean
    spread = spread + jnp.sum(cells * offsets * offsets, axis=0, keepdims=True)
    return mean, lax.rsqrt(spread / pixels + epsilon), pixels


def put_moments(out_ref, mean, inverse, pixels):
    lanes = mean.shape[1]
    out_ref[...] = jnp.concatenate([mean, inverse, pixels, jnp.zeros((5, lanes), f32)], axis=0)


def silu_slope(values):
    logistic = jax.nn.sigmoid(values)
    return logistic * (1.0 + values * (1.0 - logistic))


def shift_cols(values, by, width):
    rows = values.shape[0]
    column = lax.broadcasted_iota(jnp.int32, values.shape, 0) & (width - 1)
    moved = pltpu.roll(values, (-by) % rows, 0)
    return jnp.where(column == (0 if by < 0 else width - 1), 0.0, moved)


def shift_rows(values, by, width, grid):
    if by == 0:
        return values
    zeros = jnp.zeros((width, values.shape[1]), values.dtype)
    out = []
    for start in range(0, values.shape[0], grid):
        if by < 0:
            out += [zeros, values[start : start + grid - width]]
        else:
            out += [values[start + width : start + grid], zeros]
    return jnp.concatenate(out, axis=0)


def pixel_of(index, grid, width):
    plane = jnp.zeros_like(index)
    for at in range(1, 4):
        plane = plane + (index >= at * grid).astype(jnp.int32)
    inside = index - plane * grid
    line = inside >> (width.bit_length() - 1)
    column = inside & (width - 1)
    return (2 * line + (plane >> 1)) * (2 * width) + 2 * column + (plane & 1)


def sort_kernel(grid, width, images_ref, mask_ref, out_ref):
    size = 4 * grid
    target = lax.broadcasted_iota(jnp.int32, (size, size), 0)
    source = lax.broadcasted_iota(jnp.int32, (size, size), 1)
    pick = jnp.where(source == pixel_of(target, grid, width), 1.0, 0.0).astype(bf16)
    imgs = images_ref.shape[0]
    lanes = images_ref.shape[2]
    mask = widen(mask_ref, lanes)
    for n in range(imgs):
        ordered = dot(pick, images_ref[n])
        for plane in range(4):
            first = (plane * imgs + n) * grid
            rows = ordered[plane * grid : (plane + 1) * grid] * mask[n * grid : (n + 1) * grid]
            out_ref[first : first + grid, :] = rows.astype(bf16)


def conv_one_kernel(core_ref, cells_ref, own_ref, other_ref, weight_ref, mask_ref, out_ref, stats_ref):
    own, other = halves(weight_ref, core_ref[0], own_ref.shape[1])
    values = dot(own_ref[...], weight_ref[own, :]) + dot(other_ref[...], weight_ref[other, :])
    out_ref[...] = values
    mask = widen(mask_ref, values.shape[1])
    cells = jnp.full((1, values.shape[1]), cells_ref[0])
    put_rows(stats_ref, stats(values, jnp.concatenate([mask] * 4, axis=0), 4.0 * cells_ref[0]) + [cells, cells])


def conv_skip_kernel(core_ref, cells_ref, own_ref, other_ref, weight_ref, mask_ref, out_ref, stats_ref):
    rows = mask_ref.shape[0]
    own, other = halves(weight_ref, core_ref[0], own_ref.shape[1])
    values = dot(own_ref[:rows], weight_ref[own, :]) + dot(other_ref[:rows], weight_ref[other, :])
    out_ref[...] = values
    mask = widen(mask_ref, values.shape[1])
    stats_ref[...] = jnp.concatenate(stats(values, mask, cells_ref[0]), axis=0)


def norm_act(got_ref, all_cells_ref, scale, own_ref, other_ref, norm_ref, mask, core, raw_ref, act_ref, moments_ref):
    lanes = own_ref.shape[1]
    own, other = halves(None, core, lanes)
    raw_ref[:, own] = own_ref[...]
    raw_ref[:, other] = other_ref[...]
    count = got_ref.shape[0] // 2
    for half in range(2):
        mean, inverse, pixels = moments([got_ref[2 * at + half] for at in range(count)], all_cells_ref, scale)

        @pl.when(core == half)
        def _():
            put_moments(moments_ref, mean, inverse, pixels)

        at = slice(half * lanes, (half + 1) * lanes)
        pre = norm_ref[0:1, at] * ((raw_ref[:, at] - mean) * inverse) + norm_ref[1:2, at]
        act_ref[:, at] = (pre * jax.nn.sigmoid(pre) * mask).astype(bf16)


def conv_two_kernel(grid, width, core_ref, cells_ref, got_ref, own_ref, other_ref, norm_ref, mask_ref, weight_ref,
                    act_ref, out_ref, stats_ref, moments_ref, all_cells_ref, raw_ref):
    rows = mask_ref.shape[0]
    lanes = own_ref.shape[1]
    mask = widen(mask_ref, lanes)
    for at in range(got_ref.shape[0] // 2):
        all_cells_ref[at : at + 1, :] = got_ref[2 * at, 2:3, :128]
    norm_act(got_ref, all_cells_ref, 4.0, own_ref, other_ref, norm_ref, jnp.concatenate([mask] * 4, axis=0), core_ref[0],
             raw_ref, act_ref, moments_ref)
    values = jnp.zeros((rows, out_ref.shape[1]), f32)
    for plane in range(4):
        here = act_ref[plane * rows : (plane + 1) * rows, :]
        by_col = {1: here} if plane % 2 == 0 else {2: here, 0: shift_cols(here.astype(f32), -1, width).astype(bf16)}
        for s, moved in by_col.items():
            for r in ((1,) if plane < 2 else (0, 2)):
                values = values + dot(shift_rows(moved, -1 if r == 0 else 0, width, grid), weight_ref[r, s])
    out_ref[...] = values
    put_rows(stats_ref, stats(values, mask, cells_ref[0]))


def conv_five_kernel(grid, width, core_ref, cells_ref, got_ref, all_cells_ref, own_ref, other_ref, norm_ref, mask_ref, weight_ref,
                     act_ref, out_ref, stats_ref, moments_ref, raw_ref):
    rows = mask_ref.shape[0]
    mask = widen(mask_ref, own_ref.shape[1])
    norm_act(got_ref, all_cells_ref, 1.0, own_ref, other_ref, norm_ref, mask, core_ref[0], raw_ref, act_ref, moments_ref)
    values = jnp.zeros((rows, out_ref.shape[1]), f32)
    here = act_ref[...]
    for s in range(3):
        moved = here if s == 1 else shift_cols(here.astype(f32), s - 1, width).astype(bf16)
        for r in range(3):
            values = values + dot(shift_rows(moved, r - 1, width, grid), weight_ref[r, s])
    out_ref[...] = values
    put_rows(stats_ref, stats(values, mask, cells_ref[0]))


def expand_kernel(core_ref, cells_ref, got_ref, all_cells_ref, own_ref, other_ref, norm_ref, mask_ref, weight_ref, *refs):
    more_refs, (act_ref, out_ref, stats_ref, moments_ref, raw_ref) = refs[:-5], refs[-5:]
    norm_act(got_ref, all_cells_ref, 1.0, own_ref, other_ref, norm_ref, widen(mask_ref, own_ref.shape[1]), core_ref[0],
             raw_ref, act_ref, moments_ref)
    values = dot(act_ref[...], weight_ref[...])
    out_ref[...] = values
    more = [more_refs[0][...]] if more_refs else []
    put_rows(stats_ref, stats(values, widen(mask_ref, values.shape[1]), cells_ref[0]) + more)


def normed(raw_ref, moments_ref):
    return (raw_ref[...] - moments_ref[0:1]) * moments_ref[1:2]


def scaled(norm_ref, hat):
    return norm_ref[0:1] * hat + norm_ref[1:2]


def join_kernel(got_ref, all_cells_ref, three_ref, skip_ref, norm_three_ref, norm_skip_ref, mask_ref, out_ref, moments_three_ref,
                moments_skip_ref):
    tiles = [got_ref[at] for at in range(got_ref.shape[0])]
    put_moments(moments_three_ref, *moments(tiles, all_cells_ref))
    put_moments(moments_skip_ref, *moments(tiles, all_cells_ref, first=2))
    joined = scaled(norm_three_ref, normed(three_ref, moments_three_ref)) + scaled(
        norm_skip_ref, normed(skip_ref, moments_skip_ref))
    out_ref[...] = (joined * jax.nn.sigmoid(joined) * widen(mask_ref, joined.shape[1])).astype(bf16)


def conv_four_kernel(core_ref, cells_ref, own_ref, other_ref, weight_ref, mask_ref, out_ref, stats_ref):
    own, other = halves(weight_ref, core_ref[0], own_ref.shape[1])
    values = dot(own_ref[...], weight_ref[own, :]) + dot(other_ref[...], weight_ref[other, :])
    out_ref[...] = values
    put_rows(stats_ref, stats(values, widen(mask_ref, values.shape[1]), cells_ref[0]))


def put_sums(out_ref, grad, *hats):
    rows = [jnp.sum(grad, axis=0, keepdims=True)] + [jnp.sum(grad * hat, axis=0, keepdims=True) for hat in hats]
    put_rows(out_ref, rows + [rows[0]] * (out_ref.shape[1] - len(rows)))


def top_kernel(got_ref, all_cells_ref, six_ref, block_ref, cotangent_ref, norm_ref, mask_ref, out_ref, grad_ref, sums_ref, moments_ref):
    put_moments(moments_ref, *moments([got_ref[at] for at in range(got_ref.shape[0])], all_cells_ref))
    hat = normed(six_ref, moments_ref)
    joined = scaled(norm_ref, hat) + block_ref[...].astype(f32)
    mask = widen(mask_ref, joined.shape[1])
    logistic = jax.nn.sigmoid(joined)
    out_ref[...] = (joined * logistic * mask).astype(bf16)
    grad = cotangent_ref[...].astype(f32) * mask * (logistic * (1.0 + joined * (1.0 - logistic)))
    grad_ref[...] = grad
    put_sums(sums_ref, grad, hat)


def sums_of(got_ref, core=None):
    if core is None:
        return functools.reduce(jnp.add, [got_ref[at] for at in range(got_ref.shape[0])])
    return functools.reduce(jnp.add, [got_ref[2 * at + core] for at in range(got_ref.shape[0] // 2)])


def norm_back(grad, hat, moments_ref, norm_ref, beta, gamma, mask):
    inside = grad - (beta + hat * gamma) / moments_ref[2:3]
    return (mask * (norm_ref[0:1] * moments_ref[1:2]) * inside).astype(bf16)


def back_dense_kernel(both, core_ref, got_ref, grad_ref, raw_ref, moments_ref, norm_ref, mask_ref, weight_ref, out_ref,
                    norm_grad_ref, send_ref):
    sums = sums_of(got_ref, core_ref[0] if both else None)
    beta, gamma = sums[0:1], sums[1:2]
    norm_grad_ref[...] = jnp.concatenate([gamma, beta], axis=0)
    grad = norm_back(grad_ref[...], normed(raw_ref, moments_ref), moments_ref, norm_ref, beta, gamma,
                     widen(mask_ref, raw_ref.shape[1]))
    out_ref[...] = grad
    own, other = halves(weight_ref, core_ref[0], weight_ref.shape[0] // 2)
    send_ref[...] = dot_nt(grad, weight_ref[other, :]).astype(bf16)


def own_dense_kernel(core_ref, up_ref, got_ref, weight_ref, raw_ref, moments_ref, norm_ref, mask_ref, out_ref, sums_ref):
    own, other = halves(weight_ref, core_ref[0], weight_ref.shape[0] // 2)
    back = dot_nt(up_ref[...], weight_ref[own, :]) + got_ref[...].astype(f32)
    hat = normed(raw_ref, moments_ref)
    grad = back * widen(mask_ref, raw_ref.shape[1]) * silu_slope(scaled(norm_ref, hat))
    out_ref[...] = grad
    put_sums(sums_ref, grad, hat)


def moved_grads(grad, cols, rows, width, grid):
    wide = grad.astype(f32)
    out = {}
    for col in cols:
        moved = grad if col == 0 else shift_cols(wide, col, width).astype(bf16)
        for row in rows:
            out[row, col] = shift_rows(moved, row, width, grid)
    return out


def back_five_kernel(grid, width, core_ref, got_ref, grad_ref, raw_ref, moments_ref, norm_ref, mask_ref, weight_ref,
                     out_ref, norm_grad_ref, send_ref):
    sums = sums_of(got_ref, core_ref[0])
    beta, gamma = sums[0:1], sums[1:2]
    norm_grad_ref[...] = jnp.concatenate([gamma, beta], axis=0)
    grad = norm_back(grad_ref[...], normed(raw_ref, moments_ref), moments_ref, norm_ref, beta, gamma,
                     widen(mask_ref, raw_ref.shape[1]))
    out_ref[...] = grad
    own, other = halves(weight_ref, core_ref[0], weight_ref.shape[2] // 2)
    moved = moved_grads(grad, (-1, 0, 1), (-1, 0, 1), width, grid)
    back = functools.reduce(
        jnp.add, [dot_nt(moved[1 - r, 1 - s], weight_ref[r, s, other, :]) for r in range(3) for s in range(3)])
    send_ref[...] = back.astype(bf16)


def own_five_kernel(grid, width, core_ref, up_ref, got_ref, weight_ref, raw_ref, moments_ref, norm_ref, mask_ref, out_ref,
                    sums_ref):
    own, other = halves(weight_ref, core_ref[0], weight_ref.shape[2] // 2)
    moved = moved_grads(up_ref[...], (-1, 0, 1), (-1, 0, 1), width, grid)
    back = functools.reduce(
        jnp.add, [dot_nt(moved[1 - r, 1 - s], weight_ref[r, s, own, :]) for r in range(3) for s in range(3)])
    hat = normed(raw_ref, moments_ref)
    grad = (back + got_ref[...].astype(f32)) * widen(mask_ref, raw_ref.shape[1]) * silu_slope(scaled(norm_ref, hat))
    out_ref[...] = grad
    put_sums(sums_ref, grad, hat)


def own_four_kernel(core_ref, up_ref, got_ref, weight_ref, top_ref, three_ref, moments_three_ref, norm_three_ref, skip_ref,
                    moments_skip_ref, norm_skip_ref, mask_ref, out_ref, sums_ref):
    own, other = halves(weight_ref, core_ref[0], weight_ref.shape[0] // 2)
    back = dot_nt(up_ref[...], weight_ref[own, :]) + got_ref[...].astype(f32) + top_ref[...]
    hat_three = normed(three_ref, moments_three_ref)
    hat_skip = normed(skip_ref, moments_skip_ref)
    joined = scaled(norm_three_ref, hat_three) + scaled(norm_skip_ref, hat_skip)
    grad = back * widen(mask_ref, joined.shape[1]) * silu_slope(joined)
    out_ref[...] = grad
    put_sums(sums_ref, grad, hat_three, hat_skip)


def back_join_kernel(core_ref, got_ref, grad_ref, three_ref, moments_three_ref, norm_three_ref, skip_ref, moments_skip_ref,
                     norm_skip_ref, mask_ref, weight_ref, out_three_ref, out_skip_ref, norm_three_grad_ref,
                     norm_skip_grad_ref, send_ref):
    sums = sums_of(got_ref)
    beta, gamma_three, gamma_skip = sums[0:1], sums[1:2], sums[2:3]
    norm_three_grad_ref[...] = jnp.concatenate([gamma_three, beta], axis=0)
    norm_skip_grad_ref[...] = jnp.concatenate([gamma_skip, beta], axis=0)
    mask = widen(mask_ref, three_ref.shape[1])
    grad = norm_back(grad_ref[...], normed(three_ref, moments_three_ref), moments_three_ref, norm_three_ref, beta,
                     gamma_three, mask)
    out_three_ref[...] = grad
    own, other = halves(weight_ref, core_ref[0], weight_ref.shape[0] // 2)
    send_ref[...] = dot_nt(grad, weight_ref[other, :]).astype(bf16)
    out_skip_ref[...] = norm_back(grad_ref[...], normed(skip_ref, moments_skip_ref), moments_skip_ref, norm_skip_ref, beta,
                                  gamma_skip, mask)


def planes_back(moved, weight_ref, at):
    def term(r, s, row, col):
        return dot_nt(moved[row, col], weight_ref[r, s, at, :])

    return [
        term(1, 1, 0, 0),
        term(1, 2, 0, 0) + term(1, 0, 0, 1),
        term(2, 1, 0, 0) + term(0, 1, 1, 0),
        term(2, 2, 0, 0) + term(2, 0, 0, 1) + term(0, 2, 1, 0) + term(0, 0, 1, 1),
    ]


def back_two_kernel(grid, width, core_ref, got_ref, grad_ref, raw_ref, moments_ref, norm_ref, mask_ref, weight_ref, out_ref,
                    norm_grad_ref, send_ref):
    sums = sums_of(got_ref, core_ref[0])
    beta, gamma = sums[0:1], sums[1:2]
    norm_grad_ref[...] = jnp.concatenate([gamma, beta], axis=0)
    grad = norm_back(grad_ref[...], normed(raw_ref, moments_ref), moments_ref, norm_ref, beta, gamma,
                     widen(mask_ref, raw_ref.shape[1]))
    out_ref[...] = grad
    own, other = halves(weight_ref, core_ref[0], weight_ref.shape[2] // 2)
    rows = grad.shape[0]
    for plane, back in enumerate(planes_back(moved_grads(grad, (0, 1), (0, 1), width, grid), weight_ref, other)):
        send_ref[plane * rows : (plane + 1) * rows, :] = back.astype(bf16)


def own_two_kernel(grid, width, core_ref, up_ref, got_ref, weight_ref, raw_ref, moments_ref, norm_ref, mask_ref, out_ref,
                   sums_ref):
    own, other = halves(weight_ref, core_ref[0], weight_ref.shape[2] // 2)
    rows = up_ref.shape[0]
    mask = widen(mask_ref, raw_ref.shape[1])
    beta = jnp.zeros((1, raw_ref.shape[1]), f32)
    gamma = beta
    for plane, back in enumerate(planes_back(moved_grads(up_ref[...], (0, 1), (0, 1), width, grid), weight_ref, own)):
        at = slice(plane * rows, (plane + 1) * rows)
        hat = (raw_ref[at, :] - moments_ref[0:1]) * moments_ref[1:2]
        grad = (back + got_ref[at, :].astype(f32)) * mask * silu_slope(scaled(norm_ref, hat))
        out_ref[at, :] = grad
        beta = beta + jnp.sum(grad, axis=0, keepdims=True)
        gamma = gamma + jnp.sum(grad * hat, axis=0, keepdims=True)
    put_rows(sums_ref, [beta, gamma])


def back_one_kernel(core_ref, near_at_ref, got_ref, grad_ref, raw_ref, moments_ref, norm_ref, mask_ref, weight_ref,
                    up_skip_ref, shortcut_ref, own_x_ref, other_x_ref, out_ref, norm_grad_ref, send_ref, *refs):
    sums = sums_of(got_ref, core_ref[0])
    beta, gamma = sums[0:1], sums[1:2]
    norm_grad_ref[...] = jnp.concatenate([gamma, beta], axis=0)
    mask = jnp.concatenate([widen(mask_ref, raw_ref.shape[1])] * 4, axis=0)
    grad = norm_back(grad_ref[...], normed(raw_ref, moments_ref), moments_ref, norm_ref, beta, gamma, mask)
    out_ref[...] = grad
    own, other = halves(weight_ref, core_ref[0], weight_ref.shape[0] // 2)
    rows = mask_ref.shape[0]
    skip = dot_nt(up_skip_ref[...], shortcut_ref[other, :])
    send_ref[:rows, :] = (dot_nt(grad[:rows], weight_ref[other, :]) + skip).astype(bf16)
    send_ref[rows:, :] = dot_nt(grad[rows:], weight_ref[other, :]).astype(bf16)
    weight_one_kernel(len(refs) - 1, core_ref, near_at_ref, own_x_ref, other_x_ref, out_ref, *refs)


def own_x_kernel(grid, width, core_ref, up_ref, got_ref, weight_ref, up_skip_ref, shortcut_ref, mask_ref, out_ref):
    own, other = halves(weight_ref, core_ref[0], weight_ref.shape[0] // 2)
    rows = mask_ref.shape[0]
    imgs = out_ref.shape[0]
    back = dot_nt(up_ref[...], weight_ref[own, :]) + got_ref[...].astype(f32)
    skip = dot_nt(up_skip_ref[...], shortcut_ref[own, :])
    mask = widen(mask_ref, back.shape[1])
    planes = [back[:rows] + skip] + [back[at * rows : (at + 1) * rows] for at in range(1, 4)]
    planes = [(plane * mask).astype(bf16) for plane in planes]
    size = 4 * grid
    target = lax.broadcasted_iota(jnp.int32, (size, size), 1)
    source = lax.broadcasted_iota(jnp.int32, (size, size), 0)
    place = jnp.where(source == pixel_of(target, grid, width), 1.0, 0.0).astype(bf16)
    for n in range(imgs):
        ordered = jnp.concatenate([plane[n * grid : (n + 1) * grid] for plane in planes], axis=0)
        out_ref[n] = dot(place, ordered).astype(bf16)


def turn(value):
    return value.astype(f32).T.astype(bf16)


def put_parts(outs, start, total_ref, far_at):
    size = total_ref.shape[0] // len(outs)
    for b, out in enumerate(outs):
        first = pl.multiple_of((far_at ^ b) * size, size)
        out[start : start + size, :] = total_ref[pl.ds(first, size), :].astype(bf16)
    return start + size


def put_tap_parts(outs, start, total_ref, far_at):
    size = total_ref.shape[1] // len(outs)
    for b, out in enumerate(outs):
        first = pl.multiple_of((far_at ^ b) * size, size)
        for tap in range(9):
            at = start + tap * size
            out[at : at + size, :] = total_ref[tap, pl.ds(first, size), :].astype(bf16)
    return start + 9 * size


def add_into(ref, at, part, block):
    ref[at] = part if block == 0 else ref[at] + part


def weight_top_kernel(grid, width, near, far, core_ref, near_at_ref, own_ref, other_ref, *refs):
    up_six, up_five = refs[:near], refs[near : 2 * near]
    out_ref, dense_ref, taps_ref = refs[2 * near :]
    rows = up_six[0].shape[0]
    depth = own_ref.shape[1] // 2
    near_at = near_at_ref[0]
    share = taps_ref.shape[1]
    lane = pl.multiple_of((near_at & 1) * share, share)
    for half, act_ref in zip(halves(None, core_ref[0], depth), (own_ref, other_ref)):
        for block in range(near):
            first = pl.multiple_of((near_at ^ block) * rows, rows)
            add_into(dense_ref, half, dot(turn(act_ref[pl.ds(first, rows), depth:]), up_six[block][...]), block)
    for block in range(near):
        at = (pl.ds(pl.multiple_of((near_at ^ block) * rows, rows), rows), pl.ds(lane, share))
        act = jnp.where(core_ref[0] == (near_at >> 1), own_ref[at].astype(f32), other_ref[at].astype(f32))
        turned = act.T.astype(bf16)
        moved = moved_grads(up_five[block][...], (-1, 0, 1), (-1, 0, 1), width, grid)
        for r in range(3):
            for s in range(3):
                add_into(taps_ref, 3 * r + s, dot(turned, moved[1 - r, 1 - s]), block)
    start = 0
    for owner in range(far):
        size = dense_ref.shape[0] // far
        out_ref[start : start + size, :] = dense_ref[owner * size : (owner + 1) * size, :].astype(bf16)
        start += size
        size = taps_ref.shape[1] // far
        for tap in range(9):
            out_ref[start : start + size, :] = taps_ref[tap, owner * size : (owner + 1) * size, :].astype(bf16)
            start += size


def weight_four_kernel(near, core_ref, near_at_ref, own_ref, other_ref, up_ref, *refs):
    outs, sum_ref = refs[:near], refs[near]
    own, other = halves(None, core_ref[0], own_ref.shape[1])
    sum_ref[own, :] = dot(turn(own_ref[...]), up_ref[...])
    sum_ref[other, :] = dot(turn(other_ref[...]), up_ref[...])
    put_parts(outs, 0, sum_ref, near_at_ref[0])


def weight_bottom_kernel(near, far, split, core_ref, near_at_ref, far_at_ref, own_ref, other_ref, *refs):
    parts, up_join = refs[:near], refs[near : 2 * near]
    outs, (reduce_ref, expand_ref, shortcut_ref) = refs[2 * near : 2 * near + far], refs[2 * near + far :]
    rows, lanes = up_join[0].shape[0], up_join[0].shape[1] // 2
    depth = own_ref.shape[1] - split
    reduce_ref[...] = functools.reduce(jnp.add, [part[...].astype(f32) for part in parts])
    for half, act_ref in zip(halves(None, core_ref[0], split), (own_ref, other_ref)):
        for block in range(near):
            first = pl.multiple_of((near_at_ref[0] ^ block) * rows, rows)
            turned = turn(act_ref[pl.ds(first, rows), :])
            add_into(shortcut_ref, half, dot(turned[:split], up_join[block][:, lanes:]), block)
    for half, act_ref in zip(halves(None, core_ref[0], depth), (own_ref, other_ref)):
        for block in range(near):
            first = pl.multiple_of((near_at_ref[0] ^ block) * rows, rows)
            turned = turn(act_ref[pl.ds(first, rows), split:])
            add_into(expand_ref, half, dot(turned, up_join[block][:, :lanes]), block)
    start = put_parts(outs, 0, reduce_ref, far_at_ref[0])
    start = put_parts(outs, start, expand_ref, far_at_ref[0])
    put_parts(outs, start, shortcut_ref, far_at_ref[0])


def weight_two_kernel(grid, width, near, far, near_at_ref, far_at_ref, act_ref, *refs):
    ups, outs, taps_ref = refs[:near], refs[near : near + far], refs[near + far]
    rows = ups[0].shape[0]
    for block in range(near):
        moved = moved_grads(ups[block][...], (0, 1), (0, 1), width, grid)
        for plane in range(4):
            first = pl.multiple_of((near_at_ref[0] ^ block) * (4 * rows) + plane * rows, rows)
            turned = turn(act_ref[pl.ds(first, rows), :])
            for r in ((1,) if plane < 2 else (0, 2)):
                for s in ((1,) if plane % 2 == 0 else (0, 2)):
                    add_into(taps_ref, 3 * r + s, dot(turned, moved[int(r == 0), int(s == 0)]), block)
    put_tap_parts(outs, 0, taps_ref, far_at_ref[0])


def weight_one_kernel(near, core_ref, near_at_ref, own_ref, other_ref, up_ref, *refs):
    outs, sum_ref = refs[:near], refs[near]
    own, other = halves(None, core_ref[0], own_ref.shape[1])
    sum_ref[own, :] = dot(turn(own_ref[...]), up_ref[...])
    sum_ref[other, :] = dot(turn(other_ref[...]), up_ref[...])
    put_parts(outs, 0, sum_ref, near_at_ref[0])


def solution(mesh):
    count = mesh.shape["dp"]
    near = 4
    far = count // near
    def to_near(pieces):
        return [pieces[0]] + [send(pieces[b], count, b) for b in range(1, near)]

    def to_far(pieces):
        return [pieces[0]] + [send(pieces[b].astype(bf16), count, b * near) for b in range(1, far)]

    def tell_far(value):
        return [value] + [send(value, count, b * near) for b in range(1, far)]

    far_groups = [[at * near + b for at in range(far)] for b in range(near)]
    near_groups = [[at * near + b for b in range(near)] for at in range(far)]

    def gather_near(value):
        return lax.all_gather(value, "dp", axis=0, tiled=True, axis_index_groups=near_groups)

    def tell_near_first(value):
        rows = value.shape[0] // 2
        first, second = value[:rows], value[rows:]
        return [first, send(first, count, 1), second, send(second, count, 2)]

    def tell_near_then(halves_of):
        first = jnp.concatenate(halves_of[:2])
        second = jnp.concatenate(halves_of[2:])
        return [first, send(first, count, 2), second, send(second, count, 1)]

    def told_chunks(rows):
        half = far // 2
        out = []
        for which, members in enumerate([(0, 1), (2, 3), (0, 2), (1, 3)]):
            for at, member in enumerate(members):
                for b in range(half):
                    out.append((which, (at * half + b) * (rows // far), member, True, (which // 2) * half + b))
        return out

    def total(pieces):
        return functools.reduce(jnp.add, [piece.astype(f32) for piece in pieces])

    def local(images, extents, cotangent, reduce1, spatial1, expand1, shortcut, reduce2, spatial2, expand2,
              norm_one, norm_two, norm_three, norm_skip, norm_four, norm_five, norm_six):
        core = lax.axis_index("chan")
        place = lax.axis_index("dp")
        near_at, far_at = place % near, place // near
        near_order = [near_at ^ b for b in range(near)]
        far_order = [far_at ^ b for b in range(far)]
        imgs, height, width = cotangent.shape[:3]
        grid = height * width
        outer = imgs * grid
        cid = images.shape[3]
        mid = reduce1.shape[1]
        wide = cotangent.shape[3]
        share = 2 * mid // near
        near_place = near_at.reshape(1).astype(jnp.int32)
        far_place = far_at.reshape(1).astype(jnp.int32)
        core_at = core.reshape(1).astype(jnp.int32)

        cell = lax.broadcasted_iota(jnp.int32, (imgs, grid), 1)
        valid = (cell // width < extents[:, 0:1]) & (cell % width < extents[:, 1:2])
        mask = jnp.broadcast_to(valid.astype(f32).reshape(outer, 1), (outer, 128))
        cells = jnp.sum(extents[:, 0] * extents[:, 1]).astype(f32).reshape(1)

        def gridded(body):
            return functools.partial(body, grid, width)

        def spread(local_sums, both):
            return lax.all_to_all(local_sums, ("dp", "chan") if both else "dp", 0, 0, tiled=True)

        first_sums = ((2 * count, 4, mid), f32)
        narrow_sums = ((2 * count, 2, mid), f32)
        own_sums = ((2 * count, 2, mid), f32)
        wide_sums = ((count, 2, wide), f32)
        join_sums = ((count, 4, wide), f32)
        all_cells_out = ((count, 128), f32)
        narrow_moments = ((8, mid), f32)
        wide_moments = ((8, wide), f32)
        inner = 4 * outer

        norms = jnp.concatenate([norm_one, norm_two, norm_four, norm_five])
        norms = in_order(core, norms, swap(norms))
        both_one, both_two, both_four, both_five = norms[0:2], norms[2:4], norms[4:6], norms[6:8]

        own_x, = run_kernel(gridded(sort_kernel), [((inner, cid), bf16)], [],
                            [images.reshape(imgs, 4 * grid, cid), mask], flops=2 * imgs * 16 * grid * grid * cid, held=(1,))
        other_x = swap(own_x)
        conv_one, sums = run_kernel(conv_one_kernel, [((inner, mid), f32), first_sums], [core_at, cells],
                                    [own_x, other_x, reduce1, mask], flops=4 * inner * cid * mid, held=(2, 3,))
        got = spread(sums, True)
        other_one = swap(conv_one)
        conv_skip, skip_stats = run_kernel(conv_skip_kernel, [((outer, wide), f32), ((2, wide), f32)], [core_at, cells],
                                           [own_x, other_x, shortcut, mask], flops=4 * outer * cid * wide, held=(2, 3,))
        act_one, conv_two, sums, moments_one, all_cells = run_kernel(
            gridded(conv_two_kernel),
            [((inner, 2 * mid), bf16), ((outer, mid), f32), narrow_sums, narrow_moments, all_cells_out], [core_at, cells],
            [got, conv_one, other_one, both_one, mask, spatial1], flops=36 * outer * mid * mid,
            scratch=[pltpu.VMEM((inner, 2 * mid), f32)], held=(0, 4, 5,))
        got = spread(sums, True)
        other_two = swap(conv_two)
        near_one = gather_near(slot(act_one, core, mid, 1))
        act_two, conv_three, sums, moments_two = run_kernel(
            expand_kernel, [((outer, 2 * mid), bf16), ((outer, wide), f32), join_sums, narrow_moments], [core_at, cells],
            [got, all_cells, conv_two, other_two, both_two, mask, expand1, skip_stats], flops=4 * outer * mid * wide,
            scratch=[pltpu.VMEM((outer, 2 * mid), f32)], held=(0, 1, 5, 6,))
        (own_x, act_two), sums = tie((own_x, act_two), sums)
        got = spread(sums, False)
        own_two = slot(act_two, core, mid, 1)
        skip_two = jnp.concatenate([own_x[:outer], own_two], axis=1)
        skip_two, got = tie(skip_two, got)
        near_skip = gather_near(skip_two)
        block_one, moments_three, moments_skip = run_kernel(
            join_kernel, [((outer, wide), bf16), wide_moments, wide_moments], [],
            [got, all_cells, conv_three, conv_skip, norm_three, norm_skip, mask], flops=20 * outer * wide, held=(0, 1, 6,))
        other_block = swap(block_one)
        conv_four, sums = run_kernel(conv_four_kernel, [((outer, mid), f32), narrow_sums], [core_at, cells],
                                     [block_one, other_block, reduce2, mask], flops=4 * outer * wide * mid, held=(2, 3,))
        near_one, sums = tie(near_one, sums)
        got = spread(sums, True)
        other_four = swap(conv_four)
        act_four, conv_five, sums, moments_four = run_kernel(
            gridded(conv_five_kernel),
            [((outer, 2 * mid), bf16), ((outer, mid), f32), narrow_sums, narrow_moments], [core_at, cells],
            [got, all_cells, conv_four, other_four, both_four, mask, spatial2], flops=36 * outer * mid * mid,
            scratch=[pltpu.VMEM((outer, 2 * mid), f32)], held=(0, 1, 5, 6,))
        got = spread(sums, True)
        other_five = swap(conv_five)
        act_five, conv_six, sums, moments_five = run_kernel(
            expand_kernel, [((outer, 2 * mid), bf16), ((outer, wide), f32), wide_sums, narrow_moments], [core_at, cells],
            [got, all_cells, conv_five, other_five, both_five, mask, expand2], flops=4 * outer * mid * wide,
            scratch=[pltpu.VMEM((outer, 2 * mid), f32)], held=(0, 1, 5, 6,))
        near_skip, got = tie(near_skip, spread(sums, False))
        near_act = gather_near(jnp.concatenate([slot(act_four, core, mid, 1), slot(act_five, core, mid, 1)], axis=1))
        block_two, grad_join2, sums, moments_six = run_kernel(
            top_kernel, [((outer, wide), bf16), ((outer, wide), f32), wide_sums, wide_moments], [],
            [got, all_cells, conv_six, block_one, cotangent.reshape(outer, wide), norm_six, mask], flops=30 * outer * wide, held=(0, 1, 6,))
        near_one, sums = tie(near_one, sums)
        got = spread(sums, False)
        own_one = slot(near_one, near_at % 2, share, 1)
        own_one, got = tie(own_one, got)
        other_one = swap(own_one)

        norm_out = ((2, mid), f32)
        wide_norm_out = ((2, wide), f32)
        grad_six, norm_six_grad, part = run_kernel(
            functools.partial(back_dense_kernel, False), [((outer, wide), bf16), wide_norm_out, ((outer, mid), bf16)], [core_at],
            [got, grad_join2, conv_six, moments_six, norm_six, mask, expand2], flops=2 * outer * wide * mid, held=(0, 5, 6,))
        part = swap(part)
        grad_pre, sums = run_kernel(
            own_dense_kernel, [((outer, mid), f32), own_sums], [core_at],
            [grad_six, part, expand2, conv_five, moments_five, norm_five, mask], flops=2 * outer * wide * mid, held=(1, 2, 6,))
        grad_six, sums = tie(grad_six, sums)
        (near_act, own_one, other_one), sums = tie((near_act, own_one, other_one), sums)
        got = spread(sums, True)
        up_six = to_near([slot(grad_six, at, mid, 1) for at in near_order])
        other_near_act = swap(near_act)
        near_one = jnp.where(core == near_at // 2, own_one, other_one)
        (up_six, near_one, other_near_act), got = tie((up_six, near_one, other_near_act), got)

        grad_five, norm_five_grad, part = run_kernel(
            gridded(back_five_kernel), [((outer, mid), bf16), norm_out, ((outer, mid), bf16)], [core_at],
            [got, grad_pre, conv_five, moments_five, norm_five, mask, spatial2], flops=18 * outer * mid * mid, held=(0, 5, 6,))
        part = swap(part)
        up_five = to_near([grad_five] * near)
        grad_pre, sums = run_kernel(
            gridded(own_five_kernel), [((outer, mid), f32), own_sums], [core_at],
            [grad_five, part, spatial2, conv_four, moments_four, norm_four, mask], flops=18 * outer * mid * mid, held=(1, 2, 6,))
        up_five, sums = tie(up_five, sums)
        got = spread(sums, True)
        rows_a = 2 * mid + 9 * share
        top_part, = run_kernel(
            functools.partial(weight_top_kernel, grid, width, near, far), [((rows_a, mid), bf16)], [core_at, near_place],
            [near_act, other_near_act, *up_six, *up_five],
            scratch=[pltpu.VMEM((2 * mid, mid), f32), pltpu.VMEM((9, share, mid), f32)])
        (top_part, near_skip), got = tie((top_part, near_skip), got)
        top_rows = lax.psum_scatter(top_part, "dp", scatter_dimension=0, tiled=True, axis_index_groups=far_groups)
        other_near_skip = swap(near_skip)

        grad_four, norm_four_grad, part = run_kernel(
            functools.partial(back_dense_kernel, True), [((outer, mid), bf16), norm_out, ((outer, wide), bf16)], [core_at],
            [got, grad_pre, conv_four, moments_four, norm_four, mask, reduce2], flops=2 * outer * wide * mid, held=(0, 5, 6,))
        part = swap(part)
        grad_join1, sums = run_kernel(
            own_four_kernel, [((outer, wide), f32), join_sums], [core_at],
            [grad_four, part, reduce2, grad_join2, conv_three, moments_three, norm_three, conv_skip, moments_skip, norm_skip,
             mask], flops=2 * outer * wide * mid, held=(1, 2, 10,))
        (grad_four, other_near_skip), sums = tie((grad_four, other_near_skip), sums)
        got = spread(sums, False)
        reduce2_parts = run_kernel(
            functools.partial(weight_four_kernel, near), [((2 * mid, mid), bf16)] * near, [core_at, near_place],
            [block_one, other_block, grad_four], flops=4 * outer * wide * mid, scratch=[pltpu.VMEM((2 * wide, mid), f32)])
        reduce2_parts = to_near(reduce2_parts)

        top_rows, got = tie(top_rows, got)
        grad_three, grad_skip, norm_three_grad, norm_skip_grad, part = run_kernel(
            back_join_kernel,
            [((outer, wide), bf16), ((outer, wide), bf16), wide_norm_out, wide_norm_out, ((outer, mid), bf16)], [core_at],
            [got, grad_join1, conv_three, moments_three, norm_three, conv_skip, moments_skip, norm_skip, mask, expand1],
            flops=2 * outer * wide * mid, held=(0, 8, 9,))
        reduce2_parts, part = tie(reduce2_parts, swap(part))
        grad_pre, sums = run_kernel(
            own_dense_kernel, [((outer, mid), f32), own_sums], [core_at],
            [grad_three, part, expand1, conv_two, moments_two, norm_two, mask], flops=2 * outer * wide * mid, held=(1, 2, 6,))
        top_rows, sums = tie(top_rows, sums)
        got = spread(sums, True)
        up_join = to_near([
            jnp.concatenate([slot(grad_three, at, mid, 1), slot(grad_skip, at, mid, 1)], axis=1) for at in near_order])

        rows_b = (4 * mid + 2 * cid) // far
        bucket_b = run_kernel(
            functools.partial(weight_bottom_kernel, near, far, cid), [((rows_b, mid), bf16)] * far,
            [core_at, near_place, far_place], [near_skip, other_near_skip, *reduce2_parts, *up_join],
            flops=2 * near * outer * (4 * mid + 2 * cid) * mid,
            scratch=[pltpu.VMEM((2 * mid, mid), f32), pltpu.VMEM((2 * mid, mid), f32), pltpu.VMEM((2 * cid, mid), f32)])
        top_rows = tell_far(top_rows)
        top_rows, got = tie(top_rows, got)
        top_all = gather_near(jnp.concatenate(top_rows))
        bucket_b, got = tie(bucket_b, got)
        bucket_b = to_far(bucket_b)

        grad_two, norm_two_grad, part = run_kernel(
            gridded(back_two_kernel), [((outer, mid), bf16), norm_out, ((inner, mid), bf16)], [core_at],
            [got, grad_pre, conv_two, moments_two, norm_two, mask, spatial1], flops=18 * outer * mid * mid, held=(0, 5, 6,))
        part = swap(part)
        up_two = to_near([grad_two] * near)
        grad_pre, sums = run_kernel(
            gridded(own_two_kernel), [((inner, mid), f32), own_sums], [core_at],
            [grad_two, part, spatial1, conv_one, moments_one, norm_one, mask], flops=18 * outer * mid * mid, held=(1, 2, 6,))
        (up_two, bucket_b[3]), sums = tie((up_two, bucket_b[3]), sums)
        got = spread(sums, True)
        bucket_c = run_kernel(
            functools.partial(weight_two_kernel, grid, width, near, far), [((9 * share // far, mid), bf16)] * far,
            [near_place, far_place], [near_one, *up_two], flops=18 * near * outer * share * mid,
            scratch=[pltpu.VMEM((9, share, mid), f32)])
        (bucket_c, bucket_b), got = tie((bucket_c, bucket_b), got)
        bucket_b = tell_far(total(bucket_b).astype(bf16))

        grad_one, norm_one_grad, part, *reduce1_parts = run_kernel(
            back_one_kernel, [((inner, mid), bf16), norm_out, ((inner, cid), bf16)] + [((2 * cid // near, mid), bf16)] * near,
            [core_at, near_place],
            [got, grad_pre, conv_one, moments_one, norm_one, mask, reduce1, grad_skip, shortcut, own_x, other_x],
            scratch=[pltpu.VMEM((2 * cid, mid), f32)], flops=2 * inner * mid * cid, held=(0, 5, 6, 8,))
        part = swap(part)
        bucket_b[far // 2 + 1 :], reduce1_parts = tie(bucket_b[far // 2 + 1 :], reduce1_parts)
        reduce1_parts = to_near(reduce1_parts)
        reduce1_rows = total(reduce1_parts).astype(bf16)
        bucket_c = [jnp.concatenate([piece, slot(reduce1_rows, at, reduce1_rows.shape[0] // far, 0)])
                    for piece, at in zip(bucket_c, far_order)]
        bucket_b, bucket_c = tie(bucket_b, bucket_c)
        bucket_b = jnp.concatenate(bucket_b)
        rows_b = bucket_b.shape[0]
        bucket_b = tell_near_first(bucket_b)
        bucket_c = to_far(bucket_c)
        bucket_b, bucket_c = tie(bucket_b, bucket_c)
        def lay(arrays, chunks, layouts):
            return laid_out(arrays, chunks, near, far, near_at, far_at, layouts)

        kernel_dims = (3, 3, 2 * mid, mid)
        wide_dims = (2 * mid, 4 * mid)
        chunk = rows_a // far
        top_chunks = [(0, (member * far + b) * chunk, member, False, b) for member in range(near) for b in range(far)]
        expand2_grad, spatial2_grad = lay([top_all], top_chunks, [("columns", wide_dims), ("kernel", kernel_dims)])
        input_grad, = run_kernel(
            gridded(own_x_kernel), [((imgs, 4 * grid, cid), bf16)], [core_at],
            [grad_one, part, reduce1, grad_skip, shortcut, mask], flops=4 * inner * mid * cid, held=(1, 2, 4, 5,))
        bucket_b, sums_c = tie(bucket_b, total(bucket_c).astype(bf16))
        bucket_c = tell_far(sums_c)
        bucket_b = tell_near_then(bucket_b)
        (bucket_b, expand2_grad, spatial2_grad, input_grad), bucket_c = tie(
            (bucket_b, expand2_grad, spatial2_grad, input_grad), bucket_c)
        bucket_c = jnp.concatenate(bucket_c)
        rows_c = bucket_c.shape[0]
        bucket_c = tell_near_first(bucket_c)
        reduce2_grad, expand1_grad, shortcut_grad = lay(
            bucket_b, told_chunks(rows_b),
            [("rows", reduce2.shape), ("columns", wide_dims), ("columns", shortcut.shape)])
        (reduce2_grad, expand1_grad, shortcut_grad), bucket_c = tie((reduce2_grad, expand1_grad, shortcut_grad), bucket_c)
        bucket_c = tell_near_then(bucket_c)
        spatial1_grad, reduce1_grad = lay(
            bucket_c, told_chunks(rows_c), [("kernel", kernel_dims), ("rows", reduce1.shape)])
        grads = (reduce1_grad, spatial1_grad, expand1_grad, shortcut_grad, reduce2_grad, spatial2_grad, expand2_grad)
        return (block_one.reshape(cotangent.shape), block_two.reshape(cotangent.shape), input_grad.reshape(images.shape),
                *grads, norm_one_grad, norm_two_grad, norm_three_grad, norm_skip_grad, norm_four_grad, norm_five_grad,
                norm_six_grad)

    pixels = P("dp", None, None, "chan")
    weights = (P(None, "chan"), P(None, None, None, "chan")) + (P(None, "chan"),) * 3 + (P(None, None, None, "chan"), P(None, "chan"))
    norms = (P(None, "chan"),) * 7
    return jax.shard_map(
        local, mesh=mesh,
        in_specs=(pixels, P("dp", None), pixels) + weights + norms,
        out_specs=(pixels, pixels, pixels) + weights + norms,
        check_vma=False)
```
